128 devices in a mesh: gx: 32 (over x, z, core), gy: 4 (over y).
Axes of the slice: x: 4, y: 4, z: 4, core: 2. Of those that a mesh axis runs over, the one named last changes fastest.
Arguments:
- fine_features: bfloat16 [4096, 32, 512], P(('gx', 'gy')), may hold values from -6 to 6
- coarse_cache: bfloat16 [65536, 2048], P(('gx', 'gy')), may hold values from -6 to 6
- parent_owner: int32 [4096, 1], P(('gx', 'gy')), may hold values from 0 to 127; in each aligned block of 32 rows (0 to 31, 32 to 63, ...) at most 2 rows name the same one
- parent_cell: int32 [4096], P(('gx', 'gy')), may hold values from 0 to 511
- face_list: int32 [2560], P(('gx', 'gy')), may hold values from 0 to 31, as said below
- adjacency: int32 [4096, 26], P(('gx', 'gy')), may hold values from -1 to 51, as said below
- parent_proj: bfloat16 [32, 32], replicated, may hold values from -1 to 1
- conv_first: bfloat16 [27, 32, 32], replicated, may hold values from -0.21875 to 0.21875
- bias_first: float32 [32], replicated, may hold values from -3 to 3
- conv_second: bfloat16 [27, 32, 32], replicated, may hold values from -0.21875 to 0.21875
- bias_second: float32 [32], replicated, may hold values from -3 to 3
Outputs:
- level_out: bfloat16 [4096, 32, 512], P(('gx', 'gy'))
The draws below stay inside these ranges and needn't reach their ends.
Inputs may be any that keep to these rules, and one draw needn't show every extreme that they name: `parent_owner`: among the bricks of one device no owner is named more than 2 times; some owner is named exactly 2 times. `face_list`: each device's 20 entries are four runs of local brick indices, distinct within a run: 8 bricks on its face toward higher x, 8 toward lower x, 2 toward higher y, 2 toward lower y. `adjacency`: entries 32 to 39 appear only in columns with dx = -1, the next 8 only with dx = 1, the next 2 only with dx = 0 and dy = -1, the last 2 only with dx = 0 and dy = 1.
All inputs are finite; a program needn't handle non-finite values.
Results may differ from the reference program's by a relative error of at most 0.0051.
Values may be sent and summed in bfloat16 or wider, within the bound.
A program may use at most 128 MiB of HBM per device.

```python
import math
import jax
import jax.numpy as jnp
import numpy as np
from jax import lax

C = 32
NB = 32
CELLS = 512
FX = 8
FY = 2
FW = 20
CAP = 2
TOTAL_B = 4096
TOTAL_C = 65536
N_GX = 32
N_GY = 4
DEVICES = 128


def draw_face_list(key, part):
    key = jax.random.fold_in(key, 23)

    def one_device(device_key):
        keys = jax.random.split(device_key, 4)
        return jnp.concatenate([jax.random.permutation(keys[0], NB)[:FX], jax.random.permutation(keys[1], NB)[:FX], jax.random.permutation(keys[2], NB)[:FY], jax.random.permutation(keys[3], NB)[:FY]])
    device_keys = jax.random.split(key, DEVICES)
    return jax.vmap(one_device)(device_keys).reshape(-1).astype(jnp.int32)


def draw_adjacency(key, part):
    key = jax.random.fold_in(key, 7)
    keys = jax.random.split(key, 3)
    shape = (TOTAL_B, 26)
    pick = jax.random.randint(keys[0], shape, 0, 10)
    own_brick = jax.random.randint(keys[1], shape, 0, NB)
    spread = jax.random.randint(keys[2], shape, 0, 1 << 20)
    starts = []
    widths = []
    sides = []
    for i in range(3):
        for j in range(3):
            for k in range(3):
                if i == 1 and j == 1 and (k == 1):
                    continue
                if i == 0:
                    starts.append(NB)
                    widths.append(FX)
                    sides.append(1)
                elif i == 2:
                    starts.append(NB + FX)
                    widths.append(FX)
                    sides.append(1)
                elif j == 0:
                    starts.append(NB + 2 * FX)
                    widths.append(FY)
                    sides.append(1)
                elif j == 2:
                    starts.append(NB + 2 * FX + FY)
                    widths.append(FY)
                    sides.append(1)
                else:
                    starts.append(0)
                    widths.append(1)
                    sides.append(0)
    start_row = jnp.array(starts, jnp.int32)[None, :]
    width_row = jnp.array(widths, jnp.int32)[None, :]
    side_row = jnp.array(sides, jnp.int32)[None, :]
    halo_brick = start_row + spread % width_row
    chosen = jnp.where(pick < 3, -1, jnp.where((side_row == 1) & (pick >= 6), halo_brick, own_brick))
    chosen = chosen.at[0, 15].set(NB + 2 * FX + 2 * FY - 1)
    chosen = chosen.at[0, 0].set(-1)
    return chosen.astype(jnp.int32)


def set_ends(drawn, stream_key, least, largest):
    index_at = [jax.random.randint(jax.random.fold_in(stream_key, axis), (), 0, length) for axis, length in enumerate(drawn.shape)]
    main_axis = drawn.shape.index(max(drawn.shape))
    next_to = index_at[:main_axis] + [(index_at[main_axis] + 1) % drawn.shape[main_axis]] + index_at[main_axis + 1:]
    return drawn.at[tuple(index_at)].set(least).at[tuple(next_to)].set(largest)


def level_of(own_key, dims, shards, smallest, largest):
    def one(axis_at, shards_of):
        draws = jax.random.uniform(jax.random.fold_in(jax.random.fold_in(own_key, 6), axis_at), (shards_of,), jnp.float32, smallest / len(shards), largest / len(shards))
        return jnp.repeat(jnp.exp(draws), dims[axis_at] // shards_of).reshape((-1,) + (1,) * (len(dims) - axis_at - 1))

    factor_of = one(*shards[0])
    for cut in shards[1:]:
        factor_of = factor_of * one(*cut)
    return factor_of


def shared_out(stream_key, own, number, rows, count, top, reach, skew):
    order = jax.random.permutation(stream_key, count)
    heavy_load, common = load_shares(count, rows * top, reach, skew, True), load_shares(count, rows * top, reach, skew, False)
    places = jnp.arange(count)

    def named(sizes, offset_by):
        used = int((sizes > 0).sum())
        fixed = max(1, used // 4)
        shifted = fixed + (places - fixed + offset_by * (used - fixed)) % max(1, count - fixed)
        return jnp.zeros((count,), jnp.int32).at[order[jnp.where(places < fixed, places, shifted)]].set(jnp.asarray(sizes, jnp.int32))

    sizes = jnp.where(number % 4 == 0, named(heavy_load, number // 4), named(common, number - number // 4 - 1))
    mixed = jax.random.permutation(jax.random.fold_in(own, 3), count)
    giver, taker = mixed[0:count // 2 * 2:2], mixed[1:count // 2 * 2:2]
    slack = jnp.minimum(sizes[giver] - 1, reach - sizes[taker]) // 2
    slack = jnp.where((giver == order[0]) | (taker == order[0]) | (sizes[taker] == 0), 0, jnp.maximum(slack, 0))
    shifted = jax.random.randint(jax.random.fold_in(own, 4), (count // 2,), 0, 1 << 20) % (slack + 1)
    sizes = sizes.at[giver].add(-shifted).at[taker].add(shifted)
    items = jnp.searchsorted(jnp.cumsum(sizes), jnp.arange(rows * top), side="right").astype(jnp.int32)
    listing = items.reshape(top, rows).T
    listing = listing[jax.random.permutation(jax.random.fold_in(own, 1), rows)]
    offset_by = jax.random.randint(jax.random.fold_in(own, 2), (rows, 1), 0, top)
    return jnp.take_along_axis(listing, (jnp.arange(top)[None, :] + offset_by) % top, axis=1)


def load_shares(amount, total, limit, lean, full):
    portions = [(1 << 20) // math.isqrt(grade ** lean) + 1 for grade in range(1, amount + 1)]
    largest = limit if full else min(limit, max(-(-total // amount), total * portions[0] // sum(portions)))
    least = 1 if total - largest >= amount - 1 else 0
    holding, spare = [largest] + [least] * (amount - 1), total - largest - least * (amount - 1)
    while spare > 0:
        movable = [i for i in range(1, amount) if holding[i] < largest] or [i for i in range(1, amount) if holding[i] < limit]
        whole, budget = sum([portions[i] for i in movable]), spare
        for i in movable:
            extra = min(limit - holding[i], max(1, budget * portions[i] // whole), spare)
            holding[i] = holding[i] + extra
            spare = spare - extra
    return np.array(holding)


def normal_values(key, extent, scale, bound, shards=(), held_as=jnp.bfloat16):
    values = jax.random.normal(key, extent, jnp.float32) * scale
    if len(shards) > 0:
        values = level_of(key, extent, shards, -0.22, 0.18) * values
    return jnp.clip(values, min=-bound, max=bound).astype(held_as)


def setup_inputs(seed: int = 0) -> dict:
    arg_keys = jax.random.split(jax.random.key(seed), 12)
    fine_features = normal_values(arg_keys[0], (TOTAL_B, C, 512), 1.0, 6.0, ((0, 128),))
    coarse_cache = normal_values(arg_keys[1], (TOTAL_C, C * 64), 1.0, 6.0, ((0, 128),))
    parent_owner_keys = jax.random.split(jax.random.fold_in(arg_keys[2], 1), TOTAL_B // NB)
    parent_owner_turns = jax.random.permutation(jax.random.fold_in(arg_keys[2], 3), TOTAL_B // NB)
    parent_owner = jax.vmap(lambda own, number: shared_out(jax.random.fold_in(arg_keys[2], 2), own, number, NB, DEVICES, 1, CAP, 2))(parent_owner_keys, parent_owner_turns).reshape((TOTAL_B, 1))
    parent_cell = set_ends(jax.random.randint(arg_keys[3], (TOTAL_B,), 0, CELLS), jax.random.fold_in(arg_keys[3], 1), 0, CELLS - 1).astype(jnp.int32)
    face_list = draw_face_list(jax.random.fold_in(arg_keys[11], 71), 0)
    adjacency = draw_adjacency(jax.random.fold_in(arg_keys[11], 71), 0)
    parent_proj = normal_values(arg_keys[6], (C, C), C ** -0.5, 1.0)
    conv_first = normal_values(arg_keys[7], (27, C, C), (27 * C) ** -0.5, 0.21875)
    bias_first = normal_values(arg_keys[8], (C,), 0.5, 3.0, (), jnp.float32)
    conv_second = normal_values(arg_keys[9], (27, C, C), (27 * C) ** -0.5, 0.21875)
    bias_second = normal_values(arg_keys[10], (C,), 0.5, 3.0, (), jnp.float32)
    return {"fine_features": fine_features, "coarse_cache": coarse_cache, "parent_owner": parent_owner, "parent_cell": parent_cell, "face_list": face_list, "adjacency": adjacency, "parent_proj": parent_proj, "conv_first": conv_first, "bias_first": bias_first, "conv_second": conv_second, "bias_second": bias_second}


def cell_range(step):
    if step < 0:
        return 7, 8
    if step == 0:
        return 0, 8
    return 0, 1


def place_range(step):
    if step < 0:
        return 0, 1
    if step == 0:
        return 1, 9
    return 9, 10


def pad_tiles(own, extended, adjacency):
    bricks = own.shape[0]
    channels = own.shape[1]
    ext_five = extended.reshape(extended.shape[0], channels, 8, 8, 8)
    padded = jnp.zeros((bricks, channels, 10, 10, 10), own.dtype)
    padded = padded.at[:, :, 1:9, 1:9, 1:9].set(own.reshape(bricks, channels, 8, 8, 8))
    column = 0
    for i in range(3):
        for j in range(3):
            for k in range(3):
                if i == 1 and j == 1 and k == 1:
                    continue
                xa, xb = cell_range(i - 1)
                ya, yb = cell_range(j - 1)
                za, zb = cell_range(k - 1)
                pa, pb = place_range(i - 1)
                qa, qb = place_range(j - 1)
                ra, rb = place_range(k - 1)
                piece = ext_five[:, :, xa:xb, ya:yb, za:zb]
                index = adjacency[:, column]
                taken = jnp.take(piece, jnp.maximum(index, 0), axis=0)
                taken = jnp.where((index >= 0)[:, None, None, None, None], taken, jnp.zeros_like(taken))
                padded = padded.at[:, :, pa:pb, qa:qb, ra:rb].set(taken)
                column += 1
    return padded


def convolve(padded, weights, bias):
    bricks = padded.shape[0]
    channels = padded.shape[1]
    windows = []
    for i in range(3):
        for j in range(3):
            for k in range(3):
                windows.append(padded[:, :, i:i + 8, j:j + 8, k:k + 8].reshape(bricks, channels, 512))
    stacked = jnp.stack(windows, 1).astype(jnp.float32)
    summed = jnp.einsum("nscv,soc->nov", stacked, weights.astype(jnp.float32))
    return summed + bias[None, :, None]


def halo_blocks(bricks_grid, faces):
    selected = jax.vmap(jax.vmap(lambda field, chosen: field[chosen]))(bricks_grid, faces)
    slot_one = selected[:, :, :FX]
    slot_two = selected[:, :, FX:2 * FX]
    slot_three = selected[:, :, 2 * FX:2 * FX + FY]
    slot_four = selected[:, :, 2 * FX + FY:]
    zeros_x = jnp.zeros_like(slot_one[:1])
    zeros_y = jnp.zeros_like(slot_three[:, :1])
    block_one = jnp.concatenate([zeros_x, slot_one[:-1]], axis=0)
    block_two = jnp.concatenate([slot_two[1:], jnp.zeros_like(slot_two[:1])], axis=0)
    block_three = jnp.concatenate([zeros_y, slot_three[:, :-1]], axis=1)
    block_four = jnp.concatenate([slot_four[:, 1:], jnp.zeros_like(slot_four[:, :1])], axis=1)
    return jnp.concatenate([block_one, block_two, block_three, block_four], axis=2)


def layer(field, face_list, adjacency, weights, bias):
    bricks_grid = field.reshape(N_GX, N_GY, NB, C, 512)
    faces = face_list.reshape(N_GX, N_GY, FW)
    halos = halo_blocks(bricks_grid, faces)
    extended = jnp.concatenate([bricks_grid, halos], axis=2).reshape(N_GX * N_GY, NB + FW, C, 512)
    neighbours = adjacency.reshape(N_GX * N_GY, NB, 26)

    def one_device(inputs):
        ext_dev, adj_dev = inputs
        padded = pad_tiles(ext_dev[:NB], ext_dev, adj_dev)
        return convolve(padded, weights, bias)

    result = lax.map(one_device, (extended, neighbours))
    return result.reshape(N_GX * N_GY * NB, C, 512)


def upsample(rows, channels):
    bricks = rows.shape[0]
    blocks = rows.reshape(bricks, channels, 4, 4, 4)
    blocks = jnp.repeat(jnp.repeat(jnp.repeat(blocks, 2, axis=2), 2, axis=3), 2, axis=4)
    return blocks.reshape(bricks, channels, 512)


def reference(fine_features, coarse_cache, parent_owner, parent_cell, face_list, adjacency, parent_proj, conv_first, bias_first, conv_second, bias_second):
    parent_rows = coarse_cache[CELLS * parent_owner[:, 0] + parent_cell]
    upsampled = upsample(parent_rows, C)
    mapped = jnp.einsum("oc,ncv->nov", parent_proj.astype(jnp.float32), upsampled.astype(jnp.float32))
    level_in = (fine_features.astype(jnp.float32) + mapped).astype(jnp.bfloat16)
    hidden = jax.nn.silu(layer(level_in, face_list, adjacency, conv_first, bias_first)).astype(jnp.bfloat16)
    second = layer(hidden, face_list, adjacency, conv_second, bias_second)
    return (level_in.astype(jnp.float32) + second).astype(jnp.bfloat16)
```

```python
import functools

import jax
import jax.numpy as jnp
import numpy as np
from jax import lax
from jax.experimental import pallas as pl
from jax.experimental.pallas import tpu as pltpu
from jax.sharding import PartitionSpec as P

F32 = jnp.float32
BF16 = jnp.bfloat16
NB = 32
SLOTS = 45
BLANK = 44
MESH = pl.DeviceIdType.MESH


def column_of(dx, dy, dz):
    at = 9 * (dx + 1) + 3 * (dy + 1) + dz + 1
    return at if at < 13 else at - 1


def lane_tables():
    lane = np.arange(512)
    z = 4 * (lane // 64 % 2) + lane // 128
    x, y = lane % 64 // 8, lane % 8
    voxel = 64 * x + 8 * y + z
    cell = 16 * (x // 2) + 4 * (y // 2) + z // 2
    perm = (np.arange(512)[:, None] == voxel[None, :]).astype(np.float32)
    up = (np.arange(64)[:, None] == cell[None, :]).astype(np.float32)
    blank = np.zeros_like(up)
    even = np.concatenate([up, blank], 0)
    odd = np.concatenate([blank, up], 0)
    return perm, np.concatenate([even, odd], 1)


def strips_of(weights):
    w = weights.reshape(3, 3, 3, 32, 32)[:, :, ::-1]
    w = w.transpose(0, 1, 4, 2, 3).reshape(9, 32, 96)
    return jnp.pad(w, ((0, 0), (0, 0), (0, 160)))


def build_band(strip_ref, band_ref):
    lane = lax.broadcasted_iota(jnp.int32, (32, 256), 1)
    zero = jnp.zeros((32, 256), F32)

    def per_x(i, carry):
        first, last = [], []
        for j in range(3):
            strip = strip_ref[3 * i + j].astype(F32)
            for z in range(8):
                rolled = strip if z == 1 else pltpu.roll(strip, (32 * (z - 1)) % 256, 1)
                if z == 0:
                    first.append(jnp.where(lane >= 224, rolled, zero))
                    rolled = jnp.where(lane >= 224, zero, rolled)
                if z == 7:
                    last.append(jnp.where(lane < 32, rolled, zero))
                    rolled = jnp.where(lane < 32, zero, rolled)
                band_ref[i, pl.ds(256 * j + 32 * z, 32), :] = rolled.astype(BF16)
        order = [first[0], first[1], last[1], last[0], first[2], zero, zero, last[2]]
        for n, part in enumerate(order):
            band_ref[i, pl.ds(768 + 32 * n, 32), :] = part.astype(BF16)
        return carry

    lax.fori_loop(0, 3, per_x, 0)


def edge_lanes(low, high):
    lane = lax.broadcasted_iota(jnp.int32, low.shape, 1)
    a = jnp.where(lane < 32, low, pltpu.roll(low, 32, 1))
    b = jnp.where(lane < 96, pltpu.roll(high, 96, 1), high)
    return jnp.where(lane < 64, a, b)


def kernel(
    fine_ref, ret_ref, target_ref, adj_ref, face_ref, proj_ref, perm_ref, unperm_ref, up_ref,
    strip1_ref, bias1_ref, strip2_ref, bias2_ref, out_ref,
    tile_ref, edge_ref, pad_ref, band1_ref, band2_ref, level_ref, par_ref, even_ref, odd_ref,
    sum_ref, mix_ref, xs_ref, ys_ref, yrow_ref, xr_ref, yr_ref, send_sem, recv_sem,
):
    gx, gy = lax.axis_index("gx"), lax.axis_index("gy")
    nx, ny = lax.axis_size("gx"), lax.axis_size("gy")
    up_x, down_x = lax.rem(gx + 1, nx), lax.rem(gx + nx - 1, nx)
    up_y, down_y = lax.rem(gy + 1, ny), lax.rem(gy + ny - 1, ny)
    neighbours = [(up_x, gy), (down_x, gy), (gx, up_y), (gx, down_y)]
    barrier = pltpu.get_barrier_semaphore()
    for other in neighbours:
        pl.semaphore_signal(barrier, inc=1, device_id=other, device_id_type=MESH)
    pl.semaphore_wait(barrier, 4)

    build_band(strip1_ref, band1_ref)
    build_band(strip2_ref, band2_ref)
    for x in range(8):
        tile_ref[x, BLANK] = jnp.zeros((8, 256), F32)
        edge_ref[x, BLANK] = jnp.zeros((8, 128), F32)

    wide = jnp.concatenate([proj_ref[...]] * 8, axis=0)
    chan = lax.broadcasted_iota(jnp.int32, (32, 256), 0)
    lane = lax.broadcasted_iota(jnp.int32, (32, 256), 1)
    pick = jnp.where(chan == 2 * (lane % 16) + lane // 128, 1.0, 0.0).astype(BF16)
    spread = jnp.dot(wide, pick, preferred_element_type=F32)
    row = lax.broadcasted_iota(jnp.int32, (256, 256), 0)
    lane = lax.broadcasted_iota(jnp.int32, (256, 256), 1)
    mix_ref[...] = jnp.where(row // 32 == lane % 128 // 16, spread, 0.0).astype(BF16)

    def place(x, slot, tile):
        tile_ref[x, slot] = tile
        edge_ref[x, slot] = edge_lanes(tile[:, :128], tile[:, 128:])

    def fetch(b, carry):
        par_ref[pl.ds(pl.multiple_of(16 * b, 16), 16), :] = ret_ref[target_ref[b]]
        return carry

    lax.fori_loop(0, NB, fetch, 0)

    def level(g, carry):
        rows = pl.ds(pl.multiple_of(256 * g, 256), 256)
        pair = par_ref[pl.ds(pl.multiple_of(128 * g, 128), 128), :]
        both = jnp.dot(pair, up_ref[...], preferred_element_type=F32).astype(BF16)
        stack = jnp.concatenate([both[:, :512], both[:, 512:]], axis=0)
        mapped = jnp.dot(mix_ref[...], stack, preferred_element_type=F32)
        fine = jnp.dot(fine_ref[rows, :], perm_ref[...], preferred_element_type=F32)
        rounded = (fine + mapped).astype(BF16)
        level_ref[rows, :] = rounded
        wide = rounded.astype(F32)
        for n in range(8):
            own = wide[32 * n : 32 * n + 32, :]
            square = jnp.concatenate([own[:, 128 * k : 128 * k + 128] for k in range(4)], axis=0)
            turned = square.T
            for x in range(8):
                low, high = turned[8 * x : 8 * x + 8], turned[64 + 8 * x : 72 + 8 * x]
                place(x, 8 * g + n, jnp.concatenate([low, high], axis=1))
        return carry

    lax.fori_loop(0, 4, level, 0)

    row8 = lax.broadcasted_iota(jnp.int32, (8, 256), 0)
    row8e = lax.broadcasted_iota(jnp.int32, (8, 128), 0)
    lane8e = lax.broadcasted_iota(jnp.int32, (8, 128), 1)

    def exchange(turn):
        for d in range(2):
            x = 7 if d == 0 else 0
            for j in range(0, 8, 2):
                two = jnp.concatenate(
                    [tile_ref[x, face_ref[8 * d + j]], tile_ref[x, face_ref[8 * d + j + 1]]], axis=0
                )
                xs_ref[turn, d, pl.ds(8 * j, 16), :] = two.astype(BF16)
            y = 7 if d == 0 else 0
            for j in range(2):
                at = face_ref[16 + 2 * d + j]
                for x in range(8):
                    yrow_ref[pl.ds(8 * j + x, 1), :] = tile_ref[x, at, pl.ds(y, 1), :]
            ys_ref[turn, d] = yrow_ref[...].astype(BF16)
        copies = []
        for d in range(2):
            copies.append(pltpu.make_async_remote_copy(
                src_ref=xs_ref.at[turn, d], dst_ref=xr_ref.at[turn, d],
                send_sem=send_sem.at[turn, d], recv_sem=recv_sem.at[turn, d],
                device_id=neighbours[d], device_id_type=MESH))
            copies.append(pltpu.make_async_remote_copy(
                src_ref=ys_ref.at[turn, d], dst_ref=yr_ref.at[turn, d],
                send_sem=send_sem.at[turn, 2 + d], recv_sem=recv_sem.at[turn, 2 + d],
                device_id=neighbours[2 + d], device_id_type=MESH))
        for copy in copies:
            copy.start()
        return copies

    def land(turn, copies):
        for copy in copies:
            copy.wait()
        for d in range(2):
            here = (gx > 0) if d == 0 else (gx < nx - 1)
            for j in range(8):
                if j % 2 == 0:
                    two = xr_ref[turn, d, pl.ds(8 * j, 16), :].astype(F32)
                    two = jnp.where(here, two, 0.0)
                place(7 if d == 0 else 0, 32 + j, two[8 * (j % 2) : 8 * (j % 2) + 8])
            here = (gy > 0) if d == 0 else (gy < ny - 1)
            rows = jnp.where(here, yr_ref[turn, d].astype(F32), 0.0)
            for j in range(2):
                for x in range(8):
                    line = rows[8 * j + x : 8 * j + x + 1]
                    place(x, 40 + 2 * d + j, jnp.broadcast_to(line, (8, 256)))

    def padded_tile(b, px):
        dx = -1 if px == 0 else (1 if px == 9 else 0)
        x = 7 if px == 0 else (0 if px == 9 else px - 1)

        def at(dy, dz):
            if dx == 0 and dy == 0 and dz == 0:
                return b
            return adj_ref[b * 26 + column_of(dx, dy, dz)]

        mid = tile_ref[x, at(0, 0)]
        low = pltpu.roll(jnp.where(row8 == 7, tile_ref[x, at(-1, 0)], mid), 1, 0)
        high = pltpu.roll(jnp.where(row8 == 0, tile_ref[x, at(1, 0)], mid), 7, 0)
        ends = [
            jnp.where(lane8e < 64, edge_ref[x, at(dy, 1)], edge_ref[x, at(dy, -1)])
            for dy in (-1, 0, 1)
        ]
        elow = pltpu.roll(jnp.where(row8e == 7, ends[0], ends[1]), 1, 0)
        ehigh = pltpu.roll(jnp.where(row8e == 0, ends[2], ends[1]), 7, 0)
        emid = jnp.where((lane8e >= 32) & (lane8e < 96), ends[1], elow)
        return jnp.concatenate([low, mid, high, emid, ehigh], axis=1)

    def pad_all():
        def per_pair(n, carry):
            for px in range(10):
                two = jnp.concatenate([padded_tile(2 * n, px), padded_tile(2 * n + 1, px)], axis=0)
                pad_ref[px, pl.ds(pl.multiple_of(16 * n, 16), 16), :] = two.astype(BF16)
            return carry

        lax.fori_loop(0, NB // 2, per_pair, 0)

    def conv(x, band_ref, bias_ref):
        total = jnp.dot(pad_ref[x], band_ref[0], preferred_element_type=F32)
        total += jnp.dot(pad_ref[x + 1], band_ref[1], preferred_element_type=F32)
        total += jnp.dot(pad_ref[x + 2], band_ref[2], preferred_element_type=F32)
        return total + bias_ref[...]

    land(0, exchange(0))
    pad_all()

    def first(x, carry):
        v = conv(x, band1_ref, bias1_ref)
        h = (v / (1.0 + jnp.exp(-v))).astype(BF16).astype(F32)
        tile_ref[x, pl.ds(0, NB)] = h.reshape(NB, 8, 256)
        e = edge_lanes(h[:, :128], h[:, 128:])
        edge_ref[x, pl.ds(0, NB)] = e.reshape(NB, 8, 128)
        return carry

    lax.fori_loop(0, 8, first, 0)
    land(1, exchange(1))
    pad_all()

    def second(x, carry):
        sum_ref[x] = conv(x, band2_ref, bias2_ref).reshape(NB, 8, 256)
        return carry

    lax.fori_loop(0, 8, second, 0)

    def finish(g, carry):
        rows = pl.ds(pl.multiple_of(256 * g, 256), 256)
        parts = []
        for n in range(8):
            tall = [sum_ref[x, 8 * g + n] for x in range(8)]
            turned = jnp.concatenate([t[:, :128] for t in tall] + [t[:, 128:] for t in tall], axis=0).T
            parts.append(jnp.concatenate([turned[32 * k : 32 * k + 32] for k in range(4)], axis=1))
        total = jnp.concatenate(parts, axis=0) + level_ref[rows, :].astype(F32)
        out = jnp.dot(total.astype(BF16), unperm_ref[...], preferred_element_type=F32)
        out_ref[rows, :] = out.astype(BF16)
        return carry

    lax.fori_loop(0, 4, finish, 0)


def lookup(cache, cells):
    rows = jnp.take(cache, jnp.maximum(cells, 0), axis=0)
    return jnp.where((cells >= 0)[:, None], rows, jnp.zeros_like(rows))


def per_device(
    fine_features, coarse_cache, parent_owner, parent_cell, face_list, adjacency,
    parent_proj, conv_first, bias_first, conv_second, bias_second,
):
    devices = lax.axis_size("gx") * lax.axis_size("gy")
    owners = parent_owner[:, 0]
    onehot = (owners[:, None] == jnp.arange(devices, dtype=jnp.int32)[None, :]).astype(jnp.int32)
    before = jnp.cumsum(onehot, axis=0) - onehot
    position = jnp.sum(before * onehot, axis=1)
    target = owners * 2 + position
    requests = jnp.full((devices * 2,), -1, jnp.int32).at[target].set(parent_cell)
    arrived = lax.all_to_all(requests, ("gx", "gy"), split_axis=0, concat_axis=0, tiled=True)
    answers = lookup(coarse_cache, arrived)
    returned = lax.all_to_all(answers, ("gx", "gy"), split_axis=0, concat_axis=0, tiled=True)
    returned = returned.reshape(devices * 2, 16, 128)
    places = jnp.where(adjacency < 0, BLANK, jnp.where(adjacency >= 40, adjacency - 8, adjacency))
    perm, up = lane_tables()
    vmem = pl.BlockSpec(memory_space=pltpu.VMEM)
    smem = pl.BlockSpec(memory_space=pltpu.SMEM)
    out = pl.pallas_call(
        kernel,
        out_shape=jax.ShapeDtypeStruct((NB * 32, 512), BF16),
        in_specs=[vmem, vmem, smem, smem, smem] + [vmem] * 8,
        out_specs=vmem,
        scratch_shapes=[
            pltpu.VMEM((8, SLOTS, 8, 256), F32),
            pltpu.VMEM((8, SLOTS, 8, 128), F32),
            pltpu.VMEM((10, 256, 1024), BF16),
            pltpu.VMEM((3, 1024, 256), BF16),
            pltpu.VMEM((3, 1024, 256), BF16),
            pltpu.VMEM((NB * 32, 512), BF16),
            pltpu.VMEM((NB * 16, 128), BF16),
            pltpu.VMEM((8, 128), BF16),
            pltpu.VMEM((8, 128), BF16),
            pltpu.VMEM((8, NB, 8, 256), F32),
            pltpu.VMEM((256, 256), BF16),
            pltpu.VMEM((2, 2, 64, 256), BF16),
            pltpu.VMEM((2, 2, 16, 256), BF16),
            pltpu.VMEM((16, 256), F32),
            pltpu.VMEM((2, 2, 64, 256), BF16),
            pltpu.VMEM((2, 2, 16, 256), BF16),
            pltpu.SemaphoreType.DMA((2, 4)),
            pltpu.SemaphoreType.DMA((2, 4)),
        ],
        compiler_params=pltpu.CompilerParams(
            collective_id=0, has_side_effects=True, vmem_limit_bytes=56 * 1024 * 1024
        ),
    )(
        fine_features.reshape(NB * 32, 512), returned, target, places.reshape(-1), face_list, parent_proj,
        jnp.asarray(perm, BF16), jnp.asarray(perm.T, BF16), jnp.asarray(up, BF16),
        strips_of(conv_first), jnp.tile(bias_first, 8)[None, :],
        strips_of(conv_second), jnp.tile(bias_second, 8)[None, :],
    )
    return out.reshape(NB, 32, 512)


def solution(mesh):
    placed = (
        P(("gx", "gy"), None, None),
        P(("gx", "gy"), None),
        P(("gx", "gy"), None),
        P(("gx", "gy")),
        P(("gx", "gy")),
        P(("gx", "gy"), None),
        P(),
        P(),
        P(),
        P(),
        P(),
    )
    return jax.shard_map(
        per_device,
        mesh=mesh,
        in_specs=placed,
        out_specs=P(("gx", "gy"), None, None),
        check_vma=False,
    )
```

```python
import jax
import jax.numpy as jnp
import numpy as np
from jax import lax
from jax.experimental import pallas as pl
from jax.experimental.pallas import tpu as pltpu
from jax.sharding import PartitionSpec as P

F32 = jnp.float32
BF16 = jnp.bfloat16
NB = 32
SLOTS = 53
MESH = pl.DeviceIdType.MESH


def column_of(dx, dy, dz):
    at = 9 * (dx + 1) + 3 * (dy + 1) + dz + 1
    return at if at < 13 else at - 1


def lane_tables():
    lane = np.arange(512)
    z = 4 * (lane // 64 % 2) + lane // 128
    x, y = lane % 64 // 8, lane % 8
    voxel = 64 * x + 8 * y + z
    cell = 16 * (x // 2) + 4 * (y // 2) + z // 2
    perm = (np.arange(512)[:, None] == voxel[None, :]).astype(np.float32)
    up = (np.arange(64)[:, None] == cell[None, :]).astype(np.float32)
    blank = np.zeros_like(up)
    even = np.concatenate([up, blank], 0)
    odd = np.concatenate([blank, up], 0)
    return perm, np.concatenate([even, odd], 1)


def build_band(weight_ref, band_ref):
    lane = lax.broadcasted_iota(jnp.int32, (32, 256), 1)
    zero = jnp.zeros((32, 256), F32)

    def per_x(i, carry):
        first, last = [], []
        for j in range(3):
            taps = [weight_ref[9 * i + 3 * j + k].astype(F32) for k in (2, 1, 0)]
            taps = jnp.concatenate(taps + [jnp.zeros((32, 32), F32)], axis=0)
            strip = jnp.concatenate([taps.T, jnp.zeros((32, 128), F32)], axis=1)
            for z in range(8):
                rolled = strip if z == 1 else pltpu.roll(strip, (32 * (z - 1)) % 256, 1)
                if z == 0:
                    first.append(jnp.where(lane >= 224, rolled, zero))
                    rolled = jnp.where(lane >= 224, zero, rolled)
                if z == 7:
                    last.append(jnp.where(lane < 32, rolled, zero))
                    rolled = jnp.where(lane < 32, zero, rolled)
                band_ref[i, pl.ds(256 * j + 32 * z, 32), :] = rolled.astype(BF16)
        order = [first[0], first[1], last[1], last[0], first[2], zero, zero, last[2]]
        for n, part in enumerate(order):
            band_ref[i, pl.ds(768 + 32 * n, 32), :] = part.astype(BF16)
        return carry

    lax.fori_loop(0, 3, per_x, 0)


def edge_lanes(low, high):
    lane = lax.broadcasted_iota(jnp.int32, low.shape, 1)
    a = jnp.where(lane < 32, low, pltpu.roll(low, 32, 1))
    b = jnp.where(lane < 96, pltpu.roll(high, 96, 1), high)
    return jnp.where(lane < 64, a, b)


def wait_bytes(ref, sem):
    pltpu.make_async_copy(ref, ref, sem).wait()


def kernel(
    owner_ref, cell_ref, face_ref, adj_ref, bias1_ref, bias2_ref, proj_ref, weight1_ref, weight2_ref,
    fine_hbm, cache_hbm, perm_hbm, up_hbm, out_ref,
    fine_ref, cache_ref, perm_ref, up_ref, code_ref, codes_ref, hot_ref, ans_ref, stage_ref, ret_ref, rank_ref,
    finep_ref, tile_ref, edge_ref, pad_ref, band1_ref, band2_ref, level_ref, par_ref,
    sum_ref, mix_ref, bias_ref, xs_ref, ys_ref, yrow_ref, xr_ref, yr_ref,
    send_sem, recv_sem, load_sem, pair_sem, block_sem, reply_sem,
):
    gx, gy = lax.axis_index("gx"), lax.axis_index("gy")
    nx, ny = lax.axis_size("gx"), lax.axis_size("gy")
    devices = nx * ny
    up_x, down_x = lax.rem(gx + 1, nx), lax.rem(gx + nx - 1, nx)
    up_y, down_y = lax.rem(gy + 1, ny), lax.rem(gy + ny - 1, ny)
    neighbours = [(up_x, gy), (down_x, gy), (gx, up_y), (gx, down_y)]
    me = gx * ny + gy
    chip, core = gx // 2, lax.rem(gx, 2)
    near = 2 * ny
    far = nx // 2
    spot = gy * 2 + core

    def near_device(k):
        at = lax.rem(spot + k, near)
        return (chip * 2 + lax.rem(at, 2), at // 2)

    def far_device(k):
        return (lax.rem(chip + k, far) * 2 + core, gy)

    barrier = pltpu.get_barrier_semaphore()
    for k in range(1, near):
        pl.semaphore_signal(barrier, inc=1, device_id=near_device(k), device_id_type=MESH)
    for k in range(1, far):
        pl.semaphore_signal(barrier, inc=1, device_id=far_device(k), device_id_type=MESH)
    loads = [
        pltpu.make_async_copy(src, dst, load_sem.at[n])
        for n, (src, dst) in enumerate(
            [(fine_hbm, fine_ref), (cache_hbm, cache_ref), (perm_hbm, perm_ref), (up_hbm, up_ref)]
        )
    ]
    for load in loads:
        load.start()

    lane = lax.broadcasted_iota(jnp.int32, (1, 128), 1)
    code = jnp.full((1, 128), -1, jnp.int32)
    for b in range(NB):
        code = jnp.where(lane == b, owner_ref[b, 0] * 512 + cell_ref[b], code)
    code_ref[0:1] = code
    here = chip * near + spot
    codes_ref[pl.ds(here, 1)] = code

    build_band(weight1_ref, band1_ref)
    for x in range(8):
        tile_ref[x, 0] = jnp.zeros((8, 256), F32)
        edge_ref[x, 0] = jnp.zeros((8, 128), F32)
    lane = lax.broadcasted_iota(jnp.int32, (1, 256), 1)
    for n, ref in enumerate((bias1_ref, bias2_ref)):
        line = jnp.zeros((1, 256), F32)
        for o in range(32):
            line = jnp.where(lane % 32 == o, ref[o], line)
        bias_ref[n : n + 1] = line

    wide = jnp.concatenate([proj_ref[...]] * 8, axis=0)
    chan = lax.broadcasted_iota(jnp.int32, (32, 256), 0)
    lane = lax.broadcasted_iota(jnp.int32, (32, 256), 1)
    pick = jnp.where(chan == 2 * (lane % 16) + lane // 128, 1.0, 0.0).astype(BF16)
    spread = jnp.dot(wide, pick, preferred_element_type=F32)
    row = lax.broadcasted_iota(jnp.int32, (256, 256), 0)
    lane = lax.broadcasted_iota(jnp.int32, (256, 256), 1)
    mix_ref[...] = jnp.where(row // 32 == lane % 128 // 16, spread, 0.0).astype(BF16)

    pl.semaphore_wait(barrier, near + far - 2)

    own_row = codes_ref.at[pl.ds(here, 1)]
    for k in range(1, near):
        pltpu.make_async_remote_copy(
            src_ref=code_ref.at[pl.ds(0, 1)], dst_ref=own_row, send_sem=pair_sem.at[0], recv_sem=pair_sem.at[1],
            device_id=near_device(k), device_id_type=MESH).start()

    def ranks(b, carry):
        count = jnp.int32(0)
        for other in range(NB):
            same = (owner_ref[other, 0] == owner_ref[b, 0]) & (other < b)
            count = count + jnp.where(same, 1, 0)
        rank_ref[b] = owner_ref[b, 0] * 2 + count
        return carry

    lax.fori_loop(0, NB, ranks, 0)
    wait_bytes(codes_ref.at[pl.ds(0, near - 1)], pair_sem.at[0])
    wait_bytes(codes_ref.at[pl.ds(0, near - 1)], pair_sem.at[1])
    block = codes_ref.at[pl.ds(pl.multiple_of(chip * near, near), near)]
    for k in range(1, far):
        pltpu.make_async_remote_copy(
            src_ref=block, dst_ref=block, send_sem=block_sem.at[0], recv_sem=block_sem.at[1],
            device_id=far_device(k), device_id_type=MESH).start()
    build_band(weight2_ref, band2_ref)
    loads[1].wait()
    wait_bytes(codes_ref.at[pl.ds(0, near * (far - 1))], block_sem.at[0])
    wait_bytes(codes_ref.at[pl.ds(0, near * (far - 1))], block_sem.at[1])

    codes = codes_ref[...]
    spots = lax.broadcasted_iota(jnp.int32, codes.shape, 1).astype(F32)
    match = (codes >> 9) == me
    cells = (codes & 511).astype(F32)
    lead = jnp.min(jnp.where(match, spots, 999.0), axis=1, keepdims=True)
    one = jnp.max(jnp.where(match & (spots == lead), cells, -1.0), axis=1, keepdims=True)
    two = jnp.max(jnp.where(match & (spots != lead), cells, -1.0), axis=1, keepdims=True)
    index = lax.broadcasted_iota(jnp.int32, (codes.shape[0], 512), 1).astype(F32)
    hot_ref[pl.ds(0, devices), :] = jnp.where(index == one, 1.0, 0.0).astype(BF16)
    hot_ref[pl.ds(devices, devices), :] = jnp.where(index == two, 1.0, 0.0).astype(BF16)

    def answer(n, carry):
        cols = pl.ds(pl.multiple_of(256 * n, 256), 256)
        rows = jnp.dot(hot_ref[...], cache_ref[:, cols], preferred_element_type=F32)
        height = 2 * devices
        ans_ref[pl.ds(pl.multiple_of(2 * n * height, height), height), :] = rows[:, :128]
        ans_ref[pl.ds(pl.multiple_of((2 * n + 1) * height, height), height), :] = rows[:, 128:]
        return carry

    lax.fori_loop(0, 8, answer, 0)

    def answer_to(dx, dy):
        at = dx // 2 * near + dy * 2 + lax.rem(dx, 2)
        first = ans_ref[pl.ds(at, 16, stride=2 * devices), :]
        second = ans_ref[pl.ds(devices + at, 16, stride=2 * devices), :]
        return first.astype(BF16), second.astype(BF16)

    mine = answer_to(gx, gy)
    ret_ref[2 * me] = mine[0]
    ret_ref[2 * me + 1] = mine[1]

    def reply(i, carry):
        to = lax.rem(me + lax.rem(51 * i, devices), devices)
        dx, dy = to // ny, lax.rem(to, ny)
        pair = answer_to(dx, dy)
        stage_ref[2 * to] = pair[0]
        stage_ref[2 * to + 1] = pair[1]
        pltpu.make_async_remote_copy(
            src_ref=stage_ref.at[pl.ds(2 * to, 2)], dst_ref=ret_ref.at[pl.ds(2 * me, 2)],
            send_sem=reply_sem.at[0], recv_sem=reply_sem.at[1],
            device_id=(dx, dy), device_id_type=MESH).start()
        return carry

    lax.fori_loop(1, devices, reply, 0)

    for n in (0, 2, 3):
        loads[n].wait()

    def unfold(g, carry):
        fine = fine_ref[pl.ds(pl.multiple_of(8 * g, 8), 8)].reshape(256, 512)
        rows = pl.ds(pl.multiple_of(256 * g, 256), 256)
        finep_ref[rows, :] = jnp.dot(fine, perm_ref[...], preferred_element_type=F32)
        return carry

    lax.fori_loop(0, 4, unfold, 0)
    wait_bytes(ret_ref.at[pl.ds(0, 2 * devices - 2)], reply_sem.at[0])
    wait_bytes(ret_ref.at[pl.ds(0, 2 * devices - 2)], reply_sem.at[1])

    def place(x, slot, tile):
        tile_ref[x, slot] = tile
        edge_ref[x, slot] = edge_lanes(tile[:, :128], tile[:, 128:])

    def fetch(b, carry):
        par_ref[pl.ds(pl.multiple_of(16 * b, 16), 16), :] = ret_ref[rank_ref[b]]
        return carry

    lax.fori_loop(0, NB, fetch, 0)

    def level(g, carry):
        rows = pl.ds(pl.multiple_of(256 * g, 256), 256)
        pair = par_ref[pl.ds(pl.multiple_of(128 * g, 128), 128), :]
        both = jnp.dot(pair, up_ref[...], preferred_element_type=F32).astype(BF16)
        stack = jnp.concatenate([both[:, :512], both[:, 512:]], axis=0)
        mapped = jnp.dot(mix_ref[...], stack, preferred_element_type=F32)
        rounded = (finep_ref[rows, :] + mapped).astype(BF16)
        level_ref[rows, :] = rounded
        wide = rounded.astype(F32)
        for n in range(8):
            own = wide[32 * n : 32 * n + 32, :]
            square = jnp.concatenate([own[:, 128 * k : 128 * k + 128] for k in range(4)], axis=0)
            turned = square.T
            for x in range(8):
                low, high = turned[8 * x : 8 * x + 8], turned[64 + 8 * x : 72 + 8 * x]
                place(x, 8 * g + n + 1, jnp.concatenate([low, high], axis=1))
        return carry

    lax.fori_loop(0, 4, level, 0)

    row8 = lax.broadcasted_iota(jnp.int32, (8, 256), 0)
    row8e = lax.broadcasted_iota(jnp.int32, (8, 128), 0)
    lane8e = lax.broadcasted_iota(jnp.int32, (8, 128), 1)

    def exchange(turn):
        for d in range(2):
            x = 7 if d == 0 else 0
            for j in range(0, 8, 2):
                two = jnp.concatenate(
                    [tile_ref[x, face_ref[8 * d + j] + 1], tile_ref[x, face_ref[8 * d + j + 1] + 1]], axis=0
                )
                xs_ref[turn, d, pl.ds(8 * j, 16), :] = two.astype(BF16)
            y = 7 if d == 0 else 0
            for j in range(2):
                at = face_ref[16 + 2 * d + j] + 1
                for x in range(8):
                    yrow_ref[pl.ds(8 * j + x, 1), :] = tile_ref[x, at, pl.ds(y, 1), :]
            ys_ref[turn, d] = yrow_ref[...].astype(BF16)
        copies = []
        for d in range(2):
            copies.append(pltpu.make_async_remote_copy(
                src_ref=xs_ref.at[turn, d], dst_ref=xr_ref.at[turn, d],
                send_sem=send_sem.at[turn, d], recv_sem=recv_sem.at[turn, d],
                device_id=neighbours[d], device_id_type=MESH))
            copies.append(pltpu.make_async_remote_copy(
                src_ref=ys_ref.at[turn, d], dst_ref=yr_ref.at[turn, d],
                send_sem=send_sem.at[turn, 2 + d], recv_sem=recv_sem.at[turn, 2 + d],
                device_id=neighbours[2 + d], device_id_type=MESH))
        for copy in copies:
            copy.start()
        return copies

    def land(turn, copies):
        for copy in copies:
            copy.wait()
        for d in range(2):
            here = (gx > 0) if d == 0 else (gx < nx - 1)
            for j in range(8):
                if j % 2 == 0:
                    two = xr_ref[turn, d, pl.ds(8 * j, 16), :].astype(F32)
                    two = jnp.where(here, two, 0.0)
                place(7 if d == 0 else 0, 33 + 8 * d + j, two[8 * (j % 2) : 8 * (j % 2) + 8])
            here = (gy > 0) if d == 0 else (gy < ny - 1)
            rows = jnp.where(here, yr_ref[turn, d].astype(F32), 0.0)
            for j in range(2):
                for x in range(8):
                    line = rows[8 * j + x : 8 * j + x + 1]
                    place(x, 49 + 2 * d + j, jnp.broadcast_to(line, (8, 256)))

    def padded_tile(b, px):
        dx = -1 if px == 0 else (1 if px == 9 else 0)
        x = 7 if px == 0 else (0 if px == 9 else px - 1)

        def at(dy, dz):
            if dx == 0 and dy == 0 and dz == 0:
                return b + 1
            return adj_ref[b, column_of(dx, dy, dz)] + 1

        mid = tile_ref[x, at(0, 0)]
        low = pltpu.roll(jnp.where(row8 == 7, tile_ref[x, at(-1, 0)], mid), 1, 0)
        high = pltpu.roll(jnp.where(row8 == 0, tile_ref[x, at(1, 0)], mid), 7, 0)
        ends = [
            jnp.where(lane8e < 64, edge_ref[x, at(dy, 1)], edge_ref[x, at(dy, -1)])
            for dy in (-1, 0, 1)
        ]
        elow = pltpu.roll(jnp.where(row8e == 7, ends[0], ends[1]), 1, 0)
        ehigh = pltpu.roll(jnp.where(row8e == 0, ends[2], ends[1]), 7, 0)
        emid = jnp.where((lane8e >= 32) & (lane8e < 96), ends[1], elow)
        return jnp.concatenate([low, mid, high, emid, ehigh], axis=1)

    def pad_all():
        def per_pair(n, carry):
            for px in range(10):
                two = jnp.concatenate([padded_tile(2 * n, px), padded_tile(2 * n + 1, px)], axis=0)
                pad_ref[px, pl.ds(pl.multiple_of(16 * n, 16), 16), :] = two.astype(BF16)
            return carry

        lax.fori_loop(0, NB // 2, per_pair, 0)

    def conv(x, band_ref, bias):
        total = jnp.dot(pad_ref[x], band_ref[0], preferred_element_type=F32)
        total += jnp.dot(pad_ref[x + 1], band_ref[1], preferred_element_type=F32)
        total += jnp.dot(pad_ref[x + 2], band_ref[2], preferred_element_type=F32)
        return total + bias_ref[pl.ds(bias, 1)]

    land(0, exchange(0))
    pad_all()

    def first(x, carry):
        v = conv(x, band1_ref, 0)
        h = (v / (1.0 + jnp.exp(-v))).astype(BF16).astype(F32)
        tile_ref[x, pl.ds(1, NB)] = h.reshape(NB, 8, 256)
        e = edge_lanes(h[:, :128], h[:, 128:])
        edge_ref[x, pl.ds(1, NB)] = e.reshape(NB, 8, 128)
        return carry

    lax.fori_loop(0, 8, first, 0)
    land(1, exchange(1))
    pad_all()

    def second(x, carry):
        sum_ref[x] = conv(x, band2_ref, 1).reshape(NB, 8, 256)
        return carry

    lax.fori_loop(0, 8, second, 0)

    def finish(g, carry):
        rows = pl.ds(pl.multiple_of(256 * g, 256), 256)
        parts = []
        for n in range(8):
            tall = [sum_ref[x, 8 * g + n] for x in range(8)]
            turned = jnp.concatenate([t[:, :128] for t in tall] + [t[:, 128:] for t in tall], axis=0).T
            parts.append(jnp.concatenate([turned[32 * k : 32 * k + 32] for k in range(4)], axis=1))
        total = jnp.concatenate(parts, axis=0) + level_ref[rows, :].astype(F32)
        out_ref[rows, :] = total.astype(BF16)
        return carry

    lax.fori_loop(0, 4, finish, 0)


def per_device(
    fine_features, coarse_cache, parent_owner, parent_cell, face_list, adjacency,
    parent_proj, conv_first, bias_first, conv_second, bias_second,
):
    devices = lax.axis_size("gx") * lax.axis_size("gy")
    perm, up = lane_tables()
    vmem = pl.BlockSpec(memory_space=pltpu.VMEM)
    smem = pl.BlockSpec(memory_space=pltpu.SMEM)
    hbm = pl.BlockSpec(memory_space=pl.ANY)
    out = pl.pallas_call(
        kernel,
        out_shape=jax.ShapeDtypeStruct((NB * 32, 512), BF16),
        in_specs=[smem] * 6 + [vmem] * 3 + [hbm] * 4,
        out_specs=vmem,
        scratch_shapes=[
            pltpu.VMEM((NB, 32, 512), BF16),
            pltpu.VMEM((512, 2048), BF16),
            pltpu.VMEM((512, 512), BF16),
            pltpu.VMEM((128, 1024), BF16),
            pltpu.VMEM((8, 128), jnp.int32),
            pltpu.VMEM((devices, 128), jnp.int32),
            pltpu.VMEM((2 * devices, 512), BF16),
            pltpu.VMEM((32 * devices, 128), F32),
            pltpu.VMEM((2 * devices, 16, 128), BF16),
            pltpu.VMEM((2 * devices, 16, 128), BF16),
            pltpu.SMEM((NB,), jnp.int32),
            pltpu.VMEM((NB * 32, 512), F32),
            pltpu.VMEM((8, SLOTS, 8, 256), F32),
            pltpu.VMEM((8, SLOTS, 8, 128), F32),
            pltpu.VMEM((10, 256, 1024), BF16),
            pltpu.VMEM((3, 1024, 256), BF16),
            pltpu.VMEM((3, 1024, 256), BF16),
            pltpu.VMEM((NB * 32, 512), BF16),
            pltpu.VMEM((NB * 16, 128), BF16),
            pltpu.VMEM((8, NB, 8, 256), F32),
            pltpu.VMEM((256, 256), BF16),
            pltpu.VMEM((8, 256), F32),
            pltpu.VMEM((2, 2, 64, 256), BF16),
            pltpu.VMEM((2, 2, 16, 256), BF16),
            pltpu.VMEM((16, 256), F32),
            pltpu.VMEM((2, 2, 64, 256), BF16),
            pltpu.VMEM((2, 2, 16, 256), BF16),
            pltpu.SemaphoreType.DMA((2, 4)),
            pltpu.SemaphoreType.DMA((2, 4)),
            pltpu.SemaphoreType.DMA((4,)),
            pltpu.SemaphoreType.DMA((2,)),
            pltpu.SemaphoreType.DMA((2,)),
            pltpu.SemaphoreType.DMA((2,)),
        ],
        compiler_params=pltpu.CompilerParams(
            collective_id=0, has_side_effects=True, vmem_limit_bytes=56 * 1024 * 1024
        ),
    )(
        parent_owner, parent_cell, face_list, adjacency, bias_first, bias_second, parent_proj, conv_first,
        conv_second, fine_features, coarse_cache, jnp.asarray(perm, BF16), jnp.asarray(up, BF16),
    )
    out = jnp.dot(out, jnp.asarray(perm.T, BF16), preferred_element_type=F32).astype(BF16)
    return out.reshape(NB, 32, 512)


def solution(mesh):
    placed = (
        P(("gx", "gy"), None, None),
        P(("gx", "gy"), None),
        P(("gx", "gy"), None),
        P(("gx", "gy")),
        P(("gx", "gy")),
        P(("gx", "gy"), None),
        P(),
        P(),
        P(),
        P(),
        P(),
    )
    return jax.shard_map(
        per_device,
        mesh=mesh,
        in_specs=placed,
        out_specs=P(("gx", "gy"), None, None),
        check_vma=False,
    )
```

```python
import jax
import jax.numpy as jnp
import numpy as np
from jax import lax
from jax.experimental import pallas as pl
from jax.experimental.pallas import tpu as pltpu
from jax.sharding import PartitionSpec as P

F32 = jnp.float32
BF16 = jnp.bfloat16
NB = 32
SLOTS = 53
MESH = pl.DeviceIdType.MESH
GROUPS = [[0, 1, 6, 7, 2, 3], [4, 5]]


def column_of(dx, dy, dz):
    at = 9 * (dx + 1) + 3 * (dy + 1) + dz + 1
    return at if at < 13 else at - 1


def lane_tables():
    lane = np.arange(512)
    z = 4 * (lane // 64 % 2) + lane // 128
    x, y = lane % 64 // 8, lane % 8
    voxel = 64 * x + 8 * y + z
    cell = 16 * (x // 2) + 4 * (y // 2) + z // 2
    perm = (np.arange(512)[:, None] == voxel[None, :]).astype(np.float32)
    up = (np.arange(64)[:, None] == cell[None, :]).astype(np.float32)
    blank = np.zeros_like(up)
    even = np.concatenate([up, blank], 0)
    odd = np.concatenate([blank, up], 0)
    return perm, np.concatenate([even, odd], 1)


def build_band(weight_ref, band_ref):
    lane = lax.broadcasted_iota(jnp.int32, (32, 256), 1)
    zero = jnp.zeros((32, 256), F32)

    def per_x(i, carry):
        first, last = [], []
        for j in range(3):
            taps = [weight_ref[9 * i + 3 * j + k].astype(F32) for k in (2, 1, 0)]
            taps = jnp.concatenate(taps + [jnp.zeros((32, 32), F32)], axis=0)
            strip = jnp.concatenate([taps.T, jnp.zeros((32, 128), F32)], axis=1)
            for z in range(8):
                rolled = strip if z == 1 else pltpu.roll(strip, (32 * (z - 1)) % 256, 1)
                if z == 0:
                    first.append(jnp.where(lane >= 224, rolled, zero))
                    rolled = jnp.where(lane >= 224, zero, rolled)
                if z == 7:
                    last.append(jnp.where(lane < 32, rolled, zero))
                    rolled = jnp.where(lane < 32, zero, rolled)
                band_ref[i, pl.ds(256 * j + 32 * z, 32), :] = rolled.astype(BF16)
        order = [first[0], first[1], last[1], last[0], first[2], zero, zero, last[2]]
        for n, part in enumerate(order):
            band_ref[i, pl.ds(768 + 32 * n, 32), :] = part.astype(BF16)
        return carry

    lax.fori_loop(0, 3, per_x, 0)


def edge_lanes(low, high):
    lane = lax.broadcasted_iota(jnp.int32, low.shape, 1)
    a = jnp.where(lane < 32, low, pltpu.roll(low, 32, 1))
    b = jnp.where(lane < 96, pltpu.roll(high, 96, 1), high)
    return jnp.where(lane < 64, a, b)


def wait_bytes(ref, sem):
    pltpu.make_async_copy(ref, ref, sem).wait()


def kernel(
    owner_ref, cell_ref, face_ref, adj_ref, bias1_ref, bias2_ref, proj_ref, weight1_ref, weight2_ref,
    fine_hbm, cache_hbm, perm_hbm, up_hbm, out_ref,
    fine_ref, cache_ref, perm_ref, up_ref, code_ref, codes_ref, hot_ref, ans_ref, stage_ref, ret_ref, rank_ref,
    finep_ref, tile_ref, edge_ref, pad_ref, band1_ref, band2_ref, level_ref, par_ref,
    sum_ref, mix_ref, bias_ref, xs_ref, ys_ref, yrow_ref, xr_ref, yr_ref,
    send_sem, recv_sem, load_sem, pair_sem, block_sem, reply_sem,
):
    gx, gy = lax.axis_index("gx"), lax.axis_index("gy")
    nx, ny = lax.axis_size("gx"), lax.axis_size("gy")
    devices = nx * ny
    up_x, down_x = lax.rem(gx + 1, nx), lax.rem(gx + nx - 1, nx)
    up_y, down_y = lax.rem(gy + 1, ny), lax.rem(gy + ny - 1, ny)
    neighbours = [(up_x, gy), (down_x, gy), (gx, up_y), (gx, down_y)]
    me = gx * ny + gy
    chip, core = gx // 2, lax.rem(gx, 2)
    near = 2 * ny
    far = nx // 2
    spot = gy * 2 + core

    def near_device(k):
        at = lax.rem(spot + k, near)
        return (chip * 2 + lax.rem(at, 2), at // 2)

    def far_device(k):
        return (lax.rem(chip + k, far) * 2 + core, gy)

    barrier = pltpu.get_barrier_semaphore()
    for k in range(1, near):
        pl.semaphore_signal(barrier, inc=1, device_id=near_device(k), device_id_type=MESH)
    for k in range(1, far):
        pl.semaphore_signal(barrier, inc=1, device_id=far_device(k), device_id_type=MESH)
    loads = [
        pltpu.make_async_copy(src, dst, load_sem.at[n])
        for n, (src, dst) in enumerate(
            [(fine_hbm, fine_ref), (cache_hbm, cache_ref), (perm_hbm, perm_ref), (up_hbm, up_ref)]
        )
    ]
    for load in loads:
        load.start()

    lane = lax.broadcasted_iota(jnp.int32, (1, 128), 1)
    code = jnp.full((1, 128), -1, jnp.int32)
    for b in range(NB):
        code = jnp.where(lane == b, owner_ref[b] * 512 + cell_ref[b], code)
    code_ref[0:1] = code
    here = chip * near + spot
    codes_ref[pl.ds(here, 1)] = code

    pl.semaphore_wait(barrier, near + far - 2)

    own_row = codes_ref.at[pl.ds(here, 1)]
    for k in range(1, near):
        pltpu.make_async_remote_copy(
            src_ref=code_ref.at[pl.ds(0, 1)], dst_ref=own_row, send_sem=pair_sem.at[0], recv_sem=pair_sem.at[1],
            device_id=near_device(k), device_id_type=MESH).start()

    wait_bytes(codes_ref.at[pl.ds(0, near - 1)], pair_sem.at[0])
    wait_bytes(codes_ref.at[pl.ds(0, near - 1)], pair_sem.at[1])
    block = codes_ref.at[pl.ds(pl.multiple_of(chip * near, near), near)]
    for k in range(1, far):
        pltpu.make_async_remote_copy(
            src_ref=block, dst_ref=block, send_sem=block_sem.at[0], recv_sem=block_sem.at[1],
            device_id=far_device(k), device_id_type=MESH).start()
    loads[1].wait()
    wait_bytes(codes_ref.at[pl.ds(0, near * (far - 1))], block_sem.at[0])
    wait_bytes(codes_ref.at[pl.ds(0, near * (far - 1))], block_sem.at[1])

    codes = codes_ref[...]
    spots = lax.broadcasted_iota(jnp.int32, codes.shape, 1).astype(F32)
    match = (codes >> 9) == me
    cells = (codes & 511).astype(F32)
    lead = jnp.min(jnp.where(match, spots, 999.0), axis=1, keepdims=True)
    one = jnp.max(jnp.where(match & (spots == lead), cells, -1.0), axis=1, keepdims=True)
    two = jnp.max(jnp.where(match & (spots != lead), cells, -1.0), axis=1, keepdims=True)
    index = lax.broadcasted_iota(jnp.int32, (codes.shape[0], 512), 1).astype(F32)
    hot_ref[pl.ds(0, devices), :] = jnp.where(index == one, 1.0, 0.0).astype(BF16)
    hot_ref[pl.ds(devices, devices), :] = jnp.where(index == two, 1.0, 0.0).astype(BF16)

    def answer(n, carry):
        cols = pl.ds(pl.multiple_of(256 * n, 256), 256)
        rows = jnp.dot(hot_ref[...], cache_ref[:, cols], preferred_element_type=F32)
        height = 2 * devices
        ans_ref[pl.ds(pl.multiple_of(2 * n * height, height), height), :] = rows[:, :128]
        ans_ref[pl.ds(pl.multiple_of((2 * n + 1) * height, height), height), :] = rows[:, 128:]
        return carry

    lax.fori_loop(0, 8, answer, 0)

    def answer_to(dx, dy):
        at = dx // 2 * near + dy * 2 + lax.rem(dx, 2)
        first = ans_ref[pl.ds(at, 16, stride=2 * devices), :]
        second = ans_ref[pl.ds(devices + at, 16, stride=2 * devices), :]
        return first.astype(BF16), second.astype(BF16)

    mine = answer_to(gx, gy)
    ret_ref[2 * me] = mine[0]
    ret_ref[2 * me + 1] = mine[1]

    def reply(i, carry):
        to = lax.rem(me + lax.rem(51 * i, devices), devices)
        dx, dy = to // ny, lax.rem(to, ny)
        pair = answer_to(dx, dy)
        stage_ref[2 * to] = pair[0]
        stage_ref[2 * to + 1] = pair[1]
        pltpu.make_async_remote_copy(
            src_ref=stage_ref.at[pl.ds(2 * to, 2)], dst_ref=ret_ref.at[pl.ds(2 * me, 2)],
            send_sem=reply_sem.at[0], recv_sem=reply_sem.at[1],
            device_id=(dx, dy), device_id_type=MESH).start()
        return carry

    lax.fori_loop(1, devices, reply, 0)

    def ranks(b, carry):
        count = jnp.int32(0)
        for other in range(NB):
            same = (owner_ref[other] == owner_ref[b]) & (other < b)
            count = count + jnp.where(same, 1, 0)
        rank_ref[b] = owner_ref[b] * 2 + count
        return carry

    lax.fori_loop(0, NB, ranks, 0)
    build_band(weight1_ref, band1_ref)
    build_band(weight2_ref, band2_ref)
    yrow_ref[...] = jnp.zeros_like(yrow_ref)
    for x in range(8):
        tile_ref[x, 0] = jnp.zeros((8, 256), F32)
        edge_ref[x, 0] = jnp.zeros((8, 128), F32)
    lane = lax.broadcasted_iota(jnp.int32, (1, 256), 1)
    for n, ref in enumerate((bias1_ref, bias2_ref)):
        line = jnp.zeros((1, 256), F32)
        for o in range(32):
            line = jnp.where(lane % 32 == o, ref[o], line)
        bias_ref[n : n + 1] = line

    wide = jnp.concatenate([proj_ref[...]] * 8, axis=0)
    chan = lax.broadcasted_iota(jnp.int32, (32, 256), 0)
    lane = lax.broadcasted_iota(jnp.int32, (32, 256), 1)
    pick = jnp.where(chan == 2 * (lane % 16) + lane // 128, 1.0, 0.0).astype(BF16)
    spread = jnp.dot(wide, pick, preferred_element_type=F32)
    row = lax.broadcasted_iota(jnp.int32, (256, 256), 0)
    lane = lax.broadcasted_iota(jnp.int32, (256, 256), 1)
    mix_ref[...] = jnp.where(row // 32 == lane % 128 // 16, spread, 0.0).astype(BF16)

    for n in (0, 2, 3):
        loads[n].wait()

    def unfold(g, carry):
        fine = fine_ref[pl.ds(pl.multiple_of(8 * g, 8), 8)].reshape(256, 512)
        rows = pl.ds(pl.multiple_of(256 * g, 256), 256)
        finep_ref[rows, :] = jnp.dot(fine, perm_ref[...], preferred_element_type=F32)
        return carry

    lax.fori_loop(0, 4, unfold, 0)
    wait_bytes(ret_ref.at[pl.ds(0, 2 * devices - 2)], reply_sem.at[0])
    wait_bytes(ret_ref.at[pl.ds(0, 2 * devices - 2)], reply_sem.at[1])

    def place(x, slot, tile):
        tile_ref[x, slot] = tile
        edge_ref[x, slot] = edge_lanes(tile[:, :128], tile[:, 128:])

    def fetch(b, carry):
        par_ref[pl.ds(pl.multiple_of(16 * b, 16), 16), :] = ret_ref[rank_ref[b]]
        return carry

    lax.fori_loop(0, NB, fetch, 0)

    def level(g, carry):
        rows = pl.ds(pl.multiple_of(256 * g, 256), 256)
        pair = par_ref[pl.ds(pl.multiple_of(128 * g, 128), 128), :]
        both = jnp.dot(pair, up_ref[...], preferred_element_type=F32).astype(BF16)
        stack = jnp.concatenate([both[:, :512], both[:, 512:]], axis=0)
        mapped = jnp.dot(mix_ref[...], stack, preferred_element_type=F32)
        rounded = (finep_ref[rows, :] + mapped).astype(BF16)
        level_ref[rows, :] = rounded
        wide = rounded.astype(F32)
        for n in range(8):
            own = wide[32 * n : 32 * n + 32, :]
            square = jnp.concatenate([own[:, 128 * k : 128 * k + 128] for k in range(4)], axis=0)
            turned = square.T
            for x in range(8):
                low, high = turned[8 * x : 8 * x + 8], turned[64 + 8 * x : 72 + 8 * x]
                place(x, 8 * g + n + 1, jnp.concatenate([low, high], axis=1))
        return carry

    lax.fori_loop(0, 4, level, 0)

    row8 = lax.broadcasted_iota(jnp.int32, (8, 256), 0)
    row8e = lax.broadcasted_iota(jnp.int32, (8, 128), 0)
    lane8e = lax.broadcasted_iota(jnp.int32, (8, 128), 1)

    def copy_of(turn, src, dst, kind, other):
        return pltpu.make_async_remote_copy(
            src_ref=src, dst_ref=dst, send_sem=send_sem.at[turn, kind], recv_sem=recv_sem.at[turn, kind],
            device_id=neighbours[other], device_id_type=MESH)

    def x_copies(turn):
        return [copy_of(turn, xs_ref.at[turn, d], xr_ref.at[turn, d], d, d) for d in range(2)]

    def y_copies(turn, group):
        return [
            copy_of(turn, ys_ref.at[turn, d, group], yr_ref.at[turn, d, group], 2 + 2 * d + group, 2 + d)
            for d in range(2)
        ]

    def send_x(turn):
        for d, copy in enumerate(x_copies(turn)):
            x = 7 if d == 0 else 0
            for j in range(0, 8, 2):
                two = jnp.concatenate(
                    [tile_ref[x, face_ref[8 * d + j] + 1], tile_ref[x, face_ref[8 * d + j + 1] + 1]], axis=0
                )
                xs_ref[turn, d, pl.ds(8 * j, 16), :] = two.astype(BF16)
            copy.start()

    def send_y(turn, group):
        for d, copy in enumerate(y_copies(turn, group)):
            y = 7 if d == 0 else 0
            for j in range(2):
                at = face_ref[16 + 2 * d + j] + 1
                for n, x in enumerate(GROUPS[group]):
                    yrow_ref[pl.ds(8 * j + n, 1), :] = tile_ref[x, at, pl.ds(y, 1), :]
            ys_ref[turn, d, group] = yrow_ref[...].astype(BF16)
            copy.start()

    def land_x(turn):
        for d, copy in enumerate(x_copies(turn)):
            copy.wait()
            here = (gx > 0) if d == 0 else (gx < nx - 1)
            for j in range(8):
                if j % 2 == 0:
                    two = xr_ref[turn, d, pl.ds(8 * j, 16), :].astype(F32)
                    two = jnp.where(here, two, 0.0)
                place(7 if d == 0 else 0, 33 + 8 * d + j, two[8 * (j % 2) : 8 * (j % 2) + 8])

    def land_y(turn, group):
        for d, copy in enumerate(y_copies(turn, group)):
            copy.wait()
            here = (gy > 0) if d == 0 else (gy < ny - 1)
            rows = jnp.where(here, yr_ref[turn, d, group].astype(F32), 0.0)
            for j in range(2):
                for n, x in enumerate(GROUPS[group]):
                    line = rows[8 * j + n : 8 * j + n + 1]
                    place(x, 49 + 2 * d + j, jnp.broadcast_to(line, (8, 256)))

    def padded_tile(b, px):
        dx = -1 if px == 0 else (1 if px == 9 else 0)
        x = 7 if px == 0 else (0 if px == 9 else px - 1)

        def at(dy, dz):
            if dx == 0 and dy == 0 and dz == 0:
                return b + 1
            return adj_ref[b, column_of(dx, dy, dz)] + 1

        mid = tile_ref[x, at(0, 0)]
        low = pltpu.roll(jnp.where(row8 == 7, tile_ref[x, at(-1, 0)], mid), 1, 0)
        high = pltpu.roll(jnp.where(row8 == 0, tile_ref[x, at(1, 0)], mid), 7, 0)
        ends = [
            jnp.where(lane8e < 64, edge_ref[x, at(dy, 1)], edge_ref[x, at(dy, -1)])
            for dy in (-1, 0, 1)
        ]
        elow = pltpu.roll(jnp.where(row8e == 7, ends[0], ends[1]), 1, 0)
        ehigh = pltpu.roll(jnp.where(row8e == 0, ends[2], ends[1]), 7, 0)
        emid = jnp.where((lane8e >= 32) & (lane8e < 96), ends[1], elow)
        return jnp.concatenate([low, mid, high, emid, ehigh], axis=1)

    def pad_planes(planes):
        def per_pair(n, carry):
            for px in planes:
                two = jnp.concatenate([padded_tile(2 * n, px), padded_tile(2 * n + 1, px)], axis=0)
                pad_ref[px, pl.ds(pl.multiple_of(16 * n, 16), 16), :] = two.astype(BF16)
            return carry

        lax.fori_loop(0, NB // 2, per_pair, 0)

    def land_and_pad(turn):
        land_x(turn)
        land_y(turn, 0)
        pad_planes([0, 9] + [x + 1 for x in GROUPS[0]])
        land_y(turn, 1)
        pad_planes([x + 1 for x in GROUPS[1]])

    def conv(pair, band_ref, bias):
        total = bias_ref[pl.ds(bias, 1)]
        for i in range(3):
            rows = pad_ref[pl.ds(2 * pair + i, 2)].reshape(512, 1024)
            total = total + jnp.dot(rows, band_ref[i], preferred_element_type=F32)
        return total

    send_x(0)
    send_y(0, 0)
    send_y(0, 1)
    land_and_pad(0)

    def first(pair):
        v = conv(pair, band1_ref, 0)
        h = (v / (1.0 + jnp.exp(-v))).astype(BF16).astype(F32)
        tile_ref[pl.ds(2 * pair, 2), pl.ds(1, NB)] = h.reshape(2, NB, 8, 256)
        e = edge_lanes(h[:, :128], h[:, 128:])
        edge_ref[pl.ds(2 * pair, 2), pl.ds(1, NB)] = e.reshape(2, NB, 8, 128)

    def outer(n, carry):
        first(3 * n)
        return carry

    lax.fori_loop(0, 2, outer, 0)
    send_x(1)
    first(1)
    send_y(1, 0)
    first(2)
    send_y(1, 1)
    land_and_pad(1)

    def second(pair, carry):
        sum_ref[pl.ds(2 * pair, 2)] = conv(pair, band2_ref, 1).reshape(2, NB, 8, 256)
        return carry

    lax.fori_loop(0, 4, second, 0)

    def finish(g, carry):
        rows = pl.ds(pl.multiple_of(256 * g, 256), 256)
        parts = []
        for n in range(8):
            tall = [sum_ref[x, 8 * g + n] for x in range(8)]
            turned = jnp.concatenate([t[:, :128] for t in tall] + [t[:, 128:] for t in tall], axis=0).T
            parts.append(jnp.concatenate([turned[32 * k : 32 * k + 32] for k in range(4)], axis=1))
        total = jnp.concatenate(parts, axis=0) + level_ref[rows, :].astype(F32)
        out_ref[rows, :] = total.astype(BF16)
        return carry

    lax.fori_loop(0, 4, finish, 0)


def reorder(values_ref, perm_ref, out_ref):
    def part(g, carry):
        rows = values_ref[pl.ds(pl.multiple_of(256 * g, 256), 256)]
        rows = jnp.dot(rows, perm_ref[...], preferred_element_type=F32).astype(BF16)
        out_ref[pl.ds(8 * g, 8)] = rows.reshape(8, 32, 512)
        return carry

    lax.fori_loop(0, 4, part, 0)


def per_device(
    fine_features, coarse_cache, parent_owner, parent_cell, face_list, adjacency,
    parent_proj, conv_first, bias_first, conv_second, bias_second,
):
    devices = lax.axis_size("gx") * lax.axis_size("gy")
    perm, up = lane_tables()
    vmem = pl.BlockSpec(memory_space=pltpu.VMEM)
    smem = pl.BlockSpec(memory_space=pltpu.SMEM)
    hbm = pl.BlockSpec(memory_space=pl.ANY)
    out = pl.pallas_call(
        kernel,
        out_shape=jax.ShapeDtypeStruct((NB * 32, 512), BF16),
        in_specs=[smem] * 6 + [vmem] * 3 + [hbm] * 4,
        out_specs=vmem,
        scratch_shapes=[
            pltpu.VMEM((NB, 32, 512), BF16),
            pltpu.VMEM((512, 2048), BF16),
            pltpu.VMEM((512, 512), BF16),
            pltpu.VMEM((128, 1024), BF16),
            pltpu.VMEM((8, 128), jnp.int32),
            pltpu.VMEM((devices, 128), jnp.int32),
            pltpu.VMEM((2 * devices, 512), BF16),
            pltpu.VMEM((32 * devices, 128), F32),
            pltpu.VMEM((2 * devices, 16, 128), BF16),
            pltpu.VMEM((2 * devices, 16, 128), BF16),
            pltpu.SMEM((NB,), jnp.int32),
            pltpu.VMEM((NB * 32, 512), F32),
            pltpu.VMEM((8, SLOTS, 8, 256), F32),
            pltpu.VMEM((8, SLOTS, 8, 128), F32),
            pltpu.VMEM((10, 256, 1024), BF16),
            pltpu.VMEM((3, 1024, 256), BF16),
            pltpu.VMEM((3, 1024, 256), BF16),
            pltpu.VMEM((NB * 32, 512), BF16),
            pltpu.VMEM((NB * 16, 128), BF16),
            pltpu.VMEM((8, NB, 8, 256), F32),
            pltpu.VMEM((256, 256), BF16),
            pltpu.VMEM((8, 256), F32),
            pltpu.VMEM((2, 2, 64, 256), BF16),
            pltpu.VMEM((2, 2, 2, 16, 256), BF16),
            pltpu.VMEM((16, 256), F32),
            pltpu.VMEM((2, 2, 64, 256), BF16),
            pltpu.VMEM((2, 2, 2, 16, 256), BF16),
            pltpu.SemaphoreType.DMA((2, 6)),
            pltpu.SemaphoreType.DMA((2, 6)),
            pltpu.SemaphoreType.DMA((4,)),
            pltpu.SemaphoreType.DMA((2,)),
            pltpu.SemaphoreType.DMA((2,)),
            pltpu.SemaphoreType.DMA((2,)),
        ],
        compiler_params=pltpu.CompilerParams(
            collective_id=0, has_side_effects=True, vmem_limit_bytes=56 * 1024 * 1024
        ),
    )(
        parent_owner.reshape(NB), parent_cell, face_list, adjacency, bias_first, bias_second, parent_proj, conv_first,
        conv_second, fine_features, coarse_cache, jnp.asarray(perm, BF16), jnp.asarray(up, BF16),
    )
    return pl.pallas_call(
        reorder,
        out_shape=jax.ShapeDtypeStruct((NB, 32, 512), BF16),
        in_specs=[vmem] * 2,
        out_specs=vmem,
    )(out, jnp.asarray(perm.T, BF16))


def solution(mesh):
    placed = (
        P(("gx", "gy"), None, None),
        P(("gx", "gy"), None),
        P(("gx", "gy"), None),
        P(("gx", "gy")),
        P(("gx", "gy")),
        P(("gx", "gy"), None),
        P(),
        P(),
        P(),
        P(),
        P(),
    )
    return jax.shard_map(
        per_device,
        mesh=mesh,
        in_specs=placed,
        out_specs=P(("gx", "gy"), None, None),
        check_vma=False,
    )
```

```python
import jax
import jax.numpy as jnp
import numpy as np
from jax import lax
from jax.experimental import pallas as pl
from jax.experimental.pallas import tpu as pltpu
from jax.sharding import PartitionSpec as P

F32 = jnp.float32
BF16 = jnp.bfloat16
NB = 32
SLOTS = 53
MESH = pl.DeviceIdType.MESH
GROUPS = [[0, 1, 6, 7, 2, 3], [4, 5]]


def column_of(dx, dy, dz):
    at = 9 * (dx + 1) + 3 * (dy + 1) + dz + 1
    return at if at < 13 else at - 1


def lane_tables():
    lane = np.arange(512)
    z = 4 * (lane // 64 % 2) + lane // 128
    x, y = lane % 64 // 8, lane % 8
    voxel = 64 * x + 8 * y + z
    cell = 16 * (x // 2) + 4 * (y // 2) + z // 2
    perm = (np.arange(512)[:, None] == voxel[None, :]).astype(np.float32)
    up = (np.arange(64)[:, None] == cell[None, :]).astype(np.float32)
    blank = np.zeros_like(up)
    even = np.concatenate([up, blank], 0)
    odd = np.concatenate([blank, up], 0)
    return perm, np.concatenate([even, odd], 1)


def face_tables():
    lane = np.arange(128)
    fixed, z, free = np.where(lane < 64, 7, 0), lane % 64 // 8, lane % 8
    picks, ups = [], []
    for x, y in ((fixed, free), (free, fixed)):
        voxel = 64 * x + 8 * y + z
        cell = 16 * (x // 2) + 4 * (y // 2) + z // 2
        picks.append((np.arange(512)[:, None] == voxel[None, :]).astype(np.float32))
        up = (np.arange(64)[:, None] == cell[None, :]).astype(np.float32)
        blank = np.zeros_like(up)
        ups.append(np.concatenate([np.concatenate([up, blank], 0), np.concatenate([blank, up], 0)], 1))
    return np.stack(picks), np.stack(ups)


def build_band(weight_ref, band_ref):
    lane = lax.broadcasted_iota(jnp.int32, (32, 256), 1)
    zero = jnp.zeros((32, 256), F32)

    def per_x(i, carry):
        first, last = [], []
        for j in range(3):
            taps = [weight_ref[9 * i + 3 * j + k].astype(F32) for k in (2, 1, 0)]
            taps = jnp.concatenate(taps + [jnp.zeros((32, 32), F32)], axis=0)
            strip = jnp.concatenate([taps.T, jnp.zeros((32, 128), F32)], axis=1)
            for z in range(8):
                rolled = strip if z == 1 else pltpu.roll(strip, (32 * (z - 1)) % 256, 1)
                if z == 0:
                    first.append(jnp.where(lane >= 224, rolled, zero))
                    rolled = jnp.where(lane >= 224, zero, rolled)
                if z == 7:
                    last.append(jnp.where(lane < 32, rolled, zero))
                    rolled = jnp.where(lane < 32, zero, rolled)
                band_ref[i, pl.ds(256 * j + 32 * z, 32), :] = rolled.astype(BF16)
        order = [first[0], first[1], last[1], last[0], first[2], zero, zero, last[2]]
        for n, part in enumerate(order):
            band_ref[i, pl.ds(768 + 32 * n, 32), :] = part.astype(BF16)
        return carry

    lax.fori_loop(0, 3, per_x, 0)


def edge_lanes(low, high):
    lane = lax.broadcasted_iota(jnp.int32, low.shape, 1)
    a = jnp.where(lane < 32, low, pltpu.roll(low, 32, 1))
    b = jnp.where(lane < 96, pltpu.roll(high, 96, 1), high)
    return jnp.where(lane < 64, a, b)


def wait_bytes(ref, sem):
    pltpu.make_async_copy(ref, ref, sem).wait()


def kernel(
    owner_hbm, cell_hbm, face_hbm, adj_hbm, bias1_hbm, bias2_hbm, proj_hbm, weight1_hbm, weight2_hbm,
    fine_hbm, cache_hbm, perm_hbm, unperm_hbm, up_hbm, pick_hbm, pickup_hbm, out_hbm,
    owner_ref, cell_ref, face_ref, adj_ref, bias1_ref, bias2_ref, proj_ref, weight1_ref, weight2_ref,
    fine_ref, cache_ref, perm_ref, unperm_ref, up_ref, pick_ref, pickup_ref, code_ref, codes_ref, hot_ref, ans_ref, stage_ref, ret_ref, rank_ref,
    finep_ref, side_ref, sidep_ref, tile_ref, edge_ref, pad_ref, band1_ref, band2_ref, level_ref, par_ref,
    sum_ref, mix_ref, bias_ref, xs_ref, ys_ref, yrow_ref, row_ref, xr_ref, yr_ref,
    send_sem, recv_sem, load_sem, out_sem, pair_sem, block_sem, reply_sem,
):
    gx, gy = lax.axis_index("gx"), lax.axis_index("gy")
    nx, ny = lax.axis_size("gx"), lax.axis_size("gy")
    devices = nx * ny
    up_x, down_x = lax.rem(gx + 1, nx), lax.rem(gx + nx - 1, nx)
    up_y, down_y = lax.rem(gy + 1, ny), lax.rem(gy + ny - 1, ny)
    neighbours = [(up_x, gy), (down_x, gy), (gx, up_y), (gx, down_y)]
    me = gx * ny + gy
    chip, core = gx // 2, lax.rem(gx, 2)
    near = 2 * ny
    far = nx // 2
    spot = gy * 2 + core

    def near_device(k):
        at = lax.rem(spot + k, near)
        return (chip * 2 + lax.rem(at, 2), at // 2)

    def far_device(k):
        return (lax.rem(chip + k, far) * 2 + core, gy)

    barrier = pltpu.get_barrier_semaphore()
    for k in range(1, near):
        pl.semaphore_signal(barrier, inc=1, device_id=near_device(k), device_id_type=MESH)
    for k in range(1, far):
        pl.semaphore_signal(barrier, inc=1, device_id=far_device(k), device_id_type=MESH)
    pairs = [
        (owner_hbm, owner_ref), (cell_hbm, cell_ref), (cache_hbm, cache_ref), (face_hbm, face_ref),
        (adj_hbm, adj_ref), (bias1_hbm, bias1_ref), (bias2_hbm, bias2_ref), (proj_hbm, proj_ref),
        (weight1_hbm, weight1_ref), (weight2_hbm, weight2_ref), (fine_hbm, fine_ref), (perm_hbm, perm_ref),
        (unperm_hbm, unperm_ref), (up_hbm, up_ref), (pick_hbm, pick_ref), (pickup_hbm, pickup_ref),
    ]
    loads = [pltpu.make_async_copy(src, dst, load_sem.at[n]) for n, (src, dst) in enumerate(pairs)]
    for load in loads:
        load.start()
    loads[0].wait()
    loads[1].wait()

    lane = lax.broadcasted_iota(jnp.int32, (1, 128), 1)
    code = jnp.full((1, 128), -1, jnp.int32)
    for b in range(NB):
        code = jnp.where(lane == b, owner_ref[b] * 512 + cell_ref[b], code)
    code_ref[0:1] = code
    here = chip * near + spot
    codes_ref[pl.ds(here, 1)] = code

    pl.semaphore_wait(barrier, near + far - 2)

    own_row = codes_ref.at[pl.ds(here, 1)]
    for k in range(1, near):
        pltpu.make_async_remote_copy(
            src_ref=code_ref.at[pl.ds(0, 1)], dst_ref=own_row, send_sem=pair_sem.at[0], recv_sem=pair_sem.at[1],
            device_id=near_device(k), device_id_type=MESH).start()

    wait_bytes(codes_ref.at[pl.ds(0, near - 1)], pair_sem.at[1])
    block = codes_ref.at[pl.ds(pl.multiple_of(chip * near, near), near)]
    for k in range(1, far):
        pltpu.make_async_remote_copy(
            src_ref=block, dst_ref=block, send_sem=block_sem.at[0], recv_sem=block_sem.at[1],
            device_id=far_device(k), device_id_type=MESH).start()
    loads[2].wait()
    wait_bytes(codes_ref.at[pl.ds(0, near * (far - 1))], block_sem.at[1])

    half = devices // 2
    index = lax.broadcasted_iota(jnp.int32, (half, 512), 1).astype(F32)

    def answers(turn, its_core, start):
        codes = codes_ref[pl.ds(its_core, half, stride=2), :]
        spots = lax.broadcasted_iota(jnp.int32, codes.shape, 1).astype(F32)
        match = (codes >> 9) == me
        cells = (codes & 511).astype(F32)
        lead = jnp.min(jnp.where(match, spots, 999.0), axis=1, keepdims=True)
        one = jnp.max(jnp.where(match & (spots == lead), cells, -1.0), axis=1, keepdims=True)
        two = jnp.max(jnp.where(match & (spots != lead), cells, -1.0), axis=1, keepdims=True)
        hot_ref[turn, pl.ds(0, half), :] = jnp.where(index == one, 1.0, 0.0).astype(BF16)
        hot_ref[turn, pl.ds(half, half), :] = jnp.where(index == two, 1.0, 0.0).astype(BF16)

        def answer(n, carry):
            cols = pl.ds(pl.multiple_of(256 * n, 256), 256)
            rows = jnp.dot(hot_ref[turn], cache_ref[:, cols], preferred_element_type=F32)
            ans_ref[turn, pl.ds(pl.multiple_of(2 * n * devices, devices), devices), :] = rows[:, :128]
            ans_ref[turn, pl.ds(pl.multiple_of((2 * n + 1) * devices, devices), devices), :] = rows[:, 128:]
            return carry

        lax.fori_loop(0, 8, answer, 0)

        def answer_to(at):
            first = ans_ref[turn, pl.ds(at, 16, stride=devices), :]
            second = ans_ref[turn, pl.ds(half + at, 16, stride=devices), :]
            return first.astype(BF16), second.astype(BF16)

        if turn == 0:
            mine = answer_to(chip * ny + gy)
            ret_ref[2 * me] = mine[0]
            ret_ref[2 * me + 1] = mine[1]

        def reply(i, carry):
            at = lax.rem(chip * ny + gy + 27 * i, half)
            dx, dy = at // ny * 2 + its_core, lax.rem(at, ny)
            to = dx * ny + dy
            pair = answer_to(at)
            stage_ref[2 * to] = pair[0]
            stage_ref[2 * to + 1] = pair[1]
            pltpu.make_async_remote_copy(
                src_ref=stage_ref.at[pl.ds(2 * to, 2)], dst_ref=ret_ref.at[pl.ds(2 * me, 2)],
                send_sem=reply_sem.at[0], recv_sem=reply_sem.at[1],
                device_id=(dx, dy), device_id_type=MESH).start()
            return carry

        lax.fori_loop(start, half, reply, 0)

    answers(0, core, 1)
    answers(1, 1 - core, 0)

    for load in loads[3:]:
        load.wait()

    def ranks(b, carry):
        count = jnp.int32(0)
        for other in range(NB):
            same = (owner_ref[other] == owner_ref[b]) & (other < b)
            count = count + jnp.where(same, 1, 0)
        rank_ref[b] = owner_ref[b] * 2 + count
        return carry

    lax.fori_loop(0, NB, ranks, 0)
    build_band(weight1_ref, band1_ref)
    build_band(weight2_ref, band2_ref)
    yrow_ref[...] = jnp.zeros_like(yrow_ref)
    row_ref[...] = jnp.zeros_like(row_ref)
    for x in range(8):
        tile_ref[x, 0] = jnp.zeros((8, 256), F32)
        edge_ref[x, 0] = jnp.zeros((8, 128), F32)
    lane = lax.broadcasted_iota(jnp.int32, (1, 256), 1)
    for n, ref in enumerate((bias1_ref, bias2_ref)):
        line = jnp.zeros((1, 256), F32)
        for o in range(32):
            line = jnp.where(lane % 32 == o, ref[o], line)
        bias_ref[n : n + 1] = line

    wide = jnp.concatenate([proj_ref[...]] * 8, axis=0)
    chan = lax.broadcasted_iota(jnp.int32, (32, 256), 0)
    lane = lax.broadcasted_iota(jnp.int32, (32, 256), 1)
    pick = jnp.where(chan == 2 * (lane % 16) + lane // 128, 1.0, 0.0).astype(BF16)
    spread = jnp.dot(wide, pick, preferred_element_type=F32)
    row = lax.broadcasted_iota(jnp.int32, (256, 256), 0)
    lane = lax.broadcasted_iota(jnp.int32, (256, 256), 1)
    mix_ref[...] = jnp.where(row // 32 == lane % 128 // 16, spread, 0.0).astype(BF16)

    def unfold(g, carry):
        fine = fine_ref[pl.ds(pl.multiple_of(8 * g, 8), 8)].reshape(256, 512)
        rows = pl.ds(pl.multiple_of(256 * g, 256), 256)
        finep_ref[rows, :] = jnp.dot(fine, perm_ref[...], preferred_element_type=F32)
        return carry

    lax.fori_loop(0, 4, unfold, 0)

    def listed(group, n):
        return face_ref[8 * group + n] if group < 2 else face_ref[16 + n % 4]

    for group in range(3):
        for n in range(8):
            side_ref[group, n] = fine_ref[listed(group, n)]
        sidep_ref[group] = jnp.dot(
            side_ref[group].reshape(256, 512), pick_ref[group // 2], preferred_element_type=F32
        )
    wait_bytes(ret_ref.at[pl.ds(0, 2 * devices - 2)], reply_sem.at[1])

    def place(x, slot, tile):
        tile_ref[x, slot] = tile
        edge_ref[x, slot] = edge_lanes(tile[:, :128], tile[:, 128:])

    def copy_of(turn, src, dst, kind, other):
        return pltpu.make_async_remote_copy(
            src_ref=src, dst_ref=dst, send_sem=send_sem.at[turn, kind], recv_sem=recv_sem.at[turn, kind],
            device_id=neighbours[other], device_id_type=MESH)

    def x_copies(turn):
        return [copy_of(turn, xs_ref.at[turn, d], xr_ref.at[turn, d], d, d) for d in range(2)]

    def y_copies(turn, group):
        return [
            copy_of(turn, ys_ref.at[turn, d, group], yr_ref.at[turn, d, group], 2 + 2 * d + group, 2 + d)
            for d in range(2)
        ]

    def side_tiles(group):
        pair = jnp.concatenate([ret_ref[rank_ref[listed(group, n)]] for n in range(8)], axis=0)
        both = jnp.dot(pair, pickup_ref[group // 2], preferred_element_type=F32).astype(BF16)
        stack = jnp.concatenate([both[:, :128], both[:, 128:]], axis=0)
        mapped = jnp.dot(mix_ref[...], stack, preferred_element_type=F32)
        level = (sidep_ref[group] + mapped).astype(BF16).astype(F32)
        turned = [level[:128].T, level[128:].T]
        tiles = []
        for n in range(8 if group < 2 else 4):
            side = 64 * (group if group < 2 else n // 2)
            source = turned[n // 4]
            tiles.append(jnp.concatenate(
                [source[side + 8 * z : side + 8 * z + 8, 32 * (n % 4) : 32 * (n % 4) + 32] for z in range(8)], axis=1
            ))
        return tiles

    for d in range(2):
        xs_ref[0, d] = jnp.concatenate(side_tiles(d), axis=0).astype(BF16)
    for d, copy in enumerate(x_copies(0)):
        copy.start()
    lines = side_tiles(2)
    for d in range(2):
        for j in range(2):
            yrow_ref[pl.ds(8 * j, 8), :] = lines[2 * d + j]
        for group in range(2):
            for j in range(2):
                for n, x in enumerate(GROUPS[group]):
                    row_ref[pl.ds(8 * j + n, 1), :] = yrow_ref[pl.ds(8 * j + x, 1), :]
            ys_ref[0, d, group] = row_ref[...].astype(BF16)
    for group in range(2):
        for copy in y_copies(0, group):
            copy.start()

    def fetch(b, carry):
        par_ref[pl.ds(pl.multiple_of(16 * b, 16), 16), :] = ret_ref[rank_ref[b]]
        return carry

    lax.fori_loop(0, NB, fetch, 0)

    def level(g, carry):
        rows = pl.ds(pl.multiple_of(256 * g, 256), 256)
        pair = par_ref[pl.ds(pl.multiple_of(128 * g, 128), 128), :]
        both = jnp.dot(pair, up_ref[...], preferred_element_type=F32).astype(BF16)
        stack = jnp.concatenate([both[:, :512], both[:, 512:]], axis=0)
        mapped = jnp.dot(mix_ref[...], stack, preferred_element_type=F32)
        rounded = (finep_ref[rows, :] + mapped).astype(BF16)
        level_ref[rows, :] = rounded
        wide = rounded.astype(F32)
        for n in range(8):
            own = wide[32 * n : 32 * n + 32, :]
            square = jnp.concatenate([own[:, 128 * k : 128 * k + 128] for k in range(4)], axis=0)
            turned = square.T
            for x in range(8):
                low, high = turned[8 * x : 8 * x + 8], turned[64 + 8 * x : 72 + 8 * x]
                place(x, 8 * g + n + 1, jnp.concatenate([low, high], axis=1))
        return carry

    lax.fori_loop(0, 4, level, 0)

    row8 = lax.broadcasted_iota(jnp.int32, (8, 256), 0)
    row8e = lax.broadcasted_iota(jnp.int32, (8, 128), 0)
    lane8e = lax.broadcasted_iota(jnp.int32, (8, 128), 1)

    def send_x(turn):
        for d, copy in enumerate(x_copies(turn)):
            x = 7 if d == 0 else 0
            for j in range(0, 8, 2):
                two = jnp.concatenate(
                    [tile_ref[x, face_ref[8 * d + j] + 1], tile_ref[x, face_ref[8 * d + j + 1] + 1]], axis=0
                )
                xs_ref[turn, d, pl.ds(8 * j, 16), :] = two.astype(BF16)
            copy.start()

    def send_y(turn, group):
        for d, copy in enumerate(y_copies(turn, group)):
            y = 7 if d == 0 else 0
            for j in range(2):
                at = face_ref[16 + 2 * d + j] + 1
                for n, x in enumerate(GROUPS[group]):
                    yrow_ref[pl.ds(8 * j + n, 1), :] = tile_ref[x, at, pl.ds(y, 1), :]
            ys_ref[turn, d, group] = yrow_ref[...].astype(BF16)
            copy.start()

    def land_x(turn):
        for d, copy in enumerate(x_copies(turn)):
            copy.wait_recv()
            here = (gx > 0) if d == 0 else (gx < nx - 1)
            for j in range(8):
                if j % 2 == 0:
                    two = xr_ref[turn, d, pl.ds(8 * j, 16), :].astype(F32)
                    two = jnp.where(here, two, 0.0)
                place(7 if d == 0 else 0, 33 + 8 * d + j, two[8 * (j % 2) : 8 * (j % 2) + 8])

    def land_y(turn, group):
        for d, copy in enumerate(y_copies(turn, group)):
            copy.wait_recv()
            here = (gy > 0) if d == 0 else (gy < ny - 1)
            rows = jnp.where(here, yr_ref[turn, d, group].astype(F32), 0.0)
            for j in range(2):
                for n, x in enumerate(GROUPS[group]):
                    line = rows[8 * j + n : 8 * j + n + 1]
                    place(x, 49 + 2 * d + j, jnp.broadcast_to(line, (8, 256)))

    def padded_tile(near_by, px):
        dx = -1 if px == 0 else (1 if px == 9 else 0)
        x = 7 if px == 0 else (0 if px == 9 else px - 1)

        def at(dy, dz):
            return near_by[dx, dy, dz]

        mid = tile_ref[x, at(0, 0)]
        low = pltpu.roll(jnp.where(row8 == 7, tile_ref[x, at(-1, 0)], mid), 1, 0)
        high = pltpu.roll(jnp.where(row8 == 0, tile_ref[x, at(1, 0)], mid), 7, 0)
        ends = [
            jnp.where(lane8e < 64, edge_ref[x, at(dy, 1)], edge_ref[x, at(dy, -1)])
            for dy in (-1, 0, 1)
        ]
        elow = pltpu.roll(jnp.where(row8e == 7, ends[0], ends[1]), 1, 0)
        ehigh = pltpu.roll(jnp.where(row8e == 0, ends[2], ends[1]), 7, 0)
        emid = jnp.where((lane8e >= 32) & (lane8e < 96), ends[1], elow)
        return jnp.concatenate([low, mid, high, emid, ehigh], axis=1)

    def pad_planes(planes):
        steps = sorted({-1 if px == 0 else (1 if px == 9 else 0) for px in planes})

        def slots(b):
            return {
                (dx, dy, dz): b + 1 if dx == dy == dz == 0 else adj_ref[b, column_of(dx, dy, dz)] + 1
                for dx in steps for dy in (-1, 0, 1) for dz in (-1, 0, 1)
            }

        def per_pair(n, carry):
            even, odd = slots(2 * n), slots(2 * n + 1)
            for px in planes:
                two = jnp.concatenate([padded_tile(even, px), padded_tile(odd, px)], axis=0)
                pad_ref[px, pl.ds(pl.multiple_of(16 * n, 16), 16), :] = two.astype(BF16)
            return carry

        lax.fori_loop(0, NB // 2, per_pair, 0)

    def land_and_pad(turn):
        land_x(turn)
        land_y(turn, 0)
        pad_planes([0, 9] + [x + 1 for x in GROUPS[0]])
        land_y(turn, 1)
        pad_planes([x + 1 for x in GROUPS[1]])

    def conv(first_plane, planes, band_ref, bias):
        total = bias_ref[pl.ds(bias, 1)]
        for i in range(3):
            rows = pad_ref[pl.ds(first_plane + i, planes)].reshape(256 * planes, 1024)
            total = total + jnp.dot(rows, band_ref[i], preferred_element_type=F32)
        return total

    land_and_pad(0)

    def first(pair):
        v = conv(2 * pair, 2, band1_ref, 0)
        half = 0.5 * v
        h = (half + half * jnp.tanh(half)).astype(BF16).astype(F32)
        tile_ref[pl.ds(2 * pair, 2), pl.ds(1, NB)] = h.reshape(2, NB, 8, 256)
        e = edge_lanes(h[:, :128], h[:, 128:])
        edge_ref[pl.ds(2 * pair, 2), pl.ds(1, NB)] = e.reshape(2, NB, 8, 128)

    def outer(n, carry):
        first(3 * n)
        return carry

    lax.fori_loop(0, 2, outer, 0)
    send_x(1)
    first(1)
    send_y(1, 0)
    first(2)
    send_y(1, 1)
    land_and_pad(1)

    def second(pair, carry):
        sum_ref[pl.ds(4 * pair, 4)] = conv(4 * pair, 4, band2_ref, 1).reshape(4, NB, 8, 256)
        return carry

    lax.fori_loop(0, 2, second, 0)

    def finish(g, carry):
        rows = pl.ds(pl.multiple_of(256 * g, 256), 256)
        parts = []
        for n in range(8):
            tall = [sum_ref[x, 8 * g + n] for x in range(8)]
            turned = jnp.concatenate([t[:, :128] for t in tall] + [t[:, 128:] for t in tall], axis=0).T
            parts.append(jnp.concatenate([turned[32 * k : 32 * k + 32] for k in range(4)], axis=1))
        total = jnp.concatenate(parts, axis=0) + level_ref[rows, :].astype(F32)
        rows = jnp.dot(total.astype(BF16), unperm_ref[...], preferred_element_type=F32).astype(BF16)
        bricks = pl.ds(pl.multiple_of(8 * g, 8), 8)
        fine_ref[bricks] = rows.reshape(8, 32, 512)
        pltpu.make_async_copy(fine_ref.at[bricks], out_hbm.at[bricks], out_sem).start()
        return carry

    lax.fori_loop(0, 4, finish, 0)
    for turn in range(2):
        for copy in x_copies(turn) + y_copies(turn, 0) + y_copies(turn, 1):
            copy.wait_send()
    wait_bytes(codes_ref.at[pl.ds(0, near - 1)], pair_sem.at[0])
    wait_bytes(codes_ref.at[pl.ds(0, near * (far - 1))], block_sem.at[0])
    wait_bytes(ret_ref.at[pl.ds(0, 2 * devices - 2)], reply_sem.at[0])
    pltpu.make_async_copy(fine_ref, out_hbm, out_sem).wait()


def hand_on(values_hbm, out_hbm, held, sem):
    parts = [pl.ds(4 * n, 4) for n in range(8)]
    into = [pltpu.make_async_copy(values_hbm.at[p], held.at[p], sem.at[0, n]) for n, p in enumerate(parts)]
    onward = [pltpu.make_async_copy(held.at[p], out_hbm.at[p], sem.at[1, n]) for n, p in enumerate(parts)]
    for copy in into:
        copy.start()
    for before, after in zip(into, onward):
        before.wait()
        after.start()
    for copy in onward:
        copy.wait()


def per_device(
    fine_features, coarse_cache, parent_owner, parent_cell, face_list, adjacency,
    parent_proj, conv_first, bias_first, conv_second, bias_second,
):
    devices = lax.axis_size("gx") * lax.axis_size("gy")
    perm, up = lane_tables()
    pick, pickup = face_tables()
    hbm = pl.BlockSpec(memory_space=pl.ANY)
    out = pl.pallas_call(
        kernel,
        out_shape=jax.ShapeDtypeStruct((NB, 32, 512), BF16),
        in_specs=[hbm] * 16,
        out_specs=hbm,
        scratch_shapes=[
            pltpu.SMEM((NB,), jnp.int32),
            pltpu.SMEM((NB,), jnp.int32),
            pltpu.SMEM((20,), jnp.int32),
            pltpu.SMEM((NB, 26), jnp.int32),
            pltpu.SMEM((32,), F32),
            pltpu.SMEM((32,), F32),
            pltpu.VMEM((32, 32), BF16),
            pltpu.VMEM((27, 32, 32), BF16),
            pltpu.VMEM((27, 32, 32), BF16),
            pltpu.VMEM((NB, 32, 512), BF16),
            pltpu.VMEM((512, 2048), BF16),
            pltpu.VMEM((512, 512), BF16),
            pltpu.VMEM((512, 512), BF16),
            pltpu.VMEM((128, 1024), BF16),
            pltpu.VMEM((2, 512, 128), BF16),
            pltpu.VMEM((2, 128, 256), BF16),
            pltpu.VMEM((8, 128), jnp.int32),
            pltpu.VMEM((devices, 128), jnp.int32),
            pltpu.VMEM((2, devices, 512), BF16),
            pltpu.VMEM((2, 16 * devices, 128), F32),
            pltpu.VMEM((2 * devices, 16, 128), BF16),
            pltpu.VMEM((2 * devices, 16, 128), BF16),
            pltpu.SMEM((NB,), jnp.int32),
            pltpu.VMEM((NB * 32, 512), F32),
            pltpu.VMEM((3, 8, 32, 512), BF16),
            pltpu.VMEM((3, 256, 128), F32),
            pltpu.VMEM((8, SLOTS, 8, 256), F32),
            pltpu.VMEM((8, SLOTS, 8, 128), F32),
            pltpu.VMEM((10, 256, 1024), BF16),
            pltpu.VMEM((3, 1024, 256), BF16),
            pltpu.VMEM((3, 1024, 256), BF16),
            pltpu.VMEM((NB * 32, 512), BF16),
            pltpu.VMEM((NB * 16, 128), BF16),
            pltpu.VMEM((8, NB, 8, 256), F32),
            pltpu.VMEM((256, 256), BF16),
            pltpu.VMEM((8, 256), F32),
            pltpu.VMEM((2, 2, 64, 256), BF16),
            pltpu.VMEM((2, 2, 2, 16, 256), BF16),
            pltpu.VMEM((16, 256), F32),
            pltpu.VMEM((16, 256), F32),
            pltpu.VMEM((2, 2, 64, 256), BF16),
            pltpu.VMEM((2, 2, 2, 16, 256), BF16),
            pltpu.SemaphoreType.DMA((2, 6)),
            pltpu.SemaphoreType.DMA((2, 6)),
            pltpu.SemaphoreType.DMA((16,)),
            pltpu.SemaphoreType.DMA,
            pltpu.SemaphoreType.DMA((2,)),
            pltpu.SemaphoreType.DMA((2,)),
            pltpu.SemaphoreType.DMA((2,)),
        ],
        compiler_params=pltpu.CompilerParams(
            collective_id=0, has_side_effects=True, vmem_limit_bytes=56 * 1024 * 1024
        ),
    )(
        parent_owner.reshape(NB), parent_cell, face_list, adjacency, bias_first, bias_second, parent_proj, conv_first,
        conv_second, fine_features, coarse_cache, jnp.asarray(perm, BF16),
        jnp.asarray(perm.T, BF16), jnp.asarray(up, BF16),
        jnp.asarray(pick, BF16), jnp.asarray(pickup, BF16),
    )
    return pl.pallas_call(
        hand_on,
        out_shape=jax.ShapeDtypeStruct((NB, 32, 512), BF16),
        in_specs=[hbm],
        out_specs=hbm,
        scratch_shapes=[pltpu.VMEM((NB, 32, 512), BF16), pltpu.SemaphoreType.DMA((2, 8))],
    )(out)


def solution(mesh):
    placed = (
        P(("gx", "gy"), None, None),
        P(("gx", "gy"), None),
        P(("gx", "gy"), None),
        P(("gx", "gy")),
        P(("gx", "gy")),
        P(("gx", "gy"), None),
        P(),
        P(),
        P(),
        P(),
        P(),
    )
    return jax.shard_map(
        per_device,
        mesh=mesh,
        in_specs=placed,
        out_specs=P(("gx", "gy"), None, None),
        check_vma=False,
    )
```

```python
import jax
import jax.numpy as jnp
import numpy as np
from jax import lax
from jax.experimental import pallas as pl
from jax.experimental.pallas import tpu as pltpu
from jax.sharding import PartitionSpec as P

F32 = jnp.float32
BF16 = jnp.bfloat16
NB = 32
SLOTS = 53
MESH = pl.DeviceIdType.MESH
GROUPS = [[0, 1, 6, 7, 2, 3], [4, 5]]


def column_of(dx, dy, dz):
    at = 9 * (dx + 1) + 3 * (dy + 1) + dz + 1
    return at if at < 13 else at - 1


def lane_tables():
    lane = np.arange(512)
    x, row = lane % 64 // 8, lane % 8
    y, z = 2 * (row // 2) + lane // 64 % 2, 4 * (row % 2) + lane // 128
    voxel = 64 * x + 8 * y + z
    cell = 16 * (x // 2) + 4 * (y // 2) + z // 2
    perm = (np.arange(512)[:, None] == voxel[None, :]).astype(np.float32)
    up = (np.arange(64)[:, None] == cell[None, :]).astype(np.float32)
    blank = np.zeros_like(up)
    even = np.concatenate([up, blank], 0)
    odd = np.concatenate([blank, up], 0)
    return perm, np.concatenate([even, odd], 1)


def face_tables():
    lane = np.arange(128)
    fixed, at = np.where(lane < 64, 7, 0), lane % 64
    part, row = at // 8, at % 8
    across_x = (fixed, 2 * (row // 2) + part // 4, 4 * (row % 2) + part % 4)
    across_y = (at % 16 // 2, fixed, 4 * (at % 2) + at // 16)
    picks, ups = [], []
    for x, y, z in (across_x, across_y):
        voxel = 64 * x + 8 * y + z
        cell = 16 * (x // 2) + 4 * (y // 2) + z // 2
        picks.append((np.arange(512)[:, None] == voxel[None, :]).astype(np.float32))
        up = (np.arange(64)[:, None] == cell[None, :]).astype(np.float32)
        blank = np.zeros_like(up)
        ups.append(np.concatenate([np.concatenate([up, blank], 0), np.concatenate([blank, up], 0)], 1))
    return np.stack(picks), np.stack(ups)


def build_band(weight_ref, band_ref):
    block = lax.broadcasted_iota(jnp.int32, (32, 128), 1) // 32
    zero = jnp.zeros((32, 128), F32)

    def per_x(i, carry):
        moved = {}
        for j in range(3):
            taps = [weight_ref[9 * i + 3 * j + k].astype(F32) for k in (2, 1, 0)]
            strip = jnp.concatenate(taps + [jnp.zeros((32, 32), F32)], axis=0).T
            for z in range(-1, 5):
                rolled = strip if z == 1 else pltpu.roll(strip, (32 * (z - 1)) % 128, 1)
                fits = (block >= z - 1) & (block <= z + 1)
                moved[j, z] = jnp.where(fits, rolled, 0.0)
        order = [(y, z) for y in (0, 1, -1, 2) for z in range(4)]
        order += [(0, 4), (1, 4), (0, -1), (1, -1), (2, 4), (-1, 4), (2, -1), (-1, -1)]
        for n, (y, z) in enumerate(order):
            halves = [moved[y + 1, z] if y < 2 else zero, moved[y, z] if y > -1 else zero]
            band_ref[i, pl.ds(32 * n, 32), :] = jnp.concatenate(halves, axis=1).astype(BF16)
        return carry

    lax.fori_loop(0, 3, per_x, 0)


def edge_lanes(low, high):
    axes = low.ndim
    lane = lax.broadcasted_iota(jnp.int32, low.shape, axes - 1)
    row = lax.broadcasted_iota(jnp.int32, low.shape, axes - 2)
    a = jnp.where(lane < 32, low, pltpu.roll(high, 32, axes - 1))
    b = jnp.where(lane < 96, pltpu.roll(low, 96, axes - 1), high)
    ends = jnp.where(lane < 64, a, b)
    return jnp.where(row % 2 == 0, pltpu.roll(ends, 7, axes - 2), pltpu.roll(ends, 1, axes - 2))


def wait_bytes(ref, sem):
    pltpu.make_async_copy(ref, ref, sem).wait()


def kernel(
    owner_hbm, cell_hbm, face_hbm, adj_hbm, bias1_hbm, bias2_hbm, proj_hbm, weight1_hbm, weight2_hbm,
    fine_hbm, cache_hbm, perm_hbm, unperm_hbm, up_hbm, pick_hbm, pickup_hbm, out_hbm,
    owner_ref, cell_ref, face_ref, adj_ref, bias1_ref, bias2_ref, proj_ref, weight1_ref, weight2_ref,
    fine_ref, cache_ref, perm_ref, unperm_ref, up_ref, pick_ref, pickup_ref, code_ref, codes_ref, hot_ref, ans_ref, stage_ref, ret_ref, rank_ref,
    finep_ref, side_ref, sidep_ref, tile_ref, edge_ref, pad_ref, band1_ref, band2_ref, level_ref, par_ref,
    sum_ref, mix_ref, bias_ref, xs_ref, ys_ref, yrow_ref, row_ref, xr_ref, yr_ref,
    send_sem, recv_sem, load_sem, out_sem, pair_sem, block_sem, reply_sem,
):
    gx, gy = lax.axis_index("gx"), lax.axis_index("gy")
    nx, ny = lax.axis_size("gx"), lax.axis_size("gy")
    devices = nx * ny
    up_x, down_x = lax.rem(gx + 1, nx), lax.rem(gx + nx - 1, nx)
    up_y, down_y = lax.rem(gy + 1, ny), lax.rem(gy + ny - 1, ny)
    neighbours = [(up_x, gy), (down_x, gy), (gx, up_y), (gx, down_y)]
    me = gx * ny + gy
    chip, core = gx // 2, lax.rem(gx, 2)
    near = 2 * ny
    far = nx // 2
    spot = gy * 2 + core

    def near_device(k):
        at = lax.rem(spot + k, near)
        return (chip * 2 + lax.rem(at, 2), at // 2)

    def far_device(k):
        return (lax.rem(chip + k, far) * 2 + core, gy)

    barrier = pltpu.get_barrier_semaphore()
    for k in range(1, near):
        pl.semaphore_signal(barrier, inc=1, device_id=near_device(k), device_id_type=MESH)
    for k in range(1, far):
        pl.semaphore_signal(barrier, inc=1, device_id=far_device(k), device_id_type=MESH)
    pairs = [
        (owner_hbm, owner_ref), (cell_hbm, cell_ref), (cache_hbm, cache_ref), (face_hbm, face_ref),
        (adj_hbm, adj_ref), (bias1_hbm, bias1_ref), (bias2_hbm, bias2_ref), (proj_hbm, proj_ref),
        (weight1_hbm, weight1_ref), (weight2_hbm, weight2_ref), (fine_hbm, fine_ref), (perm_hbm, perm_ref),
        (unperm_hbm, unperm_ref), (up_hbm, up_ref), (pick_hbm, pick_ref), (pickup_hbm, pickup_ref),
    ]
    loads = [pltpu.make_async_copy(src, dst, load_sem.at[n]) for n, (src, dst) in enumerate(pairs)]
    for load in loads:
        load.start()
    loads[0].wait()
    loads[1].wait()

    lane = lax.broadcasted_iota(jnp.int32, (1, 128), 1)
    code = jnp.full((1, 128), -1, jnp.int32)
    for b in range(NB):
        code = jnp.where(lane == b, owner_ref[b] * 512 + cell_ref[b], code)
    code_ref[0:1] = code
    here = chip * near + spot
    codes_ref[pl.ds(here, 1)] = code

    pl.semaphore_wait(barrier, near + far - 2)

    own_row = codes_ref.at[pl.ds(here, 1)]
    for k in range(1, near):
        pltpu.make_async_remote_copy(
            src_ref=code_ref.at[pl.ds(0, 1)], dst_ref=own_row, send_sem=pair_sem.at[0], recv_sem=pair_sem.at[1],
            device_id=near_device(k), device_id_type=MESH).start()

    wait_bytes(codes_ref.at[pl.ds(0, near - 1)], pair_sem.at[1])
    block = codes_ref.at[pl.ds(pl.multiple_of(chip * near, near), near)]
    for k in range(1, far):
        pltpu.make_async_remote_copy(
            src_ref=block, dst_ref=block, send_sem=block_sem.at[0], recv_sem=block_sem.at[1],
            device_id=far_device(k), device_id_type=MESH).start()
    loads[2].wait()
    wait_bytes(codes_ref.at[pl.ds(0, near * (far - 1))], block_sem.at[1])

    half = devices // 2
    index = lax.broadcasted_iota(jnp.int32, (half, 512), 1).astype(F32)

    def answers(turn, its_core, start):
        codes = codes_ref[pl.ds(its_core, half, stride=2), :]
        spots = lax.broadcasted_iota(jnp.int32, codes.shape, 1).astype(F32)
        match = (codes >> 9) == me
        cells = (codes & 511).astype(F32)
        lead = jnp.min(jnp.where(match, spots, 999.0), axis=1, keepdims=True)
        one = jnp.max(jnp.where(match & (spots == lead), cells, -1.0), axis=1, keepdims=True)
        two = jnp.max(jnp.where(match & (spots != lead), cells, -1.0), axis=1, keepdims=True)
        hot_ref[turn, pl.ds(0, half), :] = jnp.where(index == one, 1.0, 0.0).astype(BF16)
        hot_ref[turn, pl.ds(half, half), :] = jnp.where(index == two, 1.0, 0.0).astype(BF16)

        def answer(n, carry):
            cols = pl.ds(pl.multiple_of(256 * n, 256), 256)
            rows = jnp.dot(hot_ref[turn], cache_ref[:, cols], preferred_element_type=F32)
            ans_ref[turn, pl.ds(pl.multiple_of(2 * n * devices, devices), devices), :] = rows[:, :128]
            ans_ref[turn, pl.ds(pl.multiple_of((2 * n + 1) * devices, devices), devices), :] = rows[:, 128:]
            return carry

        lax.fori_loop(0, 8, answer, 0)

        def answer_to(at):
            first = ans_ref[turn, pl.ds(at, 16, stride=devices), :]
            second = ans_ref[turn, pl.ds(half + at, 16, stride=devices), :]
            return first.astype(BF16), second.astype(BF16)

        if turn == 0:
            mine = answer_to(chip * ny + gy)
            ret_ref[2 * me] = mine[0]
            ret_ref[2 * me + 1] = mine[1]

        def reply(i, carry):
            at = lax.rem(chip * ny + gy + 27 * i, half)
            dx, dy = at // ny * 2 + its_core, lax.rem(at, ny)
            to = dx * ny + dy
            pair = answer_to(at)
            stage_ref[2 * to] = pair[0]
            stage_ref[2 * to + 1] = pair[1]
            pltpu.make_async_remote_copy(
                src_ref=stage_ref.at[pl.ds(2 * to, 2)], dst_ref=ret_ref.at[pl.ds(2 * me, 2)],
                send_sem=reply_sem.at[0], recv_sem=reply_sem.at[1],
                device_id=(dx, dy), device_id_type=MESH).start()
            return carry

        lax.fori_loop(start, half, reply, 0)

    answers(0, core, 1)
    answers(1, 1 - core, 0)

    for load in loads[3:]:
        load.wait()

    def ranks(b, carry):
        count = jnp.int32(0)
        for other in range(NB):
            same = (owner_ref[other] == owner_ref[b]) & (other < b)
            count = count + jnp.where(same, 1, 0)
        rank_ref[b] = owner_ref[b] * 2 + count
        return carry

    lax.fori_loop(0, NB, ranks, 0)
    build_band(weight1_ref, band1_ref)
    build_band(weight2_ref, band2_ref)
    yrow_ref[...] = jnp.zeros_like(yrow_ref)
    row_ref[...] = jnp.zeros_like(row_ref)
    for x in range(8):
        tile_ref[x, 0] = jnp.zeros((8, 256), F32)
        edge_ref[x, 0] = jnp.zeros((8, 128), F32)
    lane = lax.broadcasted_iota(jnp.int32, (1, 256), 1)
    for n, ref in enumerate((bias1_ref, bias2_ref)):
        line = jnp.zeros((1, 256), F32)
        for o in range(32):
            line = jnp.where(lane % 32 == o, ref[o], line)
        bias_ref[n : n + 1] = line

    wide = jnp.concatenate([proj_ref[...]] * 8, axis=0)
    chan = lax.broadcasted_iota(jnp.int32, (32, 256), 0)
    lane = lax.broadcasted_iota(jnp.int32, (32, 256), 1)
    pick = jnp.where(chan == 2 * (lane % 16) + lane // 128, 1.0, 0.0).astype(BF16)
    spread = jnp.dot(wide, pick, preferred_element_type=F32)
    row = lax.broadcasted_iota(jnp.int32, (256, 256), 0)
    lane = lax.broadcasted_iota(jnp.int32, (256, 256), 1)
    mix_ref[...] = jnp.where(row // 32 == lane % 128 // 16, spread, 0.0).astype(BF16)

    def unfold(g, carry):
        fine = fine_ref[pl.ds(pl.multiple_of(8 * g, 8), 8)].reshape(256, 512)
        rows = pl.ds(pl.multiple_of(256 * g, 256), 256)
        finep_ref[rows, :] = jnp.dot(fine, perm_ref[...], preferred_element_type=F32)
        return carry

    lax.fori_loop(0, 4, unfold, 0)

    def listed(group, n):
        return face_ref[8 * group + n] if group < 2 else face_ref[16 + n % 4]

    for group in range(3):
        for n in range(8):
            side_ref[group, n] = fine_ref[listed(group, n)]
        sidep_ref[group] = jnp.dot(
            side_ref[group].reshape(256, 512), pick_ref[group // 2], preferred_element_type=F32
        )
    wait_bytes(ret_ref.at[pl.ds(0, 2 * devices - 2)], reply_sem.at[1])

    def place(x, slot, tile):
        tile_ref[x, slot] = tile
        edge_ref[x, slot] = edge_lanes(tile[:, :128], tile[:, 128:])

    def copy_of(turn, src, dst, kind, other):
        return pltpu.make_async_remote_copy(
            src_ref=src, dst_ref=dst, send_sem=send_sem.at[turn, kind], recv_sem=recv_sem.at[turn, kind],
            device_id=neighbours[other], device_id_type=MESH)

    def x_copies(turn):
        return [copy_of(turn, xs_ref.at[turn, d], xr_ref.at[turn, d], d, d) for d in range(2)]

    def y_copies(turn, group):
        return [
            copy_of(turn, ys_ref.at[turn, d, group], yr_ref.at[turn, d, group], 2 + 2 * d + group, 2 + d)
            for d in range(2)
        ]

    def side_tiles(group):
        pair = jnp.concatenate([ret_ref[rank_ref[listed(group, n)]] for n in range(8)], axis=0)
        both = jnp.dot(pair, pickup_ref[group // 2], preferred_element_type=F32).astype(BF16)
        stack = jnp.concatenate([both[:, :128], both[:, 128:]], axis=0)
        mapped = jnp.dot(mix_ref[...], stack, preferred_element_type=F32)
        level = (sidep_ref[group] + mapped).astype(BF16).astype(F32)
        turned = [level[:128].T, level[128:].T]
        tiles = []
        for n in range(8 if group < 2 else 4):
            side = 64 * (group if group < 2 else n // 2)
            source = turned[n // 4]
            tall = 8 if group < 2 else 16
            tiles.append(jnp.concatenate(
                [source[side + at : side + at + tall, 32 * (n % 4) : 32 * (n % 4) + 32] for at in range(0, 64, tall)],
                axis=1,
            ))
        return tiles

    for d in range(2):
        xs_ref[0, d] = jnp.concatenate(side_tiles(d), axis=0).astype(BF16)
    for d, copy in enumerate(x_copies(0)):
        copy.start()
    lines = side_tiles(2)
    for d in range(2):
        for j in range(2):
            yrow_ref[:, pl.ds(128 * j, 128)] = lines[2 * d + j]
        for group in range(2):
            for n, x in enumerate(GROUPS[group]):
                row_ref[pl.ds(2 * n, 2), :] = yrow_ref[pl.ds(2 * x, 2), :]
            ys_ref[0, d, group] = row_ref[...].astype(BF16)
    for group in range(2):
        for copy in y_copies(0, group):
            copy.start()

    def fetch(b, carry):
        par_ref[pl.ds(pl.multiple_of(16 * b, 16), 16), :] = ret_ref[rank_ref[b]]
        return carry

    lax.fori_loop(0, NB, fetch, 0)

    def level(g, carry):
        rows = pl.ds(pl.multiple_of(256 * g, 256), 256)
        pair = par_ref[pl.ds(pl.multiple_of(128 * g, 128), 128), :]
        both = jnp.dot(pair, up_ref[...], preferred_element_type=F32).astype(BF16)
        stack = jnp.concatenate([both[:, :512], both[:, 512:]], axis=0)
        mapped = jnp.dot(mix_ref[...], stack, preferred_element_type=F32)
        rounded = (finep_ref[rows, :] + mapped).astype(BF16)
        level_ref[rows, :] = rounded
        wide = rounded.astype(F32)
        for n in range(8):
            own = wide[32 * n : 32 * n + 32, :]
            square = jnp.concatenate([own[:, 128 * k : 128 * k + 128] for k in range(4)], axis=0)
            turned = square.T
            for x in range(8):
                low, high = turned[8 * x : 8 * x + 8], turned[64 + 8 * x : 72 + 8 * x]
                place(x, 8 * g + n + 1, jnp.concatenate([low, high], axis=1))
        return carry

    lax.fori_loop(0, 4, level, 0)

    row8 = lax.broadcasted_iota(jnp.int32, (8, 128), 0)
    lane8 = lax.broadcasted_iota(jnp.int32, (8, 128), 1)
    inner = (lane8 < 64) == (row8 % 2 == 0)

    def send_x(turn):
        for d, copy in enumerate(x_copies(turn)):
            x = 7 if d == 0 else 0
            for j in range(0, 8, 2):
                two = jnp.concatenate(
                    [tile_ref[x, face_ref[8 * d + j] + 1], tile_ref[x, face_ref[8 * d + j + 1] + 1]], axis=0
                )
                xs_ref[turn, d, pl.ds(8 * j, 16), :] = two.astype(BF16)
            copy.start()

    def send_y(turn, group):
        for d, copy in enumerate(y_copies(turn, group)):
            row, side = (6, 128) if d == 0 else (0, 0)
            for j in range(2):
                at = face_ref[16 + 2 * d + j] + 1
                for n, x in enumerate(GROUPS[group]):
                    yrow_ref[pl.ds(2 * n, 2), pl.ds(128 * j, 128)] = tile_ref[x, at, pl.ds(row, 2), pl.ds(side, 128)]
            ys_ref[turn, d, group] = yrow_ref[...].astype(BF16)
            copy.start()

    def land_x(turn):
        for d, copy in enumerate(x_copies(turn)):
            copy.wait_recv()
            here = (gx > 0) if d == 0 else (gx < nx - 1)
            for j in range(8):
                if j % 2 == 0:
                    two = xr_ref[turn, d, pl.ds(8 * j, 16), :].astype(F32)
                    two = jnp.where(here, two, 0.0)
                place(7 if d == 0 else 0, 33 + 8 * d + j, two[8 * (j % 2) : 8 * (j % 2) + 8])

    def land_y(turn, group):
        for d, copy in enumerate(y_copies(turn, group)):
            copy.wait_recv()
            here = (gy > 0) if d == 0 else (gy < ny - 1)
            rows = jnp.where(here, yr_ref[turn, d, group].astype(F32), 0.0)
            for j in range(2):
                for n, x in enumerate(GROUPS[group]):
                    lines = rows[2 * n : 2 * n + 2, 128 * j : 128 * j + 128]
                    even = jnp.broadcast_to(lines[:1], (8, 128))
                    half = jnp.where(row8 % 2 == 0, even, jnp.broadcast_to(lines[1:], (8, 128)))
                    place(x, 49 + 2 * d + j, jnp.concatenate([half, half], axis=1))

    def padded_tile(near_by, px):
        dx = -1 if px == 0 else (1 if px == 9 else 0)
        x = 7 if px == 0 else (0 if px == 9 else px - 1)

        def at(dy, dz):
            return near_by[dx, dy, dz]

        def ends(dy):
            outer = jnp.where(lane8 < 64, edge_ref[x, at(dy, 1)], edge_ref[x, at(dy, -1)])
            return jnp.where(inner, edge_ref[x, at(dy, 0)], outer)

        mid = tile_ref[x, at(0, 0)]
        below = tile_ref[x, at(-1, 0), :, pl.ds(128, 128)]
        above = tile_ref[x, at(1, 0), :, pl.ds(0, 128)]
        low = pltpu.roll(jnp.where(row8 >= 6, below, mid[:, 128:]), 2, 0)
        high = pltpu.roll(jnp.where(row8 < 2, above, mid[:, :128]), 6, 0)
        here = ends(0)
        clow = pltpu.roll(jnp.where(row8 >= 6, ends(-1), here), 2, 0)
        chigh = pltpu.roll(jnp.where(row8 < 2, ends(1), here), 6, 0)
        corners = jnp.where(lane8 // 32 % 2 == 1, clow, chigh)
        return jnp.concatenate([mid, low, high, here, corners], axis=1)

    def pad_planes(planes):
        steps = sorted({-1 if px == 0 else (1 if px == 9 else 0) for px in planes})

        def slots(b):
            return {
                (dx, dy, dz): b + 1 if dx == dy == dz == 0 else adj_ref[b, column_of(dx, dy, dz)] + 1
                for dx in steps for dy in (-1, 0, 1) for dz in (-1, 0, 1)
            }

        def per_pair(n, carry):
            even, odd = slots(2 * n), slots(2 * n + 1)
            for px in planes:
                two = jnp.concatenate([padded_tile(even, px), padded_tile(odd, px)], axis=0)
                pad_ref[px, pl.ds(pl.multiple_of(16 * n, 16), 16), :] = two.astype(BF16)
            return carry

        lax.fori_loop(0, NB // 2, per_pair, 0)

    def land_and_pad(turn):
        land_x(turn)
        land_y(turn, 0)
        pad_planes([0, 9] + [x + 1 for x in GROUPS[0]])
        land_y(turn, 1)
        pad_planes([x + 1 for x in GROUPS[1]])

    def conv(first_plane, planes, band_ref, bias):
        total = bias_ref[pl.ds(bias, 1)]
        for i in range(3):
            rows = pad_ref[pl.ds(first_plane + i, planes)].reshape(256 * planes, 768)
            total = total + jnp.dot(rows, band_ref[i], preferred_element_type=F32)
        return total

    land_and_pad(0)

    def first(pair):
        v = conv(2 * pair, 2, band1_ref, 0)
        half = 0.5 * v
        h = (half + half * jnp.tanh(half)).astype(BF16).astype(F32)
        tile_ref[pl.ds(2 * pair, 2), pl.ds(1, NB)] = h.reshape(2, NB, 8, 256)
        e = edge_lanes(h[:, :128].reshape(2 * NB, 8, 128), h[:, 128:].reshape(2 * NB, 8, 128))
        edge_ref[pl.ds(2 * pair, 2), pl.ds(1, NB)] = e.reshape(2, NB, 8, 128)

    def outer(n, carry):
        first(3 * n)
        return carry

    lax.fori_loop(0, 2, outer, 0)
    send_x(1)
    first(1)
    send_y(1, 0)
    first(2)
    send_y(1, 1)
    land_and_pad(1)

    def second(pair, carry):
        sum_ref[pl.ds(4 * pair, 4)] = conv(4 * pair, 4, band2_ref, 1).reshape(4, NB, 8, 256)
        return carry

    lax.fori_loop(0, 2, second, 0)

    def finish(g, carry):
        rows = pl.ds(pl.multiple_of(256 * g, 256), 256)
        parts = []
        for n in range(8):
            tall = [sum_ref[x, 8 * g + n] for x in range(8)]
            turned = jnp.concatenate([t[:, :128] for t in tall] + [t[:, 128:] for t in tall], axis=0).T
            parts.append(jnp.concatenate([turned[32 * k : 32 * k + 32] for k in range(4)], axis=1))
        total = jnp.concatenate(parts, axis=0) + level_ref[rows, :].astype(F32)
        rows = jnp.dot(total.astype(BF16), unperm_ref[...], preferred_element_type=F32).astype(BF16)
        bricks = pl.ds(pl.multiple_of(8 * g, 8), 8)
        fine_ref[bricks] = rows.reshape(8, 32, 512)
        pltpu.make_async_copy(fine_ref.at[bricks], out_hbm.at[bricks], out_sem).start()
        return carry

    lax.fori_loop(0, 4, finish, 0)
    for turn in range(2):
        for copy in x_copies(turn) + y_copies(turn, 0) + y_copies(turn, 1):
            copy.wait_send()
    wait_bytes(codes_ref.at[pl.ds(0, near - 1)], pair_sem.at[0])
    wait_bytes(codes_ref.at[pl.ds(0, near * (far - 1))], block_sem.at[0])
    wait_bytes(ret_ref.at[pl.ds(0, 2 * devices - 2)], reply_sem.at[0])
    pltpu.make_async_copy(fine_ref, out_hbm, out_sem).wait()


def hand_on(values_hbm, out_hbm, held, sem):
    parts = [pl.ds(4 * n, 4) for n in range(8)]
    into = [pltpu.make_async_copy(values_hbm.at[p], held.at[p], sem.at[0, n]) for n, p in enumerate(parts)]
    onward = [pltpu.make_async_copy(held.at[p], out_hbm.at[p], sem.at[1, n]) for n, p in enumerate(parts)]
    for copy in into:
        copy.start()
    for before, after in zip(into, onward):
        before.wait()
        after.start()
    for copy in onward:
        copy.wait()


def per_device(
    fine_features, coarse_cache, parent_owner, parent_cell, face_list, adjacency,
    parent_proj, conv_first, bias_first, conv_second, bias_second,
):
    devices = lax.axis_size("gx") * lax.axis_size("gy")
    perm, up = lane_tables()
    pick, pickup = face_tables()
    hbm = pl.BlockSpec(memory_space=pl.ANY)
    out = pl.pallas_call(
        kernel,
        out_shape=jax.ShapeDtypeStruct((NB, 32, 512), BF16),
        in_specs=[hbm] * 16,
        out_specs=hbm,
        scratch_shapes=[
            pltpu.SMEM((NB,), jnp.int32),
            pltpu.SMEM((NB,), jnp.int32),
            pltpu.SMEM((20,), jnp.int32),
            pltpu.SMEM((NB, 26), jnp.int32),
            pltpu.SMEM((32,), F32),
            pltpu.SMEM((32,), F32),
            pltpu.VMEM((32, 32), BF16),
            pltpu.VMEM((27, 32, 32), BF16),
            pltpu.VMEM((27, 32, 32), BF16),
            pltpu.VMEM((NB, 32, 512), BF16),
            pltpu.VMEM((512, 2048), BF16),
            pltpu.VMEM((512, 512), BF16),
            pltpu.VMEM((512, 512), BF16),
            pltpu.VMEM((128, 1024), BF16),
            pltpu.VMEM((2, 512, 128), BF16),
            pltpu.VMEM((2, 128, 256), BF16),
            pltpu.VMEM((8, 128), jnp.int32),
            pltpu.VMEM((devices, 128), jnp.int32),
            pltpu.VMEM((2, devices, 512), BF16),
            pltpu.VMEM((2, 16 * devices, 128), F32),
            pltpu.VMEM((2 * devices, 16, 128), BF16),
            pltpu.VMEM((2 * devices, 16, 128), BF16),
            pltpu.SMEM((NB,), jnp.int32),
            pltpu.VMEM((NB * 32, 512), F32),
            pltpu.VMEM((3, 8, 32, 512), BF16),
            pltpu.VMEM((3, 256, 128), F32),
            pltpu.VMEM((8, SLOTS, 8, 256), F32),
            pltpu.VMEM((8, SLOTS, 8, 128), F32),
            pltpu.VMEM((10, 256, 768), BF16),
            pltpu.VMEM((3, 768, 256), BF16),
            pltpu.VMEM((3, 768, 256), BF16),
            pltpu.VMEM((NB * 32, 512), BF16),
            pltpu.VMEM((NB * 16, 128), BF16),
            pltpu.VMEM((8, NB, 8, 256), F32),
            pltpu.VMEM((256, 256), BF16),
            pltpu.VMEM((8, 256), F32),
            pltpu.VMEM((2, 2, 64, 256), BF16),
            pltpu.VMEM((2, 2, 2, 16, 256), BF16),
            pltpu.VMEM((16, 256), F32),
            pltpu.VMEM((16, 256), F32),
            pltpu.VMEM((2, 2, 64, 256), BF16),
            pltpu.VMEM((2, 2, 2, 16, 256), BF16),
            pltpu.SemaphoreType.DMA((2, 6)),
            pltpu.SemaphoreType.DMA((2, 6)),
            pltpu.SemaphoreType.DMA((16,)),
            pltpu.SemaphoreType.DMA,
            pltpu.SemaphoreType.DMA((2,)),
            pltpu.SemaphoreType.DMA((2,)),
            pltpu.SemaphoreType.DMA((2,)),
        ],
        compiler_params=pltpu.CompilerParams(
            collective_id=0, has_side_effects=True, vmem_limit_bytes=56 * 1024 * 1024
        ),
    )(
        parent_owner.reshape(NB), parent_cell, face_list, adjacency, bias_first, bias_second, parent_proj, conv_first,
        conv_second, fine_features, coarse_cache, jnp.asarray(perm, BF16),
        jnp.asarray(perm.T, BF16), jnp.asarray(up, BF16),
        jnp.asarray(pick, BF16), jnp.asarray(pickup, BF16),
    )
    return pl.pallas_call(
        hand_on,
        out_shape=jax.ShapeDtypeStruct((NB, 32, 512), BF16),
        in_specs=[hbm],
        out_specs=hbm,
        scratch_shapes=[pltpu.VMEM((NB, 32, 512), BF16), pltpu.SemaphoreType.DMA((2, 8))],
    )(out)


def solution(mesh):
    placed = (
        P(("gx", "gy"), None, None),
        P(("gx", "gy"), None),
        P(("gx", "gy"), None),
        P(("gx", "gy")),
        P(("gx", "gy")),
        P(("gx", "gy"), None),
        P(),
        P(),
        P(),
        P(),
        P(),
    )
    return jax.shard_map(
        per_device,
        mesh=mesh,
        in_specs=placed,
        out_specs=P(("gx", "gy"), None, None),
        check_vma=False,
    )
```

```python
import jax
import jax.numpy as jnp
import numpy as np
from jax import lax
from jax.experimental import pallas as pl
from jax.experimental.pallas import tpu as pltpu
from jax.sharding import PartitionSpec as P

F32 = jnp.float32
BF16 = jnp.bfloat16
NB = 32
SLOTS = 53
MESH = pl.DeviceIdType.MESH
GROUPS = [[0, 1, 6, 7, 2, 3], [4, 5]]


def column_of(dx, dy, dz):
    at = 9 * (dx + 1) + 3 * (dy + 1) + dz + 1
    return at if at < 13 else at - 1


def lane_tables():
    lane = np.arange(512)
    x, row = lane % 64 // 8, lane % 8
    y, z = 2 * (row // 2) + lane // 64 % 2, 4 * (row % 2) + lane // 128
    voxel = 64 * x + 8 * y + z
    cell = 16 * (x // 2) + 4 * (y // 2) + z // 2
    perm = (np.arange(512)[:, None] == voxel[None, :]).astype(np.float32)
    up = (np.arange(64)[:, None] == cell[None, :]).astype(np.float32)
    blank = np.zeros_like(up)
    even = np.concatenate([up, blank], 0)
    odd = np.concatenate([blank, up], 0)
    return perm, np.concatenate([even, odd], 1)


def face_tables():
    lane = np.arange(128)
    fixed, at = np.where(lane < 64, 7, 0), lane % 64
    part, row = at // 8, at % 8
    across_x = (fixed, 2 * (row // 2) + part // 4, 4 * (row % 2) + part % 4)
    across_y = (at % 16 // 2, fixed, 4 * (at % 2) + at // 16)
    picks, ups = [], []
    for x, y, z in (across_x, across_y):
        voxel = 64 * x + 8 * y + z
        cell = 16 * (x // 2) + 4 * (y // 2) + z // 2
        picks.append((np.arange(512)[:, None] == voxel[None, :]).astype(np.float32))
        up = (np.arange(64)[:, None] == cell[None, :]).astype(np.float32)
        blank = np.zeros_like(up)
        ups.append(np.concatenate([np.concatenate([up, blank], 0), np.concatenate([blank, up], 0)], 1))
    return np.stack(picks), np.stack(ups)


def build_band(weight_ref, band_ref):
    block = lax.broadcasted_iota(jnp.int32, (32, 128), 1) // 32
    zero = jnp.zeros((32, 128), F32)

    def per_x(i, carry):
        moved = {}
        for j in range(3):
            taps = [weight_ref[9 * i + 3 * j + k].astype(F32) for k in (2, 1, 0)]
            strip = jnp.concatenate(taps + [jnp.zeros((32, 32), F32)], axis=0).T
            for z in range(-1, 5):
                rolled = strip if z == 1 else pltpu.roll(strip, (32 * (z - 1)) % 128, 1)
                fits = (block >= z - 1) & (block <= z + 1)
                moved[j, z] = jnp.where(fits, rolled, 0.0)
        order = [(y, z) for y in (0, 1, -1, 2) for z in range(4)]
        order += [(0, 4), (1, 4), (0, -1), (1, -1), (2, 4), (-1, 4), (2, -1), (-1, -1)]
        for n, (y, z) in enumerate(order):
            halves = [moved[y + 1, z] if y < 2 else zero, moved[y, z] if y > -1 else zero]
            band_ref[i, pl.ds(32 * n, 32), :] = jnp.concatenate(halves, axis=1).astype(BF16)
        return carry

    lax.fori_loop(0, 3, per_x, 0)


def edge_lanes(low, high):
    axes = low.ndim
    lane = lax.broadcasted_iota(jnp.int32, low.shape, axes - 1)
    row = lax.broadcasted_iota(jnp.int32, low.shape, axes - 2)
    a = jnp.where(lane < 32, low, pltpu.roll(high, 32, axes - 1))
    b = jnp.where(lane < 96, pltpu.roll(low, 96, axes - 1), high)
    ends = jnp.where(lane < 64, a, b)
    return jnp.where(row % 2 == 0, pltpu.roll(ends, 7, axes - 2), pltpu.roll(ends, 1, axes - 2))


def wait_bytes(ref, sem):
    pltpu.make_async_copy(ref, ref, sem).wait()


def kernel(
    owner_hbm, cell_hbm, face_hbm, adj_hbm, bias1_hbm, bias2_hbm, proj_hbm, weight1_hbm, weight2_hbm,
    fine_hbm, cache_hbm, perm_hbm, unperm_hbm, up_hbm, pick_hbm, pickup_hbm, out_hbm,
    owner_ref, cell_ref, face_ref, adj_ref, bias1_ref, bias2_ref, proj_ref, weight1_ref, weight2_ref,
    fine_ref, cache_ref, perm_ref, unperm_ref, up_ref, pick_ref, pickup_ref, code_ref, codes_ref, hot_ref, ans_ref, stage_ref, ret_ref, rank_ref,
    finep_ref, side_ref, sidep_ref, tile_ref, pad_ref, band1_ref, band2_ref, level_ref, par_ref,
    sum_ref, mix_ref, bias_ref, xs_ref, ys_ref, yrow_ref, row_ref, xr_ref, yr_ref,
    send_sem, recv_sem, load_sem, out_sem, pair_sem, block_sem, reply_sem,
):
    gx, gy = lax.axis_index("gx"), lax.axis_index("gy")
    nx, ny = lax.axis_size("gx"), lax.axis_size("gy")
    devices = nx * ny
    up_x, down_x = lax.rem(gx + 1, nx), lax.rem(gx + nx - 1, nx)
    up_y, down_y = lax.rem(gy + 1, ny), lax.rem(gy + ny - 1, ny)
    neighbours = [(up_x, gy), (down_x, gy), (gx, up_y), (gx, down_y)]
    me = gx * ny + gy
    chip, core = gx // 2, lax.rem(gx, 2)
    near = 2 * ny
    far = nx // 2
    spot = gy * 2 + core

    def near_device(k):
        at = lax.rem(spot + k, near)
        return (chip * 2 + lax.rem(at, 2), at // 2)

    def far_device(k):
        return (lax.rem(chip + k, far) * 2 + core, gy)

    barrier = pltpu.get_barrier_semaphore()
    for k in range(1, near):
        pl.semaphore_signal(barrier, inc=1, device_id=near_device(k), device_id_type=MESH)
    for k in range(1, far):
        pl.semaphore_signal(barrier, inc=1, device_id=far_device(k), device_id_type=MESH)
    pairs = [
        (owner_hbm, owner_ref), (cell_hbm, cell_ref), (cache_hbm, cache_ref), (face_hbm, face_ref),
        (adj_hbm, adj_ref), (bias1_hbm, bias1_ref), (bias2_hbm, bias2_ref), (proj_hbm, proj_ref),
        (weight1_hbm, weight1_ref), (weight2_hbm, weight2_ref), (fine_hbm, fine_ref), (perm_hbm, perm_ref),
        (unperm_hbm, unperm_ref), (up_hbm, up_ref), (pick_hbm, pick_ref), (pickup_hbm, pickup_ref),
    ]
    loads = [pltpu.make_async_copy(src, dst, load_sem.at[n]) for n, (src, dst) in enumerate(pairs)]
    for load in loads:
        load.start()
    loads[0].wait()
    loads[1].wait()

    lane = lax.broadcasted_iota(jnp.int32, (1, 128), 1)
    code = jnp.full((1, 128), -1, jnp.int32)
    for b in range(NB):
        code = jnp.where(lane == b, owner_ref[b] * 512 + cell_ref[b], code)
    code_ref[0:1] = code
    here = chip * near + spot
    codes_ref[pl.ds(here, 1)] = code

    pl.semaphore_wait(barrier, near + far - 2)

    own_row = codes_ref.at[pl.ds(here, 1)]
    for k in range(1, near):
        pltpu.make_async_remote_copy(
            src_ref=code_ref.at[pl.ds(0, 1)], dst_ref=own_row, send_sem=pair_sem.at[0], recv_sem=pair_sem.at[1],
            device_id=near_device(k), device_id_type=MESH).start()

    wait_bytes(codes_ref.at[pl.ds(0, near - 1)], pair_sem.at[1])
    block = codes_ref.at[pl.ds(pl.multiple_of(chip * near, near), near)]
    for k in range(1, far):
        pltpu.make_async_remote_copy(
            src_ref=block, dst_ref=block, send_sem=block_sem.at[0], recv_sem=block_sem.at[1],
            device_id=far_device(k), device_id_type=MESH).start()
    loads[2].wait()
    wait_bytes(codes_ref.at[pl.ds(0, near * (far - 1))], block_sem.at[1])

    half = devices // 2
    index = lax.broadcasted_iota(jnp.int32, (half, 512), 1).astype(F32)

    def answers(turn, its_core, start):
        codes = codes_ref[pl.ds(its_core, half, stride=2), :]
        spots = lax.broadcasted_iota(jnp.int32, codes.shape, 1).astype(F32)
        match = (codes >> 9) == me
        cells = (codes & 511).astype(F32)
        lead = jnp.min(jnp.where(match, spots, 999.0), axis=1, keepdims=True)
        one = jnp.max(jnp.where(match & (spots == lead), cells, -1.0), axis=1, keepdims=True)
        two = jnp.max(jnp.where(match & (spots != lead), cells, -1.0), axis=1, keepdims=True)
        hot_ref[turn, pl.ds(0, half), :] = jnp.where(index == one, 1.0, 0.0).astype(BF16)
        hot_ref[turn, pl.ds(half, half), :] = jnp.where(index == two, 1.0, 0.0).astype(BF16)

        def answer(n, carry):
            cols = pl.ds(pl.multiple_of(256 * n, 256), 256)
            rows = jnp.dot(hot_ref[turn], cache_ref[:, cols], preferred_element_type=F32)
            ans_ref[turn, pl.ds(pl.multiple_of(2 * n * devices, devices), devices), :] = rows[:, :128]
            ans_ref[turn, pl.ds(pl.multiple_of((2 * n + 1) * devices, devices), devices), :] = rows[:, 128:]
            return carry

        lax.fori_loop(0, 8, answer, 0)

        def answer_to(at):
            first = ans_ref[turn, pl.ds(at, 16, stride=devices), :]
            second = ans_ref[turn, pl.ds(half + at, 16, stride=devices), :]
            return first.astype(BF16), second.astype(BF16)

        if turn == 0:
            mine = answer_to(chip * ny + gy)
            ret_ref[2 * me] = mine[0]
            ret_ref[2 * me + 1] = mine[1]

        def reply(i, carry):
            at = lax.rem(chip * ny + gy + 27 * i, half)
            dx, dy = at // ny * 2 + its_core, lax.rem(at, ny)
            to = dx * ny + dy
            pair = answer_to(at)
            stage_ref[2 * to] = pair[0]
            stage_ref[2 * to + 1] = pair[1]
            pltpu.make_async_remote_copy(
                src_ref=stage_ref.at[pl.ds(2 * to, 2)], dst_ref=ret_ref.at[pl.ds(2 * me, 2)],
                send_sem=reply_sem.at[0], recv_sem=reply_sem.at[1],
                device_id=(dx, dy), device_id_type=MESH).start()
            return carry

        lax.fori_loop(start, half, reply, 0)

    answers(0, core, 1)
    answers(1, 1 - core, 0)

    for load in loads[3:]:
        load.wait()

    def ranks(b, carry):
        count = jnp.int32(0)
        for other in range(NB):
            same = (owner_ref[other] == owner_ref[b]) & (other < b)
            count = count + jnp.where(same, 1, 0)
        rank_ref[b] = owner_ref[b] * 2 + count
        for column in range(26):
            adj_ref[b, column] = adj_ref[b, column] + 1
        return carry

    lax.fori_loop(0, NB, ranks, 0)
    build_band(weight1_ref, band1_ref)
    build_band(weight2_ref, band2_ref)
    yrow_ref[...] = jnp.zeros_like(yrow_ref)
    row_ref[...] = jnp.zeros_like(row_ref)
    for x in range(8):
        tile_ref[x, 0] = jnp.zeros((8, 384), F32)
    lane = lax.broadcasted_iota(jnp.int32, (1, 256), 1)
    for n, ref in enumerate((bias1_ref, bias2_ref)):
        line = jnp.zeros((1, 256), F32)
        for o in range(32):
            line = jnp.where(lane % 32 == o, ref[o], line)
        bias_ref[n : n + 1] = line

    wide = jnp.concatenate([proj_ref[...]] * 8, axis=0)
    chan = lax.broadcasted_iota(jnp.int32, (32, 256), 0)
    lane = lax.broadcasted_iota(jnp.int32, (32, 256), 1)
    pick = jnp.where(chan == 2 * (lane % 16) + lane // 128, 1.0, 0.0).astype(BF16)
    spread = jnp.dot(wide, pick, preferred_element_type=F32)
    row = lax.broadcasted_iota(jnp.int32, (256, 256), 0)
    lane = lax.broadcasted_iota(jnp.int32, (256, 256), 1)
    mix_ref[...] = jnp.where(row // 32 == lane % 128 // 16, spread, 0.0).astype(BF16)

    def unfold(g, carry):
        fine = fine_ref[pl.ds(pl.multiple_of(8 * g, 8), 8)].reshape(256, 512)
        rows = pl.ds(pl.multiple_of(256 * g, 256), 256)
        finep_ref[rows, :] = jnp.dot(fine, perm_ref[...], preferred_element_type=F32)
        return carry

    lax.fori_loop(0, 4, unfold, 0)

    def listed(group, n):
        return face_ref[8 * group + n] if group < 2 else face_ref[16 + n % 4]

    for group in range(3):
        for n in range(8):
            side_ref[group, n] = fine_ref[listed(group, n)]
        sidep_ref[group] = jnp.dot(
            side_ref[group].reshape(256, 512), pick_ref[group // 2], preferred_element_type=F32
        )
    wait_bytes(ret_ref.at[pl.ds(0, 2 * devices - 2)], reply_sem.at[1])

    def place(x, slot, tile):
        tile_ref[x, slot] = jnp.concatenate([tile, edge_lanes(tile[:, :128], tile[:, 128:])], axis=1)

    def copy_of(turn, src, dst, kind, other):
        return pltpu.make_async_remote_copy(
            src_ref=src, dst_ref=dst, send_sem=send_sem.at[turn, kind], recv_sem=recv_sem.at[turn, kind],
            device_id=neighbours[other], device_id_type=MESH)

    def x_copies(turn):
        return [copy_of(turn, xs_ref.at[turn, d], xr_ref.at[turn, d], d, d) for d in range(2)]

    def y_copies(turn, group):
        return [
            copy_of(turn, ys_ref.at[turn, d, group], yr_ref.at[turn, d, group], 2 + 2 * d + group, 2 + d)
            for d in range(2)
        ]

    def side_tiles(group):
        pair = jnp.concatenate([ret_ref[rank_ref[listed(group, n)]] for n in range(8)], axis=0)
        both = jnp.dot(pair, pickup_ref[group // 2], preferred_element_type=F32).astype(BF16)
        stack = jnp.concatenate([both[:, :128], both[:, 128:]], axis=0)
        mapped = jnp.dot(mix_ref[...], stack, preferred_element_type=F32)
        level = (sidep_ref[group] + mapped).astype(BF16).astype(F32)
        turned = [level[:128].T, level[128:].T]
        tiles = []
        for n in range(8 if group < 2 else 4):
            side = 64 * (group if group < 2 else n // 2)
            source = turned[n // 4]
            tall = 8 if group < 2 else 16
            tiles.append(jnp.concatenate(
                [source[side + at : side + at + tall, 32 * (n % 4) : 32 * (n % 4) + 32] for at in range(0, 64, tall)],
                axis=1,
            ))
        return tiles

    for d in range(2):
        xs_ref[0, d] = jnp.concatenate(side_tiles(d), axis=0).astype(BF16)
    for d, copy in enumerate(x_copies(0)):
        copy.start()
    lines = side_tiles(2)
    for d in range(2):
        for j in range(2):
            yrow_ref[:, pl.ds(128 * j, 128)] = lines[2 * d + j]
        for group in range(2):
            for n, x in enumerate(GROUPS[group]):
                row_ref[pl.ds(2 * n, 2), :] = yrow_ref[pl.ds(2 * x, 2), :]
            ys_ref[0, d, group] = row_ref[...].astype(BF16)
    for group in range(2):
        for copy in y_copies(0, group):
            copy.start()

    def fetch(b, carry):
        par_ref[pl.ds(pl.multiple_of(16 * b, 16), 16), :] = ret_ref[rank_ref[b]]
        return carry

    lax.fori_loop(0, NB, fetch, 0)

    def level(g, carry):
        rows = pl.ds(pl.multiple_of(256 * g, 256), 256)
        pair = par_ref[pl.ds(pl.multiple_of(128 * g, 128), 128), :]
        both = jnp.dot(pair, up_ref[...], preferred_element_type=F32).astype(BF16)
        stack = jnp.concatenate([both[:, :512], both[:, 512:]], axis=0)
        mapped = jnp.dot(mix_ref[...], stack, preferred_element_type=F32)
        rounded = (finep_ref[rows, :] + mapped).astype(BF16)
        level_ref[rows, :] = rounded
        wide = rounded.astype(F32)
        for n in range(8):
            own = wide[32 * n : 32 * n + 32, :]
            square = jnp.concatenate([own[:, 128 * k : 128 * k + 128] for k in range(4)], axis=0)
            turned = square.T
            for x in range(8):
                low, high = turned[8 * x : 8 * x + 8], turned[64 + 8 * x : 72 + 8 * x]
                place(x, 8 * g + n + 1, jnp.concatenate([low, high], axis=1))
        return carry

    lax.fori_loop(0, 4, level, 0)

    row8 = lax.broadcasted_iota(jnp.int32, (8, 128), 0)
    lane8 = lax.broadcasted_iota(jnp.int32, (8, 128), 1)
    inner = (lane8 < 64) == (row8 % 2 == 0)

    def send_x(turn):
        for d, copy in enumerate(x_copies(turn)):
            x = 7 if d == 0 else 0
            for j in range(0, 8, 2):
                two = jnp.concatenate(
                    [tile_ref[x, face_ref[8 * d + j + n] + 1, :, pl.ds(0, 256)] for n in range(2)], axis=0
                )
                xs_ref[turn, d, pl.ds(8 * j, 16), :] = two.astype(BF16)
            copy.start()

    def send_y(turn, group):
        for d, copy in enumerate(y_copies(turn, group)):
            row, side = (6, 128) if d == 0 else (0, 0)
            for j in range(2):
                at = face_ref[16 + 2 * d + j] + 1
                for n, x in enumerate(GROUPS[group]):
                    yrow_ref[pl.ds(2 * n, 2), pl.ds(128 * j, 128)] = tile_ref[x, at, pl.ds(row, 2), pl.ds(side, 128)]
            ys_ref[turn, d, group] = yrow_ref[...].astype(BF16)
            copy.start()

    def land_x(turn):
        for d, copy in enumerate(x_copies(turn)):
            copy.wait_recv()
            here = (gx > 0) if d == 0 else (gx < nx - 1)
            for j in range(8):
                if j % 2 == 0:
                    two = xr_ref[turn, d, pl.ds(8 * j, 16), :].astype(F32)
                    two = jnp.where(here, two, 0.0)
                place(7 if d == 0 else 0, 33 + 8 * d + j, two[8 * (j % 2) : 8 * (j % 2) + 8])

    def land_y(turn, group):
        for d, copy in enumerate(y_copies(turn, group)):
            copy.wait_recv()
            here = (gy > 0) if d == 0 else (gy < ny - 1)
            rows = jnp.where(here, yr_ref[turn, d, group].astype(F32), 0.0)
            for j in range(2):
                for n, x in enumerate(GROUPS[group]):
                    lines = rows[2 * n : 2 * n + 2, 128 * j : 128 * j + 128]
                    even = jnp.broadcast_to(lines[:1], (8, 128))
                    half = jnp.where(row8 % 2 == 0, even, jnp.broadcast_to(lines[1:], (8, 128)))
                    place(x, 49 + 2 * d + j, jnp.concatenate([half, half], axis=1))

    def padded_tile(near_by, px):
        dx = -1 if px == 0 else (1 if px == 9 else 0)
        x = 7 if px == 0 else (0 if px == 9 else px - 1)

        def at(dy, dz):
            return near_by[dx, dy, dz]

        def ends(dy):
            one, two, own = (tile_ref[x, at(dy, dz), :, pl.ds(256, 128)] for dz in (1, -1, 0))
            return jnp.where(inner, own, jnp.where(lane8 < 64, one, two))

        mid = tile_ref[x, at(0, 0), :, pl.ds(0, 256)]
        below = tile_ref[x, at(-1, 0), :, pl.ds(128, 128)]
        above = tile_ref[x, at(1, 0), :, pl.ds(0, 128)]
        low = pltpu.roll(jnp.where(row8 >= 6, below, mid[:, 128:]), 2, 0)
        high = pltpu.roll(jnp.where(row8 < 2, above, mid[:, :128]), 6, 0)
        here = ends(0)
        clow = pltpu.roll(jnp.where(row8 >= 6, ends(-1), here), 2, 0)
        chigh = pltpu.roll(jnp.where(row8 < 2, ends(1), here), 6, 0)
        corners = jnp.where(lane8 // 32 % 2 == 1, clow, chigh)
        return jnp.concatenate([mid, low, high, here, corners], axis=1)

    def pad_planes(planes):
        steps = sorted({-1 if px == 0 else (1 if px == 9 else 0) for px in planes})

        def slots(b):
            return {
                (dx, dy, dz): b + 1 if dx == dy == dz == 0 else adj_ref[b, column_of(dx, dy, dz)]
                for dx in steps for dy in (-1, 0, 1) for dz in (-1, 0, 1)
            }

        def per_pair(n, carry):
            even, odd = slots(2 * n), slots(2 * n + 1)
            for px in planes:
                two = jnp.concatenate([padded_tile(even, px), padded_tile(odd, px)], axis=0)
                pad_ref[px, pl.ds(pl.multiple_of(16 * n, 16), 16), :] = two.astype(BF16)
            return carry

        lax.fori_loop(0, NB // 2, per_pair, 0)

    def land_and_pad(turn):
        land_x(turn)
        land_y(turn, 0)
        pad_planes([0, 9] + [x + 1 for x in GROUPS[0]])
        land_y(turn, 1)
        pad_planes([x + 1 for x in GROUPS[1]])

    def conv(first_plane, planes, band_ref, bias):
        total = bias_ref[pl.ds(bias, 1)]
        for i in range(3):
            rows = pad_ref[pl.ds(first_plane + i, planes)].reshape(256 * planes, 768)
            total = total + jnp.dot(rows, band_ref[i], preferred_element_type=F32)
        return total

    land_x(0)
    land_y(0, 0)
    land_y(0, 1)
    pad_planes(range(10))

    def first(pair):
        v = conv(2 * pair, 2, band1_ref, 0)
        half = 0.5 * v
        h = (half + half * jnp.tanh(half)).astype(BF16).astype(F32)
        tile_ref[pl.ds(2 * pair, 2), pl.ds(1, NB), :, pl.ds(0, 256)] = h.reshape(2, NB, 8, 256)
        e = edge_lanes(h[:, :128].reshape(2 * NB, 8, 128), h[:, 128:].reshape(2 * NB, 8, 128))
        tile_ref[pl.ds(2 * pair, 2), pl.ds(1, NB), :, pl.ds(256, 128)] = e.reshape(2, NB, 8, 128)

    def outer(n, carry):
        first(3 * n)
        return carry

    lax.fori_loop(0, 2, outer, 0)
    send_x(1)
    first(1)
    send_y(1, 0)
    first(2)
    send_y(1, 1)
    land_and_pad(1)

    def second(pair, carry):
        sum_ref[pl.ds(4 * pair, 4)] = conv(4 * pair, 4, band2_ref, 1).reshape(4, NB, 8, 256)
        return carry

    lax.fori_loop(0, 2, second, 0)

    def finish(g, carry):
        rows = pl.ds(pl.multiple_of(512 * g, 512), 512)
        parts = []
        for n in range(16):
            tall = [sum_ref[x, 16 * g + n] for x in range(8)]
            turned = jnp.concatenate([t[:, :128] for t in tall] + [t[:, 128:] for t in tall], axis=0).T
            parts.append(jnp.concatenate([turned[32 * k : 32 * k + 32] for k in range(4)], axis=1))
        total = jnp.concatenate(parts, axis=0) + level_ref[rows, :].astype(F32)
        rows = jnp.dot(total.astype(BF16), unperm_ref[...], preferred_element_type=F32).astype(BF16)
        bricks = pl.ds(pl.multiple_of(16 * g, 16), 16)
        fine_ref[bricks] = rows.reshape(16, 32, 512)
        pltpu.make_async_copy(fine_ref.at[bricks], out_hbm.at[bricks], out_sem).start()
        return carry

    lax.fori_loop(0, 2, finish, 0)
    for turn in range(2):
        for copy in x_copies(turn) + y_copies(turn, 0) + y_copies(turn, 1):
            copy.wait_send()
    wait_bytes(codes_ref.at[pl.ds(0, near - 1)], pair_sem.at[0])
    wait_bytes(codes_ref.at[pl.ds(0, near * (far - 1))], block_sem.at[0])
    wait_bytes(ret_ref.at[pl.ds(0, 2 * devices - 2)], reply_sem.at[0])
    pltpu.make_async_copy(fine_ref, out_hbm, out_sem).wait()


def hand_on(values_hbm, out_hbm, held, sem):
    parts = [pl.ds(4 * n, 4) for n in range(8)]
    into = [pltpu.make_async_copy(values_hbm.at[p], held.at[p], sem.at[0, n]) for n, p in enumerate(parts)]
    onward = [pltpu.make_async_copy(held.at[p], out_hbm.at[p], sem.at[1, n]) for n, p in enumerate(parts)]
    for copy in into:
        copy.start()
    for before, after in zip(into, onward):
        before.wait()
        after.start()
    for copy in onward:
        copy.wait()


def per_device(
    fine_features, coarse_cache, parent_owner, parent_cell, face_list, adjacency,
    parent_proj, conv_first, bias_first, conv_second, bias_second,
):
    devices = lax.axis_size("gx") * lax.axis_size("gy")
    perm, up = lane_tables()
    pick, pickup = face_tables()
    hbm = pl.BlockSpec(memory_space=pl.ANY)
    out = pl.pallas_call(
        kernel,
        out_shape=jax.ShapeDtypeStruct((NB, 32, 512), BF16),
        in_specs=[hbm] * 16,
        out_specs=hbm,
        scratch_shapes=[
            pltpu.SMEM((NB,), jnp.int32),
            pltpu.SMEM((NB,), jnp.int32),
            pltpu.SMEM((20,), jnp.int32),
            pltpu.SMEM((NB, 26), jnp.int32),
            pltpu.SMEM((32,), F32),
            pltpu.SMEM((32,), F32),
            pltpu.VMEM((32, 32), BF16),
            pltpu.VMEM((27, 32, 32), BF16),
            pltpu.VMEM((27, 32, 32), BF16),
            pltpu.VMEM((NB, 32, 512), BF16),
            pltpu.VMEM((512, 2048), BF16),
            pltpu.VMEM((512, 512), BF16),
            pltpu.VMEM((512, 512), BF16),
            pltpu.VMEM((128, 1024), BF16),
            pltpu.VMEM((2, 512, 128), BF16),
            pltpu.VMEM((2, 128, 256), BF16),
            pltpu.VMEM((8, 128), jnp.int32),
            pltpu.VMEM((devices, 128), jnp.int32),
            pltpu.VMEM((2, devices, 512), BF16),
            pltpu.VMEM((2, 16 * devices, 128), F32),
            pltpu.VMEM((2 * devices, 16, 128), BF16),
            pltpu.VMEM((2 * devices, 16, 128), BF16),
            pltpu.SMEM((NB,), jnp.int32),
            pltpu.VMEM((NB * 32, 512), F32),
            pltpu.VMEM((3, 8, 32, 512), BF16),
            pltpu.VMEM((3, 256, 128), F32),
            pltpu.VMEM((8, SLOTS, 8, 384), F32),
            pltpu.VMEM((10, 256, 768), BF16),
            pltpu.VMEM((3, 768, 256), BF16),
            pltpu.VMEM((3, 768, 256), BF16),
            pltpu.VMEM((NB * 32, 512), BF16),
            pltpu.VMEM((NB * 16, 128), BF16),
            pltpu.VMEM((8, NB, 8, 256), F32),
            pltpu.VMEM((256, 256), BF16),
            pltpu.VMEM((8, 256), F32),
            pltpu.VMEM((2, 2, 64, 256), BF16),
            pltpu.VMEM((2, 2, 2, 16, 256), BF16),
            pltpu.VMEM((16, 256), F32),
            pltpu.VMEM((16, 256), F32),
            pltpu.VMEM((2, 2, 64, 256), BF16),
            pltpu.VMEM((2, 2, 2, 16, 256), BF16),
            pltpu.SemaphoreType.DMA((2, 6)),
            pltpu.SemaphoreType.DMA((2, 6)),
            pltpu.SemaphoreType.DMA((16,)),
            pltpu.SemaphoreType.DMA,
            pltpu.SemaphoreType.DMA((2,)),
            pltpu.SemaphoreType.DMA((2,)),
            pltpu.SemaphoreType.DMA((2,)),
        ],
        compiler_params=pltpu.CompilerParams(
            collective_id=0, has_side_effects=True, vmem_limit_bytes=56 * 1024 * 1024
        ),
    )(
        parent_owner.reshape(NB), parent_cell, face_list, adjacency, bias_first, bias_second, parent_proj, conv_first,
        conv_second, fine_features, coarse_cache, jnp.asarray(perm, BF16),
        jnp.asarray(perm.T, BF16), jnp.asarray(up, BF16),
        jnp.asarray(pick, BF16), jnp.asarray(pickup, BF16),
    )
    return pl.pallas_call(
        hand_on,
        out_shape=jax.ShapeDtypeStruct((NB, 32, 512), BF16),
        in_specs=[hbm],
        out_specs=hbm,
        scratch_shapes=[pltpu.VMEM((NB, 32, 512), BF16), pltpu.SemaphoreType.DMA((2, 8))],
    )(out)


def solution(mesh):
    placed = (
        P(("gx", "gy"), None, None),
        P(("gx", "gy"), None),
        P(("gx", "gy"), None),
        P(("gx", "gy")),
        P(("gx", "gy")),
        P(("gx", "gy"), None),
        P(),
        P(),
        P(),
        P(),
        P(),
    )
    return jax.shard_map(
        per_device,
        mesh=mesh,
        in_specs=placed,
        out_specs=P(("gx", "gy"), None, None),
        check_vma=False,
    )
```

```python
import jax
import jax.numpy as jnp
import numpy as np
from jax import lax
from jax.experimental import pallas as pl
from jax.experimental.pallas import tpu as pltpu
from jax.sharding import PartitionSpec as P

F32 = jnp.float32
BF16 = jnp.bfloat16
NB = 32
SLOTS = 53
MESH = pl.DeviceIdType.MESH
GROUPS = [[0, 1, 6, 7, 2, 3], [4, 5]]


def column_of(dx, dy, dz):
    at = 9 * (dx + 1) + 3 * (dy + 1) + dz + 1
    return at if at < 13 else at - 1


def lane_tables():
    lane = np.arange(512)
    x, row = lane % 64 // 8, lane % 8
    y, z = 2 * (row // 2) + lane // 64 % 2, 4 * (row % 2) + lane // 128
    voxel = 64 * x + 8 * y + z
    cell = 16 * (x // 2) + 4 * (y // 2) + z // 2
    perm = (np.arange(512)[:, None] == voxel[None, :]).astype(np.float32)
    up = (np.arange(64)[:, None] == cell[None, :]).astype(np.float32)
    blank = np.zeros_like(up)
    even = np.concatenate([up, blank], 0)
    odd = np.concatenate([blank, up], 0)
    return perm, np.concatenate([even, odd], 1)


def face_tables():
    lane = np.arange(128)
    fixed, at = np.where(lane < 64, 7, 0), lane % 64
    part, row = at // 8, at % 8
    across_x = (fixed, 2 * (row // 2) + part // 4, 4 * (row % 2) + part % 4)
    across_y = (at % 16 // 2, fixed, 4 * (at % 2) + at // 16)
    picks, ups = [], []
    for x, y, z in (across_x, across_y):
        voxel = 64 * x + 8 * y + z
        cell = 16 * (x // 2) + 4 * (y // 2) + z // 2
        picks.append((np.arange(512)[:, None] == voxel[None, :]).astype(np.float32))
        up = (np.arange(64)[:, None] == cell[None, :]).astype(np.float32)
        blank = np.zeros_like(up)
        ups.append(np.concatenate([np.concatenate([up, blank], 0), np.concatenate([blank, up], 0)], 1))
    return np.stack(picks), np.stack(ups)


def build_band(weight_ref, band_ref):
    block = lax.broadcasted_iota(jnp.int32, (32, 128), 1) // 32
    zero = jnp.zeros((32, 128), F32)

    def per_x(i, carry):
        moved = {}
        for j in range(3):
            taps = [weight_ref[9 * i + 3 * j + k].astype(F32) for k in (2, 1, 0)]
            strip = jnp.concatenate(taps + [jnp.zeros((32, 32), F32)], axis=0).T
            for z in range(-1, 5):
                rolled = strip if z == 1 else pltpu.roll(strip, (32 * (z - 1)) % 128, 1)
                fits = (block >= z - 1) & (block <= z + 1)
                moved[j, z] = jnp.where(fits, rolled, 0.0)
        order = [(y, z) for y in (0, 1, -1, 2) for z in range(4)]
        order += [(0, 4), (1, 4), (0, -1), (1, -1), (2, 4), (-1, 4), (2, -1), (-1, -1)]
        for n, (y, z) in enumerate(order):
            halves = [moved[y + 1, z] if y < 2 else zero, moved[y, z] if y > -1 else zero]
            band_ref[i, pl.ds(32 * n, 32), :] = jnp.concatenate(halves, axis=1).astype(BF16)
        return carry

    lax.fori_loop(0, 3, per_x, 0)


def edge_lanes(low, high):
    axes = low.ndim
    lane = lax.broadcasted_iota(jnp.int32, low.shape, axes - 1)
    row = lax.broadcasted_iota(jnp.int32, low.shape, axes - 2)
    a = jnp.where(lane < 32, low, pltpu.roll(high, 32, axes - 1))
    b = jnp.where(lane < 96, pltpu.roll(low, 96, axes - 1), high)
    ends = jnp.where(lane < 64, a, b)
    return jnp.where(row % 2 == 0, pltpu.roll(ends, 7, axes - 2), pltpu.roll(ends, 1, axes - 2))


def wait_bytes(ref, sem):
    pltpu.make_async_copy(ref, ref, sem).wait()


def kernel(
    owner_hbm, cell_hbm, face_hbm, adj_hbm, bias1_hbm, bias2_hbm, proj_hbm, weight1_hbm, weight2_hbm,
    fine_hbm, cache_hbm, perm_hbm, unperm_hbm, up_hbm, pick_hbm, pickup_hbm, out_hbm,
    owner_ref, cell_ref, face_ref, adj_ref, bias1_ref, bias2_ref, proj_ref, weight1_ref, weight2_ref,
    fine_ref, cache_ref, perm_ref, unperm_ref, up_ref, pick_ref, pickup_ref, code_ref, codes_ref, hot_ref, ans_ref, stage_ref, ret_ref, rank_ref,
    finep_ref, side_ref, sidep_ref, tile_ref, pad_ref, band1_ref, band2_ref, level_ref, par_ref,
    sum_ref, mix_ref, bias_ref, xs_ref, ys_ref, yrow_ref, row_ref, xr_ref, yr_ref,
    send_sem, recv_sem, load_sem, out_sem, pair_sem, block_sem, reply_sem,
):
    gx, gy = lax.axis_index("gx"), lax.axis_index("gy")
    nx, ny = lax.axis_size("gx"), lax.axis_size("gy")
    devices = nx * ny
    up_x, down_x = lax.rem(gx + 1, nx), lax.rem(gx + nx - 1, nx)
    up_y, down_y = lax.rem(gy + 1, ny), lax.rem(gy + ny - 1, ny)
    neighbours = [(up_x, gy), (down_x, gy), (gx, up_y), (gx, down_y)]
    me = gx * ny + gy
    chip, core = gx // 2, lax.rem(gx, 2)
    near = 2 * ny
    far = nx // 2
    spot = gy * 2 + core

    def near_device(k):
        at = lax.rem(spot + k, near)
        return (chip * 2 + lax.rem(at, 2), at // 2)

    def far_device(k):
        return (lax.rem(chip + k, far) * 2 + core, gy)

    barrier = pltpu.get_barrier_semaphore()
    for k in range(1, near):
        pl.semaphore_signal(barrier, inc=1, device_id=near_device(k), device_id_type=MESH)
    for k in range(1, far):
        pl.semaphore_signal(barrier, inc=1, device_id=far_device(k), device_id_type=MESH)
    pairs = [
        (owner_hbm, owner_ref), (cell_hbm, cell_ref), (cache_hbm, cache_ref), (face_hbm, face_ref),
        (adj_hbm, adj_ref), (bias1_hbm, bias1_ref), (bias2_hbm, bias2_ref), (proj_hbm, proj_ref),
        (weight1_hbm, weight1_ref), (weight2_hbm, weight2_ref), (fine_hbm, fine_ref), (perm_hbm, perm_ref),
        (unperm_hbm, unperm_ref), (up_hbm, up_ref), (pick_hbm, pick_ref), (pickup_hbm, pickup_ref),
    ]
    loads = [pltpu.make_async_copy(src, dst, load_sem.at[n]) for n, (src, dst) in enumerate(pairs)]
    for load in loads:
        load.start()
    loads[0].wait()
    loads[1].wait()

    lane = lax.broadcasted_iota(jnp.int32, (1, 128), 1)
    code = jnp.full((1, 128), -1, jnp.int32)
    for b in range(NB):
        code = jnp.where(lane == b, owner_ref[b] * 512 + cell_ref[b], code)
    code_ref[0:1] = code
    here = chip * near + spot
    codes_ref[pl.ds(here, 1)] = code

    pl.semaphore_wait(barrier, near + far - 2)

    own_row = codes_ref.at[pl.ds(here, 1)]
    for k in range(1, near):
        pltpu.make_async_remote_copy(
            src_ref=code_ref.at[pl.ds(0, 1)], dst_ref=own_row, send_sem=pair_sem.at[0], recv_sem=pair_sem.at[1],
            device_id=near_device(k), device_id_type=MESH).start()

    wait_bytes(codes_ref.at[pl.ds(0, near - 1)], pair_sem.at[1])
    block = codes_ref.at[pl.ds(pl.multiple_of(chip * near, near), near)]
    for k in range(1, far):
        pltpu.make_async_remote_copy(
            src_ref=block, dst_ref=block, send_sem=block_sem.at[0], recv_sem=block_sem.at[1],
            device_id=far_device(k), device_id_type=MESH).start()
    loads[2].wait()
    wait_bytes(codes_ref.at[pl.ds(0, near * (far - 1))], block_sem.at[1])

    half = devices // 2
    index = lax.broadcasted_iota(jnp.int32, (half, 512), 1).astype(F32)

    def answers(turn, its_core, start):
        codes = codes_ref[pl.ds(its_core, half, stride=2), :]
        spots = lax.broadcasted_iota(jnp.int32, codes.shape, 1).astype(F32)
        match = (codes >> 9) == me
        cells = (codes & 511).astype(F32)
        lead = jnp.min(jnp.where(match, spots, 999.0), axis=1, keepdims=True)
        one = jnp.max(jnp.where(match & (spots == lead), cells, -1.0), axis=1, keepdims=True)
        two = jnp.max(jnp.where(match & (spots != lead), cells, -1.0), axis=1, keepdims=True)
        hot_ref[turn, pl.ds(0, half), :] = jnp.where(index == one, 1.0, 0.0).astype(BF16)
        hot_ref[turn, pl.ds(half, half), :] = jnp.where(index == two, 1.0, 0.0).astype(BF16)

        def answer(n, carry):
            cols = pl.ds(pl.multiple_of(256 * n, 256), 256)
            rows = jnp.dot(hot_ref[turn], cache_ref[:, cols], preferred_element_type=F32)
            ans_ref[turn, pl.ds(pl.multiple_of(2 * n * devices, devices), devices), :] = rows[:, :128]
            ans_ref[turn, pl.ds(pl.multiple_of((2 * n + 1) * devices, devices), devices), :] = rows[:, 128:]
            return carry

        lax.fori_loop(0, 8, answer, 0, unroll=True)

        def answer_to(at):
            first = ans_ref[turn, pl.ds(at, 16, stride=devices), :]
            second = ans_ref[turn, pl.ds(half + at, 16, stride=devices), :]
            return first.astype(BF16), second.astype(BF16)

        if turn == 0:
            mine = answer_to(chip * ny + gy)
            ret_ref[2 * me] = mine[0]
            ret_ref[2 * me + 1] = mine[1]

        def reply(i, carry):
            at = lax.rem(chip * ny + gy + 27 * i, half)
            dx, dy = at // ny * 2 + its_core, lax.rem(at, ny)
            to = dx * ny + dy
            pair = answer_to(at)
            stage_ref[2 * to] = pair[0]
            stage_ref[2 * to + 1] = pair[1]
            pltpu.make_async_remote_copy(
                src_ref=stage_ref.at[pl.ds(2 * to, 2)], dst_ref=ret_ref.at[pl.ds(2 * me, 2)],
                send_sem=reply_sem.at[0], recv_sem=reply_sem.at[1],
                device_id=(dx, dy), device_id_type=MESH).start()
            return carry

        lax.fori_loop(start, half, reply, 0)

    answers(0, core, 1)
    answers(1, 1 - core, 0)

    for load in loads[3:]:
        load.wait()

    def ranks(b, carry):
        count = jnp.int32(0)
        for other in range(NB):
            same = (owner_ref[other] == owner_ref[b]) & (other < b)
            count = count + jnp.where(same, 1, 0)
        rank_ref[b] = owner_ref[b] * 2 + count
        for column in range(26):
            adj_ref[b, column] = adj_ref[b, column] + 1
        return carry

    lax.fori_loop(0, NB, ranks, 0)
    build_band(weight1_ref, band1_ref)
    build_band(weight2_ref, band2_ref)
    yrow_ref[...] = jnp.zeros_like(yrow_ref)
    row_ref[...] = jnp.zeros_like(row_ref)
    for x in range(8):
        tile_ref[x, 0] = jnp.zeros((8, 384), F32)
    lane = lax.broadcasted_iota(jnp.int32, (1, 256), 1)
    for n, ref in enumerate((bias1_ref, bias2_ref)):
        line = jnp.zeros((1, 256), F32)
        for o in range(32):
            line = jnp.where(lane % 32 == o, ref[o], line)
        bias_ref[n : n + 1] = line

    wide = jnp.concatenate([proj_ref[...]] * 8, axis=0)
    chan = lax.broadcasted_iota(jnp.int32, (32, 256), 0)
    lane = lax.broadcasted_iota(jnp.int32, (32, 256), 1)
    pick = jnp.where(chan == 2 * (lane % 16) + lane // 128, 1.0, 0.0).astype(BF16)
    spread = jnp.dot(wide, pick, preferred_element_type=F32)
    row = lax.broadcasted_iota(jnp.int32, (256, 256), 0)
    lane = lax.broadcasted_iota(jnp.int32, (256, 256), 1)
    mix_ref[...] = jnp.where(row // 32 == lane % 128 // 16, spread, 0.0).astype(BF16)

    def unfold(g, carry):
        fine = fine_ref[pl.ds(pl.multiple_of(8 * g, 8), 8)].reshape(256, 512)
        rows = pl.ds(pl.multiple_of(256 * g, 256), 256)
        finep_ref[rows, :] = jnp.dot(fine, perm_ref[...], preferred_element_type=F32)
        return carry

    lax.fori_loop(0, 4, unfold, 0)

    def listed(group, n):
        return face_ref[8 * group + n] if group < 2 else face_ref[16 + n % 4]

    for group in range(3):
        for n in range(8):
            side_ref[group, n] = fine_ref[listed(group, n)]
        sidep_ref[group] = jnp.dot(
            side_ref[group].reshape(256, 512), pick_ref[group // 2], preferred_element_type=F32
        )
    wait_bytes(ret_ref.at[pl.ds(0, 2 * devices - 2)], reply_sem.at[1])

    def place(x, slot, tile):
        tile_ref[x, slot] = jnp.concatenate([tile, edge_lanes(tile[:, :128], tile[:, 128:])], axis=1)

    def copy_of(turn, src, dst, kind, other):
        return pltpu.make_async_remote_copy(
            src_ref=src, dst_ref=dst, send_sem=send_sem.at[turn, kind], recv_sem=recv_sem.at[turn, kind],
            device_id=neighbours[other], device_id_type=MESH)

    def x_copies(turn):
        return [copy_of(turn, xs_ref.at[turn, d], xr_ref.at[turn, d], d, d) for d in range(2)]

    def y_copies(turn, group):
        return [
            copy_of(turn, ys_ref.at[turn, d, group], yr_ref.at[turn, d, group], 2 + 2 * d + group, 2 + d)
            for d in range(2)
        ]

    def side_tiles(group):
        pair = jnp.concatenate([ret_ref[rank_ref[listed(group, n)]] for n in range(8)], axis=0)
        both = jnp.dot(pair, pickup_ref[group // 2], preferred_element_type=F32).astype(BF16)
        stack = jnp.concatenate([both[:, :128], both[:, 128:]], axis=0)
        mapped = jnp.dot(mix_ref[...], stack, preferred_element_type=F32)
        level = (sidep_ref[group] + mapped).astype(BF16).astype(F32)
        turned = [level[:128].T, level[128:].T]
        tiles = []
        for n in range(8 if group < 2 else 4):
            side = 64 * (group if group < 2 else n // 2)
            source = turned[n // 4]
            tall = 8 if group < 2 else 16
            tiles.append(jnp.concatenate(
                [source[side + at : side + at + tall, 32 * (n % 4) : 32 * (n % 4) + 32] for at in range(0, 64, tall)],
                axis=1,
            ))
        return tiles

    for d in range(2):
        xs_ref[0, d] = jnp.concatenate(side_tiles(d), axis=0).astype(BF16)
    for d, copy in enumerate(x_copies(0)):
        copy.start()
    lines = side_tiles(2)
    for d in range(2):
        for j in range(2):
            yrow_ref[:, pl.ds(128 * j, 128)] = lines[2 * d + j]
        for group in range(2):
            for n, x in enumerate(GROUPS[group]):
                row_ref[pl.ds(2 * n, 2), :] = yrow_ref[pl.ds(2 * x, 2), :]
            ys_ref[0, d, group] = row_ref[...].astype(BF16)
    for group in range(2):
        for copy in y_copies(0, group):
            copy.start()

    def fetch(b, carry):
        par_ref[pl.ds(pl.multiple_of(16 * b, 16), 16), :] = ret_ref[rank_ref[b]]
        return carry

    lax.fori_loop(0, NB, fetch, 0)

    def level(g, carry):
        rows = pl.ds(pl.multiple_of(256 * g, 256), 256)
        pair = par_ref[pl.ds(pl.multiple_of(128 * g, 128), 128), :]
        both = jnp.dot(pair, up_ref[...], preferred_element_type=F32).astype(BF16)
        stack = jnp.concatenate([both[:, :512], both[:, 512:]], axis=0)
        mapped = jnp.dot(mix_ref[...], stack, preferred_element_type=F32)
        rounded = (finep_ref[rows, :] + mapped).astype(BF16)
        level_ref[rows, :] = rounded
        wide = rounded.astype(F32)
        for n in range(8):
            own = wide[32 * n : 32 * n + 32, :]
            square = jnp.concatenate([own[:, 128 * k : 128 * k + 128] for k in range(4)], axis=0)
            turned = square.T
            for x in range(8):
                low, high = turned[8 * x : 8 * x + 8], turned[64 + 8 * x : 72 + 8 * x]
                place(x, 8 * g + n + 1, jnp.concatenate([low, high], axis=1))
        return carry

    lax.fori_loop(0, 4, level, 0)

    row8 = lax.broadcasted_iota(jnp.int32, (8, 128), 0)
    lane8 = lax.broadcasted_iota(jnp.int32, (8, 128), 1)
    inner = (lane8 < 64) == (row8 % 2 == 0)

    def send_x(turn):
        for d, copy in enumerate(x_copies(turn)):
            x = 7 if d == 0 else 0
            for j in range(0, 8, 2):
                two = jnp.concatenate(
                    [tile_ref[x, face_ref[8 * d + j + n] + 1, :, pl.ds(0, 256)] for n in range(2)], axis=0
                )
                xs_ref[turn, d, pl.ds(8 * j, 16), :] = two.astype(BF16)
            copy.start()

    def send_y(turn, group):
        for d, copy in enumerate(y_copies(turn, group)):
            row, side = (6, 128) if d == 0 else (0, 0)
            for j in range(2):
                at = face_ref[16 + 2 * d + j] + 1
                for n, x in enumerate(GROUPS[group]):
                    yrow_ref[pl.ds(2 * n, 2), pl.ds(128 * j, 128)] = tile_ref[x, at, pl.ds(row, 2), pl.ds(side, 128)]
            ys_ref[turn, d, group] = yrow_ref[...].astype(BF16)
            copy.start()

    def land_x(turn):
        for d, copy in enumerate(x_copies(turn)):
            copy.wait_recv()
            here = (gx > 0) if d == 0 else (gx < nx - 1)
            for j in range(8):
                if j % 2 == 0:
                    two = xr_ref[turn, d, pl.ds(8 * j, 16), :].astype(F32)
                    two = jnp.where(here, two, 0.0)
                place(7 if d == 0 else 0, 33 + 8 * d + j, two[8 * (j % 2) : 8 * (j % 2) + 8])

    def land_y(turn, group):
        for d, copy in enumerate(y_copies(turn, group)):
            copy.wait_recv()
            here = (gy > 0) if d == 0 else (gy < ny - 1)
            rows = jnp.where(here, yr_ref[turn, d, group].astype(F32), 0.0)
            for j in range(2):
                for n, x in enumerate(GROUPS[group]):
                    lines = rows[2 * n : 2 * n + 2, 128 * j : 128 * j + 128]
                    even = jnp.broadcast_to(lines[:1], (8, 128))
                    half = jnp.where(row8 % 2 == 0, even, jnp.broadcast_to(lines[1:], (8, 128)))
                    place(x, 49 + 2 * d + j, jnp.concatenate([half, half], axis=1))

    def padded_tile(near_by, px):
        dx = -1 if px == 0 else (1 if px == 9 else 0)
        x = 7 if px == 0 else (0 if px == 9 else px - 1)

        def at(dy, dz):
            return near_by[dx, dy, dz]

        def ends(dy):
            one, two, own = (tile_ref[x, at(dy, dz), :, pl.ds(256, 128)] for dz in (1, -1, 0))
            return jnp.where(inner, own, jnp.where(lane8 < 64, one, two))

        mid = tile_ref[x, at(0, 0), :, pl.ds(0, 256)]
        below = tile_ref[x, at(-1, 0), :, pl.ds(128, 128)]
        above = tile_ref[x, at(1, 0), :, pl.ds(0, 128)]
        low = pltpu.roll(jnp.where(row8 >= 6, below, mid[:, 128:]), 2, 0)
        high = pltpu.roll(jnp.where(row8 < 2, above, mid[:, :128]), 6, 0)
        here = ends(0)
        clow = pltpu.roll(jnp.where(row8 >= 6, ends(-1), here), 2, 0)
        chigh = pltpu.roll(jnp.where(row8 < 2, ends(1), here), 6, 0)
        corners = jnp.where(lane8 // 32 % 2 == 1, clow, chigh)
        return jnp.concatenate([mid, low, high, here, corners], axis=1)

    def pad_planes(planes):
        steps = sorted({-1 if px == 0 else (1 if px == 9 else 0) for px in planes})

        def slots(b):
            return {
                (dx, dy, dz): b + 1 if dx == dy == dz == 0 else adj_ref[b, column_of(dx, dy, dz)]
                for dx in steps for dy in (-1, 0, 1) for dz in (-1, 0, 1)
            }

        def per_pair(n, carry):
            even, odd = slots(2 * n), slots(2 * n + 1)
            for px in planes:
                two = jnp.concatenate([padded_tile(even, px), padded_tile(odd, px)], axis=0)
                pad_ref[px, pl.ds(pl.multiple_of(16 * n, 16), 16), :] = two.astype(BF16)
            return carry

        lax.fori_loop(0, NB // 2, per_pair, 0, unroll=2)

    def land_and_pad(turn):
        land_x(turn)
        land_y(turn, 0)
        pad_planes([0, 9] + [x + 1 for x in GROUPS[0]])
        land_y(turn, 1)
        pad_planes([x + 1 for x in GROUPS[1]])

    def conv(first_plane, planes, band_ref, bias):
        total = bias_ref[pl.ds(bias, 1)]
        for i in range(3):
            rows = pad_ref[pl.ds(first_plane + i, planes)].reshape(256 * planes, 768)
            total = total + jnp.dot(rows, band_ref[i], preferred_element_type=F32)
        return total

    land_x(0)
    land_y(0, 0)
    land_y(0, 1)
    pad_planes(range(10))

    def first(pair):
        v = conv(2 * pair, 2, band1_ref, 0)
        half = 0.5 * v
        h = (half + half * jnp.tanh(half)).astype(BF16).astype(F32)
        tile_ref[pl.ds(2 * pair, 2), pl.ds(1, NB), :, pl.ds(0, 256)] = h.reshape(2, NB, 8, 256)
        e = edge_lanes(h[:, :128].reshape(2 * NB, 8, 128), h[:, 128:].reshape(2 * NB, 8, 128))
        tile_ref[pl.ds(2 * pair, 2), pl.ds(1, NB), :, pl.ds(256, 128)] = e.reshape(2, NB, 8, 128)

    def outer(n, carry):
        first(3 * n)
        return carry

    lax.fori_loop(0, 2, outer, 0)
    send_x(1)
    first(1)
    send_y(1, 0)
    first(2)
    send_y(1, 1)
    land_and_pad(1)

    def second(pair, carry):
        sum_ref[pl.ds(4 * pair, 4)] = conv(4 * pair, 4, band2_ref, 1).reshape(4, NB, 8, 256)
        return carry

    lax.fori_loop(0, 2, second, 0)

    def finish(g, carry):
        rows = pl.ds(pl.multiple_of(512 * g, 512), 512)
        parts = []
        for n in range(16):
            tall = [sum_ref[x, 16 * g + n] for x in range(8)]
            turned = jnp.concatenate([t[:, :128] for t in tall] + [t[:, 128:] for t in tall], axis=0).T
            parts.append(jnp.concatenate([turned[32 * k : 32 * k + 32] for k in range(4)], axis=1))
        total = jnp.concatenate(parts, axis=0) + level_ref[rows, :].astype(F32)
        rows = jnp.dot(total.astype(BF16), unperm_ref[...], preferred_element_type=F32).astype(BF16)
        bricks = pl.ds(pl.multiple_of(16 * g, 16), 16)
        fine_ref[bricks] = rows.reshape(16, 32, 512)
        pltpu.make_async_copy(fine_ref.at[bricks], out_hbm.at[bricks], out_sem).start()
        return carry

    lax.fori_loop(0, 2, finish, 0)
    for turn in range(2):
        for copy in x_copies(turn) + y_copies(turn, 0) + y_copies(turn, 1):
            copy.wait_send()
    wait_bytes(codes_ref.at[pl.ds(0, near - 1)], pair_sem.at[0])
    wait_bytes(codes_ref.at[pl.ds(0, near * (far - 1))], block_sem.at[0])
    wait_bytes(ret_ref.at[pl.ds(0, 2 * devices - 2)], reply_sem.at[0])
    pltpu.make_async_copy(fine_ref, out_hbm, out_sem).wait()


def hand_on(values_hbm, out_hbm, held, sem):
    parts = [pl.ds(4 * n, 4) for n in range(8)]
    into = [pltpu.make_async_copy(values_hbm.at[p], held.at[p], sem.at[0, n]) for n, p in enumerate(parts)]
    onward = [pltpu.make_async_copy(held.at[p], out_hbm.at[p], sem.at[1, n]) for n, p in enumerate(parts)]
    for copy in into:
        copy.start()
    for before, after in zip(into, onward):
        before.wait()
        after.start()
    for copy in onward:
        copy.wait()


def per_device(
    fine_features, coarse_cache, parent_owner, parent_cell, face_list, adjacency,
    parent_proj, conv_first, bias_first, conv_second, bias_second,
):
    devices = lax.axis_size("gx") * lax.axis_size("gy")
    perm, up = lane_tables()
    pick, pickup = face_tables()
    hbm = pl.BlockSpec(memory_space=pl.ANY)
    out = pl.pallas_call(
        kernel,
        out_shape=jax.ShapeDtypeStruct((NB, 32, 512), BF16),
        in_specs=[hbm] * 16,
        out_specs=hbm,
        scratch_shapes=[
            pltpu.SMEM((NB,), jnp.int32),
            pltpu.SMEM((NB,), jnp.int32),
            pltpu.SMEM((20,), jnp.int32),
            pltpu.SMEM((NB, 26), jnp.int32),
            pltpu.SMEM((32,), F32),
            pltpu.SMEM((32,), F32),
            pltpu.VMEM((32, 32), BF16),
            pltpu.VMEM((27, 32, 32), BF16),
            pltpu.VMEM((27, 32, 32), BF16),
            pltpu.VMEM((NB, 32, 512), BF16),
            pltpu.VMEM((512, 2048), BF16),
            pltpu.VMEM((512, 512), BF16),
            pltpu.VMEM((512, 512), BF16),
            pltpu.VMEM((128, 1024), BF16),
            pltpu.VMEM((2, 512, 128), BF16),
            pltpu.VMEM((2, 128, 256), BF16),
            pltpu.VMEM((8, 128), jnp.int32),
            pltpu.VMEM((devices, 128), jnp.int32),
            pltpu.VMEM((2, devices, 512), BF16),
            pltpu.VMEM((2, 16 * devices, 128), F32),
            pltpu.VMEM((2 * devices, 16, 128), BF16),
            pltpu.VMEM((2 * devices, 16, 128), BF16),
            pltpu.SMEM((NB,), jnp.int32),
            pltpu.VMEM((NB * 32, 512), F32),
            pltpu.VMEM((3, 8, 32, 512), BF16),
            pltpu.VMEM((3, 256, 128), F32),
            pltpu.VMEM((8, SLOTS, 8, 384), F32),
            pltpu.VMEM((10, 256, 768), BF16),
            pltpu.VMEM((3, 768, 256), BF16),
            pltpu.VMEM((3, 768, 256), BF16),
            pltpu.VMEM((NB * 32, 512), BF16),
            pltpu.VMEM((NB * 16, 128), BF16),
            pltpu.VMEM((8, NB, 8, 256), F32),
            pltpu.VMEM((256, 256), BF16),
            pltpu.VMEM((8, 256), F32),
            pltpu.VMEM((2, 2, 64, 256), BF16),
            pltpu.VMEM((2, 2, 2, 16, 256), BF16),
            pltpu.VMEM((16, 256), F32),
            pltpu.VMEM((16, 256), F32),
            pltpu.VMEM((2, 2, 64, 256), BF16),
            pltpu.VMEM((2, 2, 2, 16, 256), BF16),
            pltpu.SemaphoreType.DMA((2, 6)),
            pltpu.SemaphoreType.DMA((2, 6)),
            pltpu.SemaphoreType.DMA((16,)),
            pltpu.SemaphoreType.DMA,
            pltpu.SemaphoreType.DMA((2,)),
            pltpu.SemaphoreType.DMA((2,)),
            pltpu.SemaphoreType.DMA((2,)),
        ],
        compiler_params=pltpu.CompilerParams(
            collective_id=0, has_side_effects=True, vmem_limit_bytes=56 * 1024 * 1024
        ),
    )(
        parent_owner.reshape(NB), parent_cell, face_list, adjacency, bias_first, bias_second, parent_proj, conv_first,
        conv_second, fine_features, coarse_cache, jnp.asarray(perm, BF16),
        jnp.asarray(perm.T, BF16), jnp.asarray(up, BF16),
        jnp.asarray(pick, BF16), jnp.asarray(pickup, BF16),
    )
    return pl.pallas_call(
        hand_on,
        out_shape=jax.ShapeDtypeStruct((NB, 32, 512), BF16),
        in_specs=[hbm],
        out_specs=hbm,
        scratch_shapes=[pltpu.VMEM((NB, 32, 512), BF16), pltpu.SemaphoreType.DMA((2, 8))],
    )(out)


def solution(mesh):
    placed = (
        P(("gx", "gy"), None, None),
        P(("gx", "gy"), None),
        P(("gx", "gy"), None),
        P(("gx", "gy")),
        P(("gx", "gy")),
        P(("gx", "gy"), None),
        P(),
        P(),
        P(),
        P(),
        P(),
    )
    return jax.shard_map(
        per_device,
        mesh=mesh,
        in_specs=placed,
        out_specs=P(("gx", "gy"), None, None),
        check_vma=False,
    )
```

```python
import jax
import jax.numpy as jnp
import numpy as np
from jax import lax
from jax.experimental import pallas as pl
from jax.experimental.pallas import tpu as pltpu
from jax.sharding import PartitionSpec as P

F32 = jnp.float32
BF16 = jnp.bfloat16
NB = 32
SLOTS = 53
MESH = pl.DeviceIdType.MESH
GROUPS = [[0, 1, 6, 7, 2, 3], [4, 5]]


def column_of(dx, dy, dz):
    at = 9 * (dx + 1) + 3 * (dy + 1) + dz + 1
    return at if at < 13 else at - 1


def lane_tables():
    lane = np.arange(512)
    x, row = lane % 64 // 8, lane % 8
    y, z = 2 * (row // 2) + lane // 64 % 2, 4 * (row % 2) + lane // 128
    voxel = 64 * x + 8 * y + z
    cell = 16 * (x // 2) + 4 * (y // 2) + z // 2
    perm = (np.arange(512)[:, None] == voxel[None, :]).astype(np.float32)
    up = (np.arange(64)[:, None] == cell[None, :]).astype(np.float32)
    blank = np.zeros_like(up)
    even = np.concatenate([up, blank], 0)
    odd = np.concatenate([blank, up], 0)
    return perm, np.concatenate([even, odd], 1)


def face_tables():
    lane = np.arange(128)
    fixed, at = np.where(lane < 64, 7, 0), lane % 64
    part, row = at // 8, at % 8
    across_x = (fixed, 2 * (row // 2) + part // 4, 4 * (row % 2) + part % 4)
    across_y = (at % 16 // 2, fixed, 4 * (at % 2) + at // 16)
    picks, ups = [], []
    for x, y, z in (across_x, across_y):
        voxel = 64 * x + 8 * y + z
        cell = 16 * (x // 2) + 4 * (y // 2) + z // 2
        picks.append((np.arange(512)[:, None] == voxel[None, :]).astype(np.float32))
        up = (np.arange(64)[:, None] == cell[None, :]).astype(np.float32)
        blank = np.zeros_like(up)
        ups.append(np.concatenate([np.concatenate([up, blank], 0), np.concatenate([blank, up], 0)], 1))
    return np.stack(picks), np.stack(ups)


def build_band(weight_ref, band_ref):
    block = lax.broadcasted_iota(jnp.int32, (32, 128), 1) // 32
    zero = jnp.zeros((32, 128), F32)

    def per_x(i, carry):
        moved = {}
        for j in range(3):
            taps = [weight_ref[9 * i + 3 * j + k].astype(F32) for k in (2, 1, 0)]
            strip = jnp.concatenate(taps + [jnp.zeros((32, 32), F32)], axis=0).T
            for z in range(-1, 5):
                rolled = strip if z == 1 else pltpu.roll(strip, (32 * (z - 1)) % 128, 1)
                fits = (block >= z - 1) & (block <= z + 1)
                moved[j, z] = jnp.where(fits, rolled, 0.0)
        order = [(y, z) for y in (0, 1, -1, 2) for z in range(4)]
        order += [(0, 4), (1, 4), (0, -1), (1, -1), (2, 4), (-1, 4), (2, -1), (-1, -1)]
        for n, (y, z) in enumerate(order):
            halves = [moved[y + 1, z] if y < 2 else zero, moved[y, z] if y > -1 else zero]
            band_ref[i, pl.ds(32 * n, 32), :] = jnp.concatenate(halves, axis=1).astype(BF16)
        return carry

    lax.fori_loop(0, 3, per_x, 0)


def edge_lanes(low, high):
    axes = low.ndim
    lane = lax.broadcasted_iota(jnp.int32, low.shape, axes - 1)
    row = lax.broadcasted_iota(jnp.int32, low.shape, axes - 2)
    a = jnp.where(lane < 32, low, pltpu.roll(high, 32, axes - 1))
    b = jnp.where(lane < 96, pltpu.roll(low, 96, axes - 1), high)
    ends = jnp.where(lane < 64, a, b)
    return jnp.where(row % 2 == 0, pltpu.roll(ends, 7, axes - 2), pltpu.roll(ends, 1, axes - 2))


def wait_bytes(ref, sem):
    pltpu.make_async_copy(ref, ref, sem).wait()


def kernel(
    owner_hbm, cell_hbm, face_hbm, adj_hbm, bias1_hbm, bias2_hbm, proj_hbm, weight1_hbm, weight2_hbm,
    fine_hbm, cache_hbm, perm_hbm, unperm_hbm, up_hbm, pick_hbm, pickup_hbm, out_hbm,
    owner_ref, cell_ref, face_ref, adj_ref, bias1_ref, bias2_ref, proj_ref, weight1_ref, weight2_ref,
    fine_ref, cache_ref, perm_ref, unperm_ref, up_ref, pick_ref, pickup_ref, code_ref, codes_ref, hot_ref, ans_ref, stage_ref, ret_ref, rank_ref,
    finep_ref, side_ref, sidep_ref, tile_ref, pad_ref, band1_ref, band2_ref, level_ref, par_ref,
    sum_ref, mix_ref, bias_ref, xs_ref, ys_ref, yrow_ref, row_ref, xr_ref, yr_ref,
    send_sem, recv_sem, load_sem, out_sem, pair_sem, block_sem, reply_sem,
):
    gx, gy = lax.axis_index("gx"), lax.axis_index("gy")
    nx, ny = lax.axis_size("gx"), lax.axis_size("gy")
    devices = nx * ny
    up_x, down_x = lax.rem(gx + 1, nx), lax.rem(gx + nx - 1, nx)
    up_y, down_y = lax.rem(gy + 1, ny), lax.rem(gy + ny - 1, ny)
    neighbours = [(up_x, gy), (down_x, gy), (gx, up_y), (gx, down_y)]
    me = gx * ny + gy
    chip, core = gx // 2, lax.rem(gx, 2)
    near = 2 * ny
    far = nx // 2
    spot = gy * 2 + core

    def near_device(k):
        at = lax.rem(spot + k, near)
        return (chip * 2 + lax.rem(at, 2), at // 2)

    def far_device(k):
        return (lax.rem(chip + k, far) * 2 + core, gy)

    barrier = pltpu.get_barrier_semaphore()
    for k in range(1, near):
        pl.semaphore_signal(barrier, inc=1, device_id=near_device(k), device_id_type=MESH)
    for k in range(1, far):
        pl.semaphore_signal(barrier, inc=1, device_id=far_device(k), device_id_type=MESH)
    pairs = [
        (owner_hbm, owner_ref), (cell_hbm, cell_ref), (cache_hbm, cache_ref), (face_hbm, face_ref),
        (adj_hbm, adj_ref), (bias1_hbm, bias1_ref), (bias2_hbm, bias2_ref), (proj_hbm, proj_ref),
        (weight1_hbm, weight1_ref), (weight2_hbm, weight2_ref), (fine_hbm, fine_ref), (perm_hbm, perm_ref),
        (unperm_hbm, unperm_ref), (up_hbm, up_ref), (pick_hbm, pick_ref), (pickup_hbm, pickup_ref),
    ]
    loads = [pltpu.make_async_copy(src, dst, load_sem.at[n]) for n, (src, dst) in enumerate(pairs)]
    for load in loads:
        load.start()
    loads[0].wait()
    loads[1].wait()

    lane = lax.broadcasted_iota(jnp.int32, (1, 128), 1)
    code = jnp.full((1, 128), -1, jnp.int32)
    for b in range(NB):
        code = jnp.where(lane == b, owner_ref[b] * 512 + cell_ref[b], code)
    code_ref[0:1] = code
    here = chip * near + spot
    codes_ref[pl.ds(here, 1)] = code

    pl.semaphore_wait(barrier, near + far - 2)

    own_row = codes_ref.at[pl.ds(here, 1)]
    for k in range(1, near):
        pltpu.make_async_remote_copy(
            src_ref=code_ref.at[pl.ds(0, 1)], dst_ref=own_row, send_sem=pair_sem.at[0], recv_sem=pair_sem.at[1],
            device_id=near_device(k), device_id_type=MESH).start()

    wait_bytes(codes_ref.at[pl.ds(0, near - 1)], pair_sem.at[1])
    block = codes_ref.at[pl.ds(pl.multiple_of(chip * near, near), near)]
    for k in range(1, far):
        pltpu.make_async_remote_copy(
            src_ref=block, dst_ref=block, send_sem=block_sem.at[0], recv_sem=block_sem.at[1],
            device_id=far_device(k), device_id_type=MESH).start()
    loads[2].wait()
    wait_bytes(codes_ref.at[pl.ds(0, near * (far - 1))], block_sem.at[1])

    half = devices // 2
    index = lax.broadcasted_iota(jnp.int32, (half, 512), 1).astype(F32)

    def answers(turn, its_core, start):
        codes = codes_ref[pl.ds(its_core, half, stride=2), :]
        spots = lax.broadcasted_iota(jnp.int32, codes.shape, 1).astype(F32)
        match = (codes >> 9) == me
        cells = (codes & 511).astype(F32)
        lead = jnp.min(jnp.where(match, spots, 999.0), axis=1, keepdims=True)
        one = jnp.max(jnp.where(match & (spots == lead), cells, -1.0), axis=1, keepdims=True)
        two = jnp.max(jnp.where(match & (spots != lead), cells, -1.0), axis=1, keepdims=True)
        hot_ref[turn, pl.ds(0, half), :] = jnp.where(index == one, 1.0, 0.0).astype(BF16)
        hot_ref[turn, pl.ds(half, half), :] = jnp.where(index == two, 1.0, 0.0).astype(BF16)

        def answer(n, carry):
            cols = pl.ds(pl.multiple_of(256 * n, 256), 256)
            rows = jnp.dot(hot_ref[turn], cache_ref[:, cols], preferred_element_type=F32)
            ans_ref[turn, pl.ds(pl.multiple_of(2 * n * devices, devices), devices), :] = rows[:, :128]
            ans_ref[turn, pl.ds(pl.multiple_of((2 * n + 1) * devices, devices), devices), :] = rows[:, 128:]
            return carry

        lax.fori_loop(0, 8, answer, 0, unroll=True)

        def answer_to(at):
            first = ans_ref[turn, pl.ds(at, 16, stride=devices), :]
            second = ans_ref[turn, pl.ds(half + at, 16, stride=devices), :]
            return first.astype(BF16), second.astype(BF16)

        if turn == 0:
            mine = answer_to(chip * ny + gy)
            ret_ref[2 * me] = mine[0]
            ret_ref[2 * me + 1] = mine[1]

        def reply(i, carry):
            at = lax.rem(chip * ny + gy + 27 * i, half)
            dx, dy = at // ny * 2 + its_core, lax.rem(at, ny)
            to = dx * ny + dy
            pair = answer_to(at)
            stage_ref[2 * to] = pair[0]
            stage_ref[2 * to + 1] = pair[1]
            pltpu.make_async_remote_copy(
                src_ref=stage_ref.at[pl.ds(2 * to, 2)], dst_ref=ret_ref.at[pl.ds(2 * me, 2)],
                send_sem=reply_sem.at[0], recv_sem=reply_sem.at[1],
                device_id=(dx, dy), device_id_type=MESH).start()
            return carry

        lax.fori_loop(start, half, reply, 0, unroll=3 if start else 2)

    answers(0, core, 1)
    answers(1, 1 - core, 0)

    for load in loads[3:]:
        load.wait()

    def ranks(b, carry):
        count = jnp.int32(0)
        for other in range(NB):
            same = (owner_ref[other] == owner_ref[b]) & (other < b)
            count = count + jnp.where(same, 1, 0)
        rank_ref[b] = owner_ref[b] * 2 + count
        for column in range(26):
            adj_ref[b, column] = adj_ref[b, column] + 1
        return carry

    lax.fori_loop(0, NB, ranks, 0)
    build_band(weight1_ref, band1_ref)
    build_band(weight2_ref, band2_ref)
    yrow_ref[...] = jnp.zeros_like(yrow_ref)
    row_ref[...] = jnp.zeros_like(row_ref)
    for x in range(8):
        tile_ref[x, 0] = jnp.zeros((8, 384), F32)
    lane = lax.broadcasted_iota(jnp.int32, (1, 256), 1)
    for n, ref in enumerate((bias1_ref, bias2_ref)):
        line = jnp.zeros((1, 256), F32)
        for o in range(32):
            line = jnp.where(lane % 32 == o, ref[o], line)
        bias_ref[n : n + 1] = line

    wide = jnp.concatenate([proj_ref[...]] * 8, axis=0)
    chan = lax.broadcasted_iota(jnp.int32, (32, 256), 0)
    lane = lax.broadcasted_iota(jnp.int32, (32, 256), 1)
    pick = jnp.where(chan == 2 * (lane % 16) + lane // 128, 1.0, 0.0).astype(BF16)
    spread = jnp.dot(wide, pick, preferred_element_type=F32)
    row = lax.broadcasted_iota(jnp.int32, (256, 256), 0)
    lane = lax.broadcasted_iota(jnp.int32, (256, 256), 1)
    mix_ref[...] = jnp.where(row // 32 == lane % 128 // 16, spread, 0.0).astype(BF16)

    def unfold(g, carry):
        fine = fine_ref[pl.ds(pl.multiple_of(8 * g, 8), 8)].reshape(256, 512)
        rows = pl.ds(pl.multiple_of(256 * g, 256), 256)
        finep_ref[rows, :] = jnp.dot(fine, perm_ref[...], preferred_element_type=F32)
        return carry

    lax.fori_loop(0, 4, unfold, 0)

    def listed(group, n):
        return face_ref[8 * group + n] if group < 2 else face_ref[16 + n % 4]

    for group in range(3):
        for n in range(8):
            side_ref[group, n] = fine_ref[listed(group, n)]
        sidep_ref[group] = jnp.dot(
            side_ref[group].reshape(256, 512), pick_ref[group // 2], preferred_element_type=F32
        )
    wait_bytes(ret_ref.at[pl.ds(0, 2 * devices - 2)], reply_sem.at[1])

    def place(x, slot, tile):
        tile_ref[x, slot] = jnp.concatenate([tile, edge_lanes(tile[:, :128], tile[:, 128:])], axis=1)

    def copy_of(turn, src, dst, kind, other):
        return pltpu.make_async_remote_copy(
            src_ref=src, dst_ref=dst, send_sem=send_sem.at[turn, kind], recv_sem=recv_sem.at[turn, kind],
            device_id=neighbours[other], device_id_type=MESH)

    def x_copies(turn):
        return [copy_of(turn, xs_ref.at[turn, d], xr_ref.at[turn, d], d, d) for d in range(2)]

    def y_copies(turn, group):
        return [
            copy_of(turn, ys_ref.at[turn, d, group], yr_ref.at[turn, d, group], 2 + 2 * d + group, 2 + d)
            for d in range(2)
        ]

    def side_tiles(group):
        pair = jnp.concatenate([ret_ref[rank_ref[listed(group, n)]] for n in range(8)], axis=0)
        both = jnp.dot(pair, pickup_ref[group // 2], preferred_element_type=F32).astype(BF16)
        stack = jnp.concatenate([both[:, :128], both[:, 128:]], axis=0)
        mapped = jnp.dot(mix_ref[...], stack, preferred_element_type=F32)
        level = (sidep_ref[group] + mapped).astype(BF16).astype(F32)
        turned = [level[:128].T, level[128:].T]
        tiles = []
        for n in range(8 if group < 2 else 4):
            side = 64 * (group if group < 2 else n // 2)
            source = turned[n // 4]
            tall = 8 if group < 2 else 16
            tiles.append(jnp.concatenate(
                [source[side + at : side + at + tall, 32 * (n % 4) : 32 * (n % 4) + 32] for at in range(0, 64, tall)],
                axis=1,
            ))
        return tiles

    for d in range(2):
        xs_ref[0, d] = jnp.concatenate(side_tiles(d), axis=0).astype(BF16)
    for d, copy in enumerate(x_copies(0)):
        copy.start()
    lines = side_tiles(2)
    for d in range(2):
        for j in range(2):
            yrow_ref[:, pl.ds(128 * j, 128)] = lines[2 * d + j]
        for group in range(2):
            for n, x in enumerate(GROUPS[group]):
                row_ref[pl.ds(2 * n, 2), :] = yrow_ref[pl.ds(2 * x, 2), :]
            ys_ref[0, d, group] = row_ref[...].astype(BF16)
    for group in range(2):
        for copy in y_copies(0, group):
            copy.start()

    def fetch(b, carry):
        par_ref[pl.ds(pl.multiple_of(16 * b, 16), 16), :] = ret_ref[rank_ref[b]]
        return carry

    lax.fori_loop(0, NB, fetch, 0)

    def level(g, carry):
        rows = pl.ds(pl.multiple_of(256 * g, 256), 256)
        pair = par_ref[pl.ds(pl.multiple_of(128 * g, 128), 128), :]
        both = jnp.dot(pair, up_ref[...], preferred_element_type=F32).astype(BF16)
        stack = jnp.concatenate([both[:, :512], both[:, 512:]], axis=0)
        mapped = jnp.dot(mix_ref[...], stack, preferred_element_type=F32)
        rounded = (finep_ref[rows, :] + mapped).astype(BF16)
        level_ref[rows, :] = rounded
        wide = rounded.astype(F32)
        for n in range(8):
            own = wide[32 * n : 32 * n + 32, :]
            square = jnp.concatenate([own[:, 128 * k : 128 * k + 128] for k in range(4)], axis=0)
            turned = square.T
            for x in range(8):
                low, high = turned[8 * x : 8 * x + 8], turned[64 + 8 * x : 72 + 8 * x]
                place(x, 8 * g + n + 1, jnp.concatenate([low, high], axis=1))
        return carry

    lax.fori_loop(0, 4, level, 0)

    row8 = lax.broadcasted_iota(jnp.int32, (8, 128), 0)
    lane8 = lax.broadcasted_iota(jnp.int32, (8, 128), 1)
    inner = (lane8 < 64) == (row8 % 2 == 0)

    def send_x(turn):
        for d, copy in enumerate(x_copies(turn)):
            x = 7 if d == 0 else 0
            for j in range(0, 8, 2):
                two = jnp.concatenate(
                    [tile_ref[x, face_ref[8 * d + j + n] + 1, :, pl.ds(0, 256)] for n in range(2)], axis=0
                )
                xs_ref[turn, d, pl.ds(8 * j, 16), :] = two.astype(BF16)
            copy.start()

    def send_y(turn, group):
        for d, copy in enumerate(y_copies(turn, group)):
            row, side = (6, 128) if d == 0 else (0, 0)
            for j in range(2):
                at = face_ref[16 + 2 * d + j] + 1
                for n, x in enumerate(GROUPS[group]):
                    yrow_ref[pl.ds(2 * n, 2), pl.ds(128 * j, 128)] = tile_ref[x, at, pl.ds(row, 2), pl.ds(side, 128)]
            ys_ref[turn, d, group] = yrow_ref[...].astype(BF16)
            copy.start()

    def land_x(turn):
        for d, copy in enumerate(x_copies(turn)):
            copy.wait_recv()
            here = (gx > 0) if d == 0 else (gx < nx - 1)
            for j in range(8):
                if j % 2 == 0:
                    two = xr_ref[turn, d, pl.ds(8 * j, 16), :].astype(F32)
                    two = jnp.where(here, two, 0.0)
                place(7 if d == 0 else 0, 33 + 8 * d + j, two[8 * (j % 2) : 8 * (j % 2) + 8])

    def land_y(turn, group):
        for d, copy in enumerate(y_copies(turn, group)):
            copy.wait_recv()
            here = (gy > 0) if d == 0 else (gy < ny - 1)
            rows = jnp.where(here, yr_ref[turn, d, group].astype(F32), 0.0)
            for j in range(2):
                for n, x in enumerate(GROUPS[group]):
                    lines = rows[2 * n : 2 * n + 2, 128 * j : 128 * j + 128]
                    even = jnp.broadcast_to(lines[:1], (8, 128))
                    half = jnp.where(row8 % 2 == 0, even, jnp.broadcast_to(lines[1:], (8, 128)))
                    place(x, 49 + 2 * d + j, jnp.concatenate([half, half], axis=1))

    def padded_tile(near_by, px):
        dx = -1 if px == 0 else (1 if px == 9 else 0)
        x = 7 if px == 0 else (0 if px == 9 else px - 1)

        def at(dy, dz):
            return near_by[dx, dy, dz]

        def ends(dy):
            one, two, own = (tile_ref[x, at(dy, dz), :, pl.ds(256, 128)] for dz in (1, -1, 0))
            return jnp.where(inner, own, jnp.where(lane8 < 64, one, two))

        mid = tile_ref[x, at(0, 0), :, pl.ds(0, 256)]
        below = tile_ref[x, at(-1, 0), :, pl.ds(128, 128)]
        above = tile_ref[x, at(1, 0), :, pl.ds(0, 128)]
        low = pltpu.roll(jnp.where(row8 >= 6, below, mid[:, 128:]), 2, 0)
        high = pltpu.roll(jnp.where(row8 < 2, above, mid[:, :128]), 6, 0)
        here = ends(0)
        clow = pltpu.roll(jnp.where(row8 >= 6, ends(-1), here), 2, 0)
        chigh = pltpu.roll(jnp.where(row8 < 2, ends(1), here), 6, 0)
        corners = jnp.where(lane8 // 32 % 2 == 1, clow, chigh)
        return jnp.concatenate([mid, low, high, here, corners], axis=1)

    def pad_planes(planes):
        steps = sorted({-1 if px == 0 else (1 if px == 9 else 0) for px in planes})

        def slots(b):
            return {
                (dx, dy, dz): b + 1 if dx == dy == dz == 0 else adj_ref[b, column_of(dx, dy, dz)]
                for dx in steps for dy in (-1, 0, 1) for dz in (-1, 0, 1)
            }

        def per_pair(n, carry):
            even, odd = slots(2 * n), slots(2 * n + 1)
            for px in planes:
                two = jnp.concatenate([padded_tile(even, px), padded_tile(odd, px)], axis=0)
                pad_ref[px, pl.ds(pl.multiple_of(16 * n, 16), 16), :] = two.astype(BF16)
            return carry

        lax.fori_loop(0, NB // 2, per_pair, 0, unroll=2)

    def land_and_pad(turn):
        land_x(turn)
        land_y(turn, 0)
        pad_planes([0, 9] + [x + 1 for x in GROUPS[0]])
        land_y(turn, 1)
        pad_planes([x + 1 for x in GROUPS[1]])

    def conv(first_plane, planes, band_ref, bias):
        total = bias_ref[pl.ds(bias, 1)]
        for i in range(3):
            rows = pad_ref[pl.ds(first_plane + i, planes)].reshape(256 * planes, 768)
            total = total + jnp.dot(rows, band_ref[i], preferred_element_type=F32)
        return total

    land_x(0)
    land_y(0, 0)
    land_y(0, 1)
    pad_planes(range(10))

    def first(pair):
        v = conv(2 * pair, 2, band1_ref, 0)
        half = 0.5 * v
        h = (half + half * jnp.tanh(half)).astype(BF16).astype(F32)
        tile_ref[pl.ds(2 * pair, 2), pl.ds(1, NB), :, pl.ds(0, 256)] = h.reshape(2, NB, 8, 256)
        e = edge_lanes(h[:, :128].reshape(2 * NB, 8, 128), h[:, 128:].reshape(2 * NB, 8, 128))
        tile_ref[pl.ds(2 * pair, 2), pl.ds(1, NB), :, pl.ds(256, 128)] = e.reshape(2, NB, 8, 128)

    def outer(n, carry):
        first(3 * n)
        return carry

    lax.fori_loop(0, 2, outer, 0)
    send_x(1)
    first(1)
    send_y(1, 0)
    first(2)
    send_y(1, 1)
    land_and_pad(1)

    def second(pair, carry):
        sum_ref[pl.ds(4 * pair, 4)] = conv(4 * pair, 4, band2_ref, 1).reshape(4, NB, 8, 256)
        return carry

    lax.fori_loop(0, 2, second, 0)

    def finish(g, carry):
        rows = pl.ds(pl.multiple_of(512 * g, 512), 512)
        parts = []
        for n in range(16):
            tall = [sum_ref[x, 16 * g + n] for x in range(8)]
            turned = jnp.concatenate([t[:, :128] for t in tall] + [t[:, 128:] for t in tall], axis=0).T
            parts.append(jnp.concatenate([turned[32 * k : 32 * k + 32] for k in range(4)], axis=1))
        total = jnp.concatenate(parts, axis=0) + level_ref[rows, :].astype(F32)
        rows = jnp.dot(total.astype(BF16), unperm_ref[...], preferred_element_type=F32).astype(BF16)
        bricks = pl.ds(pl.multiple_of(16 * g, 16), 16)
        fine_ref[bricks] = rows.reshape(16, 32, 512)
        pltpu.make_async_copy(fine_ref.at[bricks], out_hbm.at[bricks], out_sem).start()
        return carry

    lax.fori_loop(0, 2, finish, 0)
    for turn in range(2):
        for copy in x_copies(turn) + y_copies(turn, 0) + y_copies(turn, 1):
            copy.wait_send()
    wait_bytes(codes_ref.at[pl.ds(0, near - 1)], pair_sem.at[0])
    wait_bytes(codes_ref.at[pl.ds(0, near * (far - 1))], block_sem.at[0])
    wait_bytes(ret_ref.at[pl.ds(0, 2 * devices - 2)], reply_sem.at[0])
    pltpu.make_async_copy(fine_ref, out_hbm, out_sem).wait()


def hand_on(values_hbm, out_hbm, held, sem):
    parts = [pl.ds(4 * n, 4) for n in range(8)]
    into = [pltpu.make_async_copy(values_hbm.at[p], held.at[p], sem.at[0, n]) for n, p in enumerate(parts)]
    onward = [pltpu.make_async_copy(held.at[p], out_hbm.at[p], sem.at[1, n]) for n, p in enumerate(parts)]
    for copy in into:
        copy.start()
    for before, after in zip(into, onward):
        before.wait()
        after.start()
    for copy in onward:
        copy.wait()


def per_device(
    fine_features, coarse_cache, parent_owner, parent_cell, face_list, adjacency,
    parent_proj, conv_first, bias_first, conv_second, bias_second,
):
    devices = lax.axis_size("gx") * lax.axis_size("gy")
    perm, up = lane_tables()
    pick, pickup = face_tables()
    hbm = pl.BlockSpec(memory_space=pl.ANY)
    out = pl.pallas_call(
        kernel,
        out_shape=jax.ShapeDtypeStruct((NB, 32, 512), BF16),
        in_specs=[hbm] * 16,
        out_specs=hbm,
        scratch_shapes=[
            pltpu.SMEM((NB,), jnp.int32),
            pltpu.SMEM((NB,), jnp.int32),
            pltpu.SMEM((20,), jnp.int32),
            pltpu.SMEM((NB, 26), jnp.int32),
            pltpu.SMEM((32,), F32),
            pltpu.SMEM((32,), F32),
            pltpu.VMEM((32, 32), BF16),
            pltpu.VMEM((27, 32, 32), BF16),
            pltpu.VMEM((27, 32, 32), BF16),
            pltpu.VMEM((NB, 32, 512), BF16),
            pltpu.VMEM((512, 2048), BF16),
            pltpu.VMEM((512, 512), BF16),
            pltpu.VMEM((512, 512), BF16),
            pltpu.VMEM((128, 1024), BF16),
            pltpu.VMEM((2, 512, 128), BF16),
            pltpu.VMEM((2, 128, 256), BF16),
            pltpu.VMEM((8, 128), jnp.int32),
            pltpu.VMEM((devices, 128), jnp.int32),
            pltpu.VMEM((2, devices, 512), BF16),
            pltpu.VMEM((2, 16 * devices, 128), F32),
            pltpu.VMEM((2 * devices, 16, 128), BF16),
            pltpu.VMEM((2 * devices, 16, 128), BF16),
            pltpu.SMEM((NB,), jnp.int32),
            pltpu.VMEM((NB * 32, 512), F32),
            pltpu.VMEM((3, 8, 32, 512), BF16),
            pltpu.VMEM((3, 256, 128), F32),
            pltpu.VMEM((8, SLOTS, 8, 384), F32),
            pltpu.VMEM((10, 256, 768), BF16),
            pltpu.VMEM((3, 768, 256), BF16),
            pltpu.VMEM((3, 768, 256), BF16),
            pltpu.VMEM((NB * 32, 512), BF16),
            pltpu.VMEM((NB * 16, 128), BF16),
            pltpu.VMEM((8, NB, 8, 256), F32),
            pltpu.VMEM((256, 256), BF16),
            pltpu.VMEM((8, 256), F32),
            pltpu.VMEM((2, 2, 64, 256), BF16),
            pltpu.VMEM((2, 2, 2, 16, 256), BF16),
            pltpu.VMEM((16, 256), F32),
            pltpu.VMEM((16, 256), F32),
            pltpu.VMEM((2, 2, 64, 256), BF16),
            pltpu.VMEM((2, 2, 2, 16, 256), BF16),
            pltpu.SemaphoreType.DMA((2, 6)),
            pltpu.SemaphoreType.DMA((2, 6)),
            pltpu.SemaphoreType.DMA((16,)),
            pltpu.SemaphoreType.DMA,
            pltpu.SemaphoreType.DMA((2,)),
            pltpu.SemaphoreType.DMA((2,)),
            pltpu.SemaphoreType.DMA((2,)),
        ],
        compiler_params=pltpu.CompilerParams(
            collective_id=0, has_side_effects=True, vmem_limit_bytes=56 * 1024 * 1024
        ),
    )(
        parent_owner.reshape(NB), parent_cell, face_list, adjacency, bias_first, bias_second, parent_proj, conv_first,
        conv_second, fine_features, coarse_cache, jnp.asarray(perm, BF16),
        jnp.asarray(perm.T, BF16), jnp.asarray(up, BF16),
        jnp.asarray(pick, BF16), jnp.asarray(pickup, BF16),
    )
    return pl.pallas_call(
        hand_on,
        out_shape=jax.ShapeDtypeStruct((NB, 32, 512), BF16),
        in_specs=[hbm],
        out_specs=hbm,
        scratch_shapes=[pltpu.VMEM((NB, 32, 512), BF16), pltpu.SemaphoreType.DMA((2, 8))],
    )(out)


def solution(mesh):
    placed = (
        P(("gx", "gy"), None, None),
        P(("gx", "gy"), None),
        P(("gx", "gy"), None),
        P(("gx", "gy")),
        P(("gx", "gy")),
        P(("gx", "gy"), None),
        P(),
        P(),
        P(),
        P(),
        P(),
    )
    return jax.shard_map(
        per_device,
        mesh=mesh,
        in_specs=placed,
        out_specs=P(("gx", "gy"), None, None),
        check_vma=False,
    )
```
